32 devices in a mesh: rep: 1, wide: 16 (over z, y, x), narrow: 2 (over core).
Axes of the slice: x: 2, y: 2, z: 4, core: 2. Of those that a mesh axis runs over, the one named last changes fastest.
Arguments:
- hidden_in: bfloat16 [2048, 2048], P(('rep', 'wide', 'narrow')), may hold values from -6 to 6
- queries: bfloat16 [2048, 2048], P(('rep', 'wide'), 'narrow')
- out_gate: bfloat16 [2048, 2048], P(('rep', 'wide'), 'narrow'), may hold values from -6 to 6
- draft_kv: bfloat16 [2, 2048, 256], P(None, ('rep', 'wide')), may hold values from -6 to 6
- cache_keys: bfloat16 [128, 256, 256], P(('rep', 'wide'))
- cache_values: bfloat16 [128, 256, 256], P(('rep', 'wide')), may hold values from -6 to 6
- draft_len: int32 [128], P(('rep', 'wide')), may hold values from 1 to 16, as said below
- cache_len: int32 [128], P(('rep', 'wide')), may hold values from 1 to 256, as said below
- o_weight: bfloat16 [2048, 2048], P('narrow'), may hold values from -0.125 to 0.125
- norm_gain: float32 [2048], replicated, may hold values from 0.5 to 1.5
- route_ids: int32 [2048, 10], P(('rep', 'wide', 'narrow')), may hold values from 0 to 31, all different within a row; in each aligned block of 64 rows (0 to 63, 64 to 127, ...) at most 30 rows name the same one
- route_weights: float32 [2048, 10], P(('rep', 'wide', 'narrow')), may hold values from 0.05 to 0.4
- w_gate: bfloat16 [32, 2048, 512], P(('wide', 'narrow')), may hold values from -0.125 to 0.125
- w_up: bfloat16 [32, 2048, 512], P(('wide', 'narrow')), may hold values from -0.125 to 0.125
- w_down: bfloat16 [32, 512, 2048], P(('wide', 'narrow')), may hold values from -0.25 to 0.25
Outputs:
- mixed: bfloat16 [2048, 2048], P(('rep', 'wide', 'narrow'))
The draws below stay inside these ranges and needn't reach their ends.
Inputs may be any that keep to these rules, and one draw needn't show every extreme that they name: `route_ids`: in each aligned block of 64 rows (the rows of one device) no expert is named by more than 30 pairs (row, choice), a bound that some block reaches. `draft_len`: some request has all 16 draft rows live. `cache_len`: some request has all 256 cache slots live.
All inputs are finite; a program needn't handle non-finite values.
Results may differ from the reference program's by a relative error of at most 0.0044.
Values may be sent and summed in bfloat16 or wider, within the bound.
No kernel may reach another device: no remote copies, remote signals or barrier semaphores. Data moves between devices by JAX's collectives and lax.ppermute only.
A program may use at most 128 MiB of HBM per device.

```python
import math
import jax
import jax.numpy as jnp
import numpy as np
from jax import lax

D = 2048
HD = 256
FF = 512
TOPK = 10
Q_HEADS = 8
DRAFT = 16
CTX = 256
OWN = 64
REQS = 128
ROWS_ALL = 2048
EXPERTS = 32
CAP = 30


def draw_queries(key, part):
    values = jax.random.normal(key, (ROWS_ALL, Q_HEADS * HD), jnp.float32)
    return values.astype(jnp.bfloat16)


def draw_cache_keys(key, part):
    values = jax.random.normal(key, (REQS, CTX, HD), jnp.float32)
    return values.astype(jnp.bfloat16)


def draw_draft_len(key, part):
    lengths = jax.random.randint(key, (REQS,), 1, DRAFT + 1, dtype=jnp.int32)
    return lengths.at[0].set(DRAFT)


def draw_cache_len(key, part):
    lengths = jax.random.randint(key, (REQS,), 1, CTX + 1, dtype=jnp.int32)
    return lengths.at[0].set(CTX)


def shard_levels(stream_key, extent, pieces, least, high):
    factor_of, own = 1.0, jax.random.fold_in(stream_key, 6)
    for dim, parts in pieces:
        steps = jnp.exp(jax.random.uniform(jax.random.fold_in(own, dim), (parts,), jnp.float32, least / len(pieces), high / len(pieces)))
        factor_of = factor_of * jnp.repeat(steps, extent[dim] // parts).reshape([-1 if axis == dim else 1 for axis in range(len(extent))])
    return factor_of


def shared_out(rng, own, number, rows, count, top, reach, lean):
    order = jax.random.permutation(rng, count)
    heavy_load, ordinary = load_shares(count, rows * top, reach, lean, True), load_shares(count, rows * top, reach, lean, False)
    places = jnp.arange(count)

    def named(sizes, offset_by):
        used = int((sizes > 0).sum())
        fixed = max(1, used // 4)
        passed = fixed + (places - fixed + offset_by * (used - fixed)) % max(1, count - fixed)
        return jnp.zeros((count,), jnp.int32).at[order[jnp.where(places < fixed, places, passed)]].set(jnp.asarray(sizes, jnp.int32))

    sizes = jnp.where(number % 4 == 0, named(heavy_load, number // 4), named(ordinary, number - number // 4 - 1))
    mixed = jax.random.permutation(jax.random.fold_in(own, 3), count)
    donor, sink = mixed[0:count // 2 * 2:2], mixed[1:count // 2 * 2:2]
    room = jnp.minimum(sizes[donor] - 1, reach - sizes[sink]) // 2
    room = jnp.where((donor == order[0]) | (sink == order[0]) | (sizes[sink] == 0), 0, jnp.maximum(room, 0))
    passed = jax.random.randint(jax.random.fold_in(own, 4), (count // 2,), 0, 1 << 20) % (room + 1)
    sizes = sizes.at[donor].add(-passed).at[sink].add(passed)
    members = jnp.searchsorted(jnp.cumsum(sizes), jnp.arange(rows * top), side="right").astype(jnp.int32)
    table = members.reshape(top, rows).T
    table = table[jax.random.permutation(jax.random.fold_in(own, 1), rows)]
    offset_by = jax.random.randint(jax.random.fold_in(own, 2), (rows, 1), 0, top)
    return jnp.take_along_axis(table, (jnp.arange(top)[None, :] + offset_by) % top, axis=1)


def load_shares(number_of, total, reach, lean, full):
    weights = [(1 << 20) // math.isqrt(rank ** lean) + 1 for rank in range(1, number_of + 1)]
    largest = reach if full else min(reach, max(-(-total // number_of), total * weights[0] // sum(weights)))
    least = 1 if total - largest >= number_of - 1 else 0
    holding, rest = [largest] + [least] * (number_of - 1), total - largest - least * (number_of - 1)
    while rest > 0:
        free = [i for i in range(1, number_of) if holding[i] < largest] or [i for i in range(1, number_of) if holding[i] < reach]
        mass, left = sum([weights[i] for i in free]), rest
        for i in free:
            more = min(reach - holding[i], max(1, left * weights[i] // mass), rest)
            holding[i] = holding[i] + more
            rest = rest - more
    return np.array(holding)


def normal_values(key, extent, width, limit, shards=(), kind=jnp.bfloat16):
    array = width * jax.random.normal(key, extent, jnp.float32)
    if shards:
        array = array * shard_levels(key, extent, shards, -0.22, 0.18)
    return jnp.clip(array, -limit, limit).astype(kind)


def setup_inputs(seed: int = 0, part: int = 0) -> dict:
    streams_of = jax.random.split(jax.random.key(seed), 16)
    own_keys = jax.random.split(jax.random.fold_in(streams_of[15], part), 16)
    hidden_in = normal_values(own_keys[0], (ROWS_ALL, D), 1.0, 6.0, ((0, 32),))
    queries = draw_queries(jax.random.fold_in(jax.random.fold_in(streams_of[15], part), 71), part)
    out_gate = normal_values(own_keys[2], (ROWS_ALL, Q_HEADS * HD), 1.5, 6.0, ((0, 16), (1, 2)))
    draft_kv = normal_values(own_keys[3], (2, ROWS_ALL, HD), 1.0, 6.0, ((1, 16),))
    cache_keys = draw_cache_keys(jax.random.fold_in(jax.random.fold_in(streams_of[15], part), 71), part)
    cache_values = normal_values(own_keys[5], (REQS, CTX, HD), 1.0, 6.0, ((0, 16),))
    draft_len = draw_draft_len(jax.random.fold_in(jax.random.fold_in(streams_of[15], part), 71), part)
    cache_len = draw_cache_len(jax.random.fold_in(jax.random.fold_in(streams_of[15], part), 71), part)
    o_weight = normal_values(streams_of[8], (Q_HEADS * HD, D), (Q_HEADS * HD) ** -0.5, 0.125, ((0, 2),))
    norm_gain = jnp.clip(1.0 + 0.1 * jax.random.normal(streams_of[9], (D,), jnp.float32), 0.5, 1.5)
    route_ids_keys = jax.random.split(jax.random.fold_in(own_keys[10], 1), ROWS_ALL // OWN)
    route_ids_turns = jax.random.permutation(jax.random.fold_in(own_keys[10], 3), ROWS_ALL // OWN)
    route_ids = jax.vmap(lambda own, number: shared_out(jax.random.fold_in(own_keys[10], 2), own, number, OWN, EXPERTS, TOPK, CAP, 2))(route_ids_keys, route_ids_turns).reshape((ROWS_ALL, TOPK))
    route_weights = jnp.clip(0.05 + 0.35 * jax.random.uniform(own_keys[11], (ROWS_ALL, TOPK), jnp.float32) ** shard_levels(own_keys[11], (ROWS_ALL, TOPK), ((0, 32),), -0.2, 0.2), 0.05, 0.4)
    w_gate = normal_values(streams_of[12], (EXPERTS, D, FF), D ** -0.5, 0.125, ((0, 32),))
    w_up = normal_values(streams_of[13], (EXPERTS, D, FF), D ** -0.5, 0.125, ((0, 32),))
    w_down = normal_values(streams_of[14], (EXPERTS, FF, D), FF ** -0.5, 0.25, ((0, 32),))
    return {"hidden_in": hidden_in, "queries": queries, "out_gate": out_gate, "draft_kv": draft_kv, "cache_keys": cache_keys, "cache_values": cache_values, "draft_len": draft_len, "cache_len": cache_len, "o_weight": o_weight, "norm_gain": norm_gain, "route_ids": route_ids, "route_weights": route_weights, "w_gate": w_gate, "w_up": w_up, "w_down": w_down}


def attention_rows(queries, out_gate, draft_kv, cache_keys, cache_values, draft_len, cache_len):
    query_blocks = queries.reshape(REQS, DRAFT, Q_HEADS, HD).astype(jnp.float32)
    draft_keys = draft_kv[0].reshape(REQS, DRAFT, HD).astype(jnp.float32)
    draft_values = draft_kv[1].reshape(REQS, DRAFT, HD).astype(jnp.float32)
    score_scale = 1.0 / math.sqrt(HD)
    cache_scores = jnp.einsum('rjhd,rcd->rjhc', query_blocks, cache_keys.astype(jnp.float32)) * score_scale
    draft_scores = jnp.einsum('rjhd,rid->rjhi', query_blocks, draft_keys) * score_scale
    slots = jnp.arange(CTX, dtype=jnp.int32)
    cache_live = slots[None, :] < cache_len[:, None]
    cache_scores = jnp.where(cache_live[:, None, None, :], cache_scores, -jnp.inf)
    positions = jnp.arange(DRAFT, dtype=jnp.int32)
    causal = positions[None, :] <= positions[:, None]
    draft_live = causal[None, :, :] & (positions[None, None, :] < draft_len[:, None, None])
    draft_scores = jnp.where(draft_live[:, :, None, :], draft_scores, -jnp.inf)
    row_max = jnp.maximum(lax.optimization_barrier(jnp.max(cache_scores, axis=-1)), lax.optimization_barrier(jnp.max(draft_scores, axis=-1)))
    cache_probs = jnp.exp(cache_scores - row_max[..., None])
    draft_probs = jnp.exp(draft_scores - row_max[..., None])
    denominator = lax.optimization_barrier(jnp.sum(cache_probs, axis=-1)) + lax.optimization_barrier(jnp.sum(draft_probs, axis=-1))
    cache_probs = cache_probs.astype(jnp.bfloat16).astype(jnp.float32)
    draft_probs = draft_probs.astype(jnp.bfloat16).astype(jnp.float32)
    context = jnp.einsum('rjhc,rcd->rjhd', cache_probs, cache_values.astype(jnp.float32))
    context = context + jnp.einsum('rjhi,rid->rjhd', draft_probs, draft_values)
    context = context / denominator[..., None]
    gate_open = jax.nn.sigmoid(out_gate.astype(jnp.float32)).reshape(REQS, DRAFT, Q_HEADS, HD)
    row_live = (positions[None, :] < draft_len[:, None]).astype(jnp.float32)
    attended = context * gate_open * row_live[:, :, None, None]
    return attended.reshape(ROWS_ALL, Q_HEADS * HD).astype(jnp.bfloat16)

def reference(hidden_in, queries, out_gate, draft_kv, cache_keys, cache_values, draft_len, cache_len, o_weight, norm_gain, route_ids, route_weights, w_gate, w_up, w_down):
    attended = attention_rows(queries, out_gate, draft_kv, cache_keys, cache_values, draft_len, cache_len)
    residual = hidden_in.astype(jnp.float32) + jnp.dot(attended, o_weight, preferred_element_type=jnp.float32)
    spread = lax.optimization_barrier(jnp.mean(residual * residual, axis=-1, keepdims=True))
    normed = (residual * lax.rsqrt(spread + 1e-06) * norm_gain).astype(jnp.bfloat16)
    pair_total = ROWS_ALL * TOPK
    expert_rows = EXPERTS * CAP
    flat_ids = route_ids.reshape(-1).astype(jnp.int32)
    order = jnp.argsort(flat_ids, stable=True).astype(jnp.int32)
    sorted_ids = flat_ids[order]
    starts = jnp.searchsorted(sorted_ids, jnp.arange(EXPERTS, dtype=jnp.int32)).astype(jnp.int32)

    def one_expert(inputs):
        index, gate_mat, up_mat, down_mat = inputs
        position = starts[index] + jnp.arange(expert_rows, dtype=jnp.int32)
        clipped = jnp.minimum(position, pair_total - 1)
        inside = (position < pair_total) & (sorted_ids[clipped] == index)
        pair_index = order[clipped]
        row_block = normed[pair_index // TOPK]
        gate_proj = jnp.dot(row_block, gate_mat, preferred_element_type=jnp.float32)
        up_proj = jnp.dot(row_block, up_mat, preferred_element_type=jnp.float32)
        hidden_act = (jax.nn.silu(gate_proj) * up_proj).astype(jnp.bfloat16)
        produced = jnp.dot(hidden_act, down_mat, preferred_element_type=jnp.float32).astype(jnp.bfloat16)
        return (produced, jnp.where(inside, pair_index, pair_total).astype(jnp.int32))
    produced, destinations = lax.map(one_expert, (jnp.arange(EXPERTS, dtype=jnp.int32), w_gate, w_up, w_down))
    expert_out = jnp.zeros((pair_total, D), produced.dtype)
    expert_out = expert_out.at[destinations.reshape(-1)].set(produced.reshape(-1, D), mode='drop')
    expert_out = expert_out.reshape(ROWS_ALL, TOPK, D).astype(jnp.float32)
    expert_mix = lax.optimization_barrier(jnp.sum(route_weights[:, :, None] * expert_out, axis=1))
    return (residual + expert_mix).astype(jnp.bfloat16)
```

```python
import functools
import math

import jax
import jax.numpy as jnp
from jax import lax
from jax.experimental import pallas as pl
from jax.experimental.pallas import tpu as pltpu
from jax.sharding import PartitionSpec as P

BF16 = jnp.bfloat16
F32 = jnp.float32
LOWEST = -1e30


def _dot(a, b):
    return jnp.dot(a, b, preferred_element_type=F32)


def _dot_t(a, b):
    return lax.dot_general(a, b, (((1,), (1,)), ((), ())), preferred_element_type=F32)


def attention_kernel(
    half_ref,
    draft_len_ref,
    cache_len_ref,
    queries,
    out_gate,
    draft_kv,
    cache_keys,
    cache_values,
    o_weight,
    out_ref,
    q_buf,
    g_buf,
    d_buf,
    k_buf,
    v_buf,
    w_buf,
    attended,
    sems,
):
    half = half_ref[0]
    reqs, context_len, head_size = k_buf.shape
    rows = q_buf.shape[0]
    drafts = rows // reqs
    heads = q_buf.shape[1] // head_size
    row_span = pl.ds(pl.multiple_of(half * rows, rows), rows)
    req_span = pl.ds(half * reqs, reqs)
    copies = [
        pltpu.make_async_copy(queries.at[row_span], q_buf, sems.at[0]),
        pltpu.make_async_copy(cache_keys.at[req_span], k_buf, sems.at[1]),
        pltpu.make_async_copy(draft_kv.at[:, row_span], d_buf, sems.at[2]),
        pltpu.make_async_copy(cache_values.at[req_span], v_buf, sems.at[3]),
        pltpu.make_async_copy(out_gate.at[row_span], g_buf, sems.at[4]),
        pltpu.make_async_copy(o_weight, w_buf, sems.at[5]),
    ]
    for copy in copies:
        copy.start()
    for copy in copies[:3]:
        copy.wait()
    scale = 1.0 / math.sqrt(head_size)
    stacked = heads * drafts
    slot = lax.broadcasted_iota(jnp.int32, (stacked, context_len), 1)
    draft_slot = lax.broadcasted_iota(jnp.int32, (stacked, drafts), 1)
    draft_row = lax.broadcasted_iota(jnp.int32, (heads, drafts, drafts), 1).reshape(stacked, drafts)
    row_index = lax.broadcasted_iota(jnp.int32, (drafts, head_size), 0)
    probs = []
    for r in range(reqs):
        span = slice(r * drafts, (r + 1) * drafts)
        query = jnp.concatenate(
            [q_buf[span, h * head_size : (h + 1) * head_size] for h in range(heads)], axis=0
        )
        cache_len = cache_len_ref[half * reqs + r]
        draft_len = draft_len_ref[half * reqs + r]
        cache_scores = _dot_t(query, k_buf[r]) * scale
        draft_scores = _dot_t(query, d_buf[0, span]) * scale
        cache_scores = jnp.where(slot < cache_len, cache_scores, LOWEST)
        live = (draft_slot <= draft_row) & (draft_slot < draft_len)
        draft_scores = jnp.where(live, draft_scores, LOWEST)
        row_max = jnp.maximum(
            jnp.max(cache_scores, axis=-1, keepdims=True),
            jnp.max(draft_scores, axis=-1, keepdims=True),
        )
        cache_probs = jnp.exp(cache_scores - row_max)
        draft_probs = jnp.exp(draft_scores - row_max)
        denominator = jnp.sum(cache_probs, axis=-1, keepdims=True) + jnp.sum(
            draft_probs, axis=-1, keepdims=True
        )
        probs.append((cache_probs.astype(BF16), draft_probs.astype(BF16), denominator))
    copies[3].wait()
    copies[4].wait()
    for r in range(reqs):
        span = slice(r * drafts, (r + 1) * drafts)
        cache_probs, draft_probs, denominator = probs[r]
        context = _dot(cache_probs, v_buf[r]) + _dot(draft_probs, d_buf[1, span])
        context = context / denominator
        draft_len = draft_len_ref[half * reqs + r]
        for h in range(heads):
            cols = slice(h * head_size, (h + 1) * head_size)
            gate = jax.nn.sigmoid(g_buf[span, cols].astype(F32))
            piece = context[h * drafts : (h + 1) * drafts] * gate
            piece = jnp.where(row_index < draft_len, piece, 0.0)
            attended[span, cols] = piece.astype(BF16)
    copies[5].wait()
    rows_in = attended[...]
    width = out_ref.shape[1]
    tile = min(512, width)
    for c in range(0, width, tile):
        out_ref[:, c : c + tile] = _dot(rows_in, w_buf[:, c : c + tile]).astype(out_ref.dtype)


def attention(half, own_rows, out_dtype, arrays):
    queries, out_gate, draft_kv, cache_keys, cache_values, draft_len, cache_len, o_weight = arrays
    reqs_all, context_len, head_size = cache_keys.shape
    reqs = reqs_all * own_rows // queries.shape[0]
    width = o_weight.shape[1]
    inner = o_weight.shape[0]
    smem = pl.BlockSpec(memory_space=pltpu.SMEM)
    hbm = pl.BlockSpec(memory_space=pl.ANY)
    return pl.pallas_call(
        attention_kernel,
        out_shape=jax.ShapeDtypeStruct((own_rows, width), out_dtype),
        in_specs=[smem] * 3 + [hbm] * 6,
        out_specs=pl.BlockSpec(memory_space=pltpu.VMEM),
        scratch_shapes=[
            pltpu.VMEM((own_rows, inner), BF16),
            pltpu.VMEM((own_rows, inner), BF16),
            pltpu.VMEM((2, own_rows, head_size), BF16),
            pltpu.VMEM((reqs, context_len, head_size), BF16),
            pltpu.VMEM((reqs, context_len, head_size), BF16),
            pltpu.VMEM((inner, width), BF16),
            pltpu.VMEM((own_rows, inner), BF16),
            pltpu.SemaphoreType.DMA((6,)),
        ],
        compiler_params=pltpu.CompilerParams(vmem_limit_bytes=24 * 1024 * 1024),
        cost_estimate=pl.CostEstimate(
            flops=2 * own_rows * inner * (width + 2 * context_len),
            bytes_accessed=2 * inner * width + 4 * reqs * context_len * head_size,
            transcendentals=0,
        ),
    )(
        half.reshape(1),
        draft_len,
        cache_len,
        queries,
        out_gate,
        draft_kv,
        cache_keys,
        cache_values,
        o_weight,
    )


def norm_kernel(hidden_ref, kept_ref, received_ref, gain_ref, residual_ref, top_ref, bottom_ref):
    residual = hidden_ref[...].astype(F32) + kept_ref[...] + received_ref[...].astype(F32)
    spread = jnp.mean(residual * residual, axis=-1, keepdims=True)
    normed = (residual * lax.rsqrt(spread + 1e-06) * gain_ref[...]).astype(BF16)
    residual_ref[...] = residual
    mid = top_ref.shape[0]
    top_ref[...] = normed[:mid]
    bottom_ref[...] = normed[mid:]


def residual_norm(hidden, kept, received, gain):
    rows, width = hidden.shape
    piece = jax.ShapeDtypeStruct((rows // 2, width), BF16)
    return pl.pallas_call(
        norm_kernel,
        out_shape=(jax.ShapeDtypeStruct((rows, width), F32), piece, piece),
        compiler_params=pltpu.CompilerParams(vmem_limit_bytes=16 * 1024 * 1024),
    )(hidden, kept, received, gain.reshape(1, width))


def experts_kernel(pieces, steps, where_ref, *refs):
    rows_in = refs[:pieces]
    weights = refs[pieces : pieces + 4]
    gates, ups, downs = (refs[pieces + 4 + 2 * i : pieces + 6 + 2 * i] for i in range(3))
    outs = refs[pieces + 10 : 2 * pieces + 10]
    rows, total, weight_buf, sems = refs[2 * pieces + 10 :]
    step = pl.program_id(0)
    size = rows_in[0].shape[0]

    @pl.when(step == 0)
    def _():
        copies = [
            pltpu.make_async_copy(
                rows_in[i], rows.at[pl.ds(i * size, size)], sems.at[i]
            )
            for i in range(pieces)
        ]
        for copy in copies:
            copy.start()
        own = weights[0].shape[1]
        for e in range(2):
            for i in range(4):
                table = weights[i][0]
                column = lax.broadcasted_iota(jnp.int32, table.shape, 1)
                chosen = jnp.where(column == where_ref[4 + e], table, 0.0)
                weight_buf[e, i * own : (i + 1) * own, :] = jnp.sum(
                    chosen, axis=1, keepdims=True
                )
        for copy in copies:
            copy.wait()

    for e in range(2):

        @pl.when(step // steps == e)
        def _():
            block = rows[...]
            gate = _dot(block, gates[e][0])
            up = _dot(block, ups[e][0])
            act = (jax.nn.silu(gate) * up * weight_buf[e]).astype(BF16)
            added = _dot(act, downs[e][0])

            @pl.when(step == 0)
            def _():
                total[...] = added

            @pl.when((step > 0) & (step < 2 * steps - 1))
            def _():
                total[...] += added

            @pl.when(step == 2 * steps - 1)
            def _():
                full = total[...] + added
                for i in range(pieces):
                    outs[i][...] = full[i * size : (i + 1) * size].astype(BF16)


def plane_experts(where, rows_in, table, own_weights, other_weights):
    pieces = len(rows_in)
    size, width = rows_in[0].shape
    hidden = own_weights[0].shape[2]
    tile = min(256, hidden)
    steps = hidden // tile
    own, count = table.shape[1:]
    hbm = pl.BlockSpec(memory_space=pl.ANY)

    def at_step(e):
        return lambda t: jnp.clip(t - e * steps, 0, steps - 1)

    def column_spec(e):
        return pl.BlockSpec((1, width, tile), lambda t, where: (0, 0, at_step(e)(t)))

    def row_spec(e):
        return pl.BlockSpec((1, tile, width), lambda t, where: (0, at_step(e)(t), 0))

    def table_spec(i):
        return pl.BlockSpec((1, own, count), lambda t, where: (where[i], 0, 0))

    piece = jax.ShapeDtypeStruct((size, width), BF16)
    weights = [w for pair in zip(own_weights, other_weights) for w in pair]
    return pl.pallas_call(
        functools.partial(experts_kernel, pieces, steps),
        out_shape=(piece,) * pieces,
        grid_spec=pltpu.PrefetchScalarGridSpec(
            num_scalar_prefetch=1,
            grid=(2 * steps,),
            in_specs=[hbm] * pieces
            + [table_spec(i) for i in range(4)]
            + [column_spec(0), column_spec(1)] * 2
            + [row_spec(0), row_spec(1)],
            out_specs=[pl.BlockSpec((size, width), lambda t, where: (0, 0))] * pieces,
            scratch_shapes=[
                pltpu.VMEM((pieces * size, width), BF16),
                pltpu.VMEM((pieces * size, width), F32),
                pltpu.VMEM((2, pieces * size, 1), F32),
                pltpu.SemaphoreType.DMA((pieces,)),
            ],
        ),
        compiler_params=pltpu.CompilerParams(vmem_limit_bytes=40 * 1024 * 1024),
        cost_estimate=pl.CostEstimate(
            flops=12 * pieces * size * width * hidden,
            bytes_accessed=12 * width * hidden,
            transcendentals=0,
        ),
    )(where, *rows_in, *([table] * 4), *weights)


def final_kernel(count, residual_ref, *refs):
    out_ref = refs[-1]
    mid = residual_ref.shape[0] // 2
    for i in range(2):
        span = slice(i * mid, (i + 1) * mid)
        mix = refs[i][...].astype(F32)
        for ref in refs[2 + i : 2 * count : 2]:
            mix = mix + ref[...].astype(F32)
        out_ref[span] = (residual_ref[span] + mix).astype(BF16)


def final_sum(residual, pieces):
    return pl.pallas_call(
        functools.partial(final_kernel, len(pieces)),
        out_shape=jax.ShapeDtypeStruct(residual.shape, BF16),
        compiler_params=pltpu.CompilerParams(vmem_limit_bytes=16 * 1024 * 1024),
    )(residual, *[half for pair in pieces for half in pair])


def add_bf16(*terms):
    total = terms[0].astype(F32)
    for term in terms[1:]:
        total = total + term.astype(F32)
    return total.astype(BF16)


def on_device(
    hidden_in,
    queries,
    out_gate,
    draft_kv,
    cache_keys,
    cache_values,
    draft_len,
    cache_len,
    o_weight,
    norm_gain,
    route_ids,
    route_weights,
    w_gate,
    w_up,
    w_down,
):
    wide = lax.axis_size("wide")
    narrow = lax.axis_size("narrow")
    chip = lax.axis_index("wide")
    core = lax.axis_index("narrow")
    plane = 4
    planes = wide // plane
    assert narrow == 2 and wide % plane == 0
    experts = wide * narrow
    own_rows = hidden_in.shape[0]

    swap = [(0, 1), (1, 0)]
    own_weights = (w_gate, w_up, w_down)
    other_weights = tuple(lax.ppermute(w, "narrow", swap) for w in own_weights)

    chosen = route_ids[:, :, None] == jnp.arange(experts, dtype=jnp.int32)
    table = jnp.sum(jnp.where(chosen, route_weights[:, :, None], 0.0), axis=1)
    table = lax.all_gather(table, "wide", axis=0, tiled=False)

    arrays = (queries, out_gate, draft_kv, cache_keys, cache_values, draft_len, cache_len, o_weight)
    outgoing = attention(1 - core, own_rows, BF16, arrays)
    received = lax.ppermute(outgoing, "narrow", swap)
    kept = attention(core, own_rows, F32, arrays)
    residual, top, bottom = residual_norm(hidden_in, kept, received, norm_gain)

    def across(flip):
        pairs = [(i, i ^ flip) for i in range(wide)]
        return lambda a: lax.ppermute(a, "wide", pairs)

    def shifted(by):
        pairs = [(i, (i + by * plane) % wide) for i in range(wide)]
        return lambda a: lax.ppermute(a, "wide", pairs)

    over_x, over_y = across(1), across(2)
    order = sorted(range(planes), key=lambda s: min(s, planes - s))

    results = []
    for s in order:
        if s:
            mine_t, mine_b = shifted(s)(top), shifted(s)(bottom)
        else:
            mine_t, mine_b = top, bottom
        x_t, y_b = over_x(mine_t), over_y(mine_b)
        x_b, y_t = over_x(mine_b), over_y(mine_t)
        d_t, d_b = over_y(x_t), over_x(y_b)
        first = (chip + (planes - s) * plane) % wide
        own_expert = chip * narrow + core
        where = jnp.stack(
            [first, first ^ 1, first ^ 2, first ^ 3, own_expert, own_expert ^ 1]
        ).astype(jnp.int32)
        made = plane_experts(
            where, [mine_t, mine_b, x_t, x_b, y_t, y_b, d_t, d_b], table, own_weights, other_weights
        )
        mine_t, mine_b, x_t, x_b, y_t, y_b, d_t, d_b = made
        from_x_t, from_y_b = over_x(x_t), over_y(y_b)
        y_t = add_bf16(y_t, over_x(d_t))
        x_b = add_bf16(x_b, over_y(d_b))
        from_y_t, from_x_b = over_y(y_t), over_x(x_b)
        if s:
            sum_t = add_bf16(mine_t, from_x_t, from_y_t)
            sum_b = add_bf16(mine_b, from_x_b, from_y_b)
            results.append((shifted(planes - s)(sum_t), shifted(planes - s)(sum_b)))
        else:
            results += [(mine_t, mine_b), (from_x_t, from_x_b), (from_y_t, from_y_b)]
    return final_sum(residual, results)


def solution(mesh):
    placed = (
        P(("rep", "wide", "narrow"), None),
        P(("rep", "wide"), "narrow"),
        P(("rep", "wide"), "narrow"),
        P(None, ("rep", "wide"), None),
        P(("rep", "wide"), None, None),
        P(("rep", "wide"), None, None),
        P(("rep", "wide")),
        P(("rep", "wide")),
        P("narrow", None),
        P(),
        P(("rep", "wide", "narrow"), None),
        P(("rep", "wide", "narrow"), None),
        P(("wide", "narrow"), None, None),
        P(("wide", "narrow"), None, None),
        P(("wide", "narrow"), None, None),
    )
    return jax.shard_map(
        on_device,
        mesh=mesh,
        in_specs=placed,
        out_specs=P(("rep", "wide", "narrow"), None),
        check_vma=False,
    )
```

```python
import functools
import math

import jax
import jax.numpy as jnp
from jax import lax
from jax.experimental import pallas as pl
from jax.experimental.pallas import tpu as pltpu
from jax.sharding import PartitionSpec as P

BF16 = jnp.bfloat16
F32 = jnp.float32
LOWEST = -1e30


def _dot(a, b):
    return jnp.dot(a, b, preferred_element_type=F32)


def _dot_t(a, b):
    return lax.dot_general(a, b, (((1,), (1,)), ((), ())), preferred_element_type=F32)


def attention_kernel(
    half_ref,
    draft_len_ref,
    cache_len_ref,
    queries,
    out_gate,
    draft_kv,
    cache_keys,
    cache_values,
    o_weight,
    out_ref,
    q_buf,
    g_buf,
    d_buf,
    k_buf,
    v_buf,
    w_buf,
    attended,
    sems,
):
    half = half_ref[0]
    reqs, context_len, head_size = k_buf.shape
    rows = q_buf.shape[0]
    drafts = rows // reqs
    heads = q_buf.shape[1] // head_size
    row_span = pl.ds(pl.multiple_of(half * rows, rows), rows)
    req_span = pl.ds(half * reqs, reqs)
    copies = [
        pltpu.make_async_copy(queries.at[row_span], q_buf, sems.at[0]),
        pltpu.make_async_copy(cache_keys.at[req_span], k_buf, sems.at[1]),
        pltpu.make_async_copy(draft_kv.at[:, row_span], d_buf, sems.at[2]),
        pltpu.make_async_copy(cache_values.at[req_span], v_buf, sems.at[3]),
        pltpu.make_async_copy(out_gate.at[row_span], g_buf, sems.at[4]),
        pltpu.make_async_copy(o_weight, w_buf, sems.at[5]),
    ]
    for copy in copies:
        copy.start()
    for copy in copies[:3]:
        copy.wait()
    scale = 1.0 / math.sqrt(head_size)
    stacked = heads * drafts
    slot = lax.broadcasted_iota(jnp.int32, (stacked, context_len), 1)
    draft_slot = lax.broadcasted_iota(jnp.int32, (stacked, drafts), 1)
    draft_row = lax.broadcasted_iota(jnp.int32, (heads, drafts, drafts), 1).reshape(stacked, drafts)
    row_index = lax.broadcasted_iota(jnp.int32, (drafts, head_size), 0)
    probs = []
    for r in range(reqs):
        span = slice(r * drafts, (r + 1) * drafts)
        query = jnp.concatenate(
            [q_buf[span, h * head_size : (h + 1) * head_size] for h in range(heads)], axis=0
        )
        cache_len = cache_len_ref[half * reqs + r]
        draft_len = draft_len_ref[half * reqs + r]
        cache_scores = _dot_t(query, k_buf[r]) * scale
        draft_scores = _dot_t(query, d_buf[0, span]) * scale
        cache_scores = jnp.where(slot < cache_len, cache_scores, LOWEST)
        live = (draft_slot <= draft_row) & (draft_slot < draft_len)
        draft_scores = jnp.where(live, draft_scores, LOWEST)
        row_max = jnp.maximum(
            jnp.max(cache_scores, axis=-1, keepdims=True),
            jnp.max(draft_scores, axis=-1, keepdims=True),
        )
        cache_probs = jnp.exp(cache_scores - row_max)
        draft_probs = jnp.exp(draft_scores - row_max)
        denominator = jnp.sum(cache_probs, axis=-1, keepdims=True) + jnp.sum(
            draft_probs, axis=-1, keepdims=True
        )
        probs.append((cache_probs.astype(BF16), draft_probs.astype(BF16), denominator))
    copies[3].wait()
    copies[4].wait()
    for r in range(reqs):
        span = slice(r * drafts, (r + 1) * drafts)
        cache_probs, draft_probs, denominator = probs[r]
        context = _dot(cache_probs, v_buf[r]) + _dot(draft_probs, d_buf[1, span])
        context = context / denominator
        draft_len = draft_len_ref[half * reqs + r]
        for h in range(heads):
            cols = slice(h * head_size, (h + 1) * head_size)
            gate = jax.nn.sigmoid(g_buf[span, cols].astype(F32))
            piece = context[h * drafts : (h + 1) * drafts] * gate
            piece = jnp.where(row_index < draft_len, piece, 0.0)
            attended[span, cols] = piece.astype(BF16)
    copies[5].wait()
    rows_in = attended[...]
    width = out_ref.shape[1]
    tile = min(512, width)
    for c in range(0, width, tile):
        out_ref[:, c : c + tile] = _dot(rows_in, w_buf[:, c : c + tile]).astype(out_ref.dtype)


def attention(half, own_rows, out_dtype, arrays):
    queries, out_gate, draft_kv, cache_keys, cache_values, draft_len, cache_len, o_weight = arrays
    reqs_all, context_len, head_size = cache_keys.shape
    reqs = reqs_all * own_rows // queries.shape[0]
    width = o_weight.shape[1]
    inner = o_weight.shape[0]
    smem = pl.BlockSpec(memory_space=pltpu.SMEM)
    hbm = pl.BlockSpec(memory_space=pl.ANY)
    return pl.pallas_call(
        attention_kernel,
        out_shape=jax.ShapeDtypeStruct((own_rows, width), out_dtype),
        in_specs=[smem] * 3 + [hbm] * 6,
        out_specs=pl.BlockSpec(memory_space=pltpu.VMEM),
        scratch_shapes=[
            pltpu.VMEM((own_rows, inner), BF16),
            pltpu.VMEM((own_rows, inner), BF16),
            pltpu.VMEM((2, own_rows, head_size), BF16),
            pltpu.VMEM((reqs, context_len, head_size), BF16),
            pltpu.VMEM((reqs, context_len, head_size), BF16),
            pltpu.VMEM((inner, width), BF16),
            pltpu.VMEM((own_rows, inner), BF16),
            pltpu.SemaphoreType.DMA((6,)),
        ],
        compiler_params=pltpu.CompilerParams(vmem_limit_bytes=60 * 1024 * 1024),
        cost_estimate=pl.CostEstimate(
            flops=2 * own_rows * inner * (width + 2 * context_len),
            bytes_accessed=2 * inner * width + 4 * reqs * context_len * head_size,
            transcendentals=0,
        ),
    )(
        half.reshape(1),
        draft_len,
        cache_len,
        queries,
        out_gate,
        draft_kv,
        cache_keys,
        cache_values,
        o_weight,
    )


def norm_kernel(
    experts, hidden_ref, kept_ref, received_ref, gain_ref, ids_ref, weights_ref, residual_ref, sent_ref
):
    residual = hidden_ref[...].astype(F32) + kept_ref[...] + received_ref[...].astype(F32)
    width = residual.shape[1]
    spread = jnp.mean(residual * residual, axis=-1, keepdims=True)
    normed = (residual * lax.rsqrt(spread + 1e-06) * gain_ref[...]).astype(BF16)
    residual_ref[...] = residual
    sent_ref[:, :width] = normed
    rows, lanes = sent_ref.shape[0], sent_ref.shape[1] - width
    column = lax.broadcasted_iota(jnp.int32, (rows, lanes), 1)
    table = jnp.zeros((rows, lanes), F32)
    for k in range(ids_ref.shape[1]):
        index = ids_ref[:, k : k + 1]
        weight = weights_ref[:, k : k + 1]
        high = weight.astype(BF16).astype(F32)
        table = jnp.where(column == index, high, table)
        table = jnp.where(column == index + experts, weight - high, table)
    sent_ref[:, width:] = table.astype(BF16)


def residual_norm(hidden, kept, received, gain, ids, weights, experts):
    rows, width = hidden.shape
    lanes = -(-2 * experts // 128) * 128
    return pl.pallas_call(
        functools.partial(norm_kernel, experts),
        out_shape=(
            jax.ShapeDtypeStruct((rows, width), F32),
            jax.ShapeDtypeStruct((rows, width + lanes), BF16),
        ),
        compiler_params=pltpu.CompilerParams(vmem_limit_bytes=16 * 1024 * 1024),
    )(hidden, kept, received, gain.reshape(1, width), ids, weights)


def experts_kernel(spans, experts, where_ref, *refs):
    pieces = len(spans)
    rows_in = refs[:pieces]
    gates, ups, downs = (refs[pieces + 2 * i : pieces + 2 + 2 * i] for i in range(3))
    outs = refs[pieces + 6 : -2]
    rows, total = refs[-2:]
    width = total.shape[1]
    at = 0
    for ref, (start, size) in zip(rows_in, spans):
        rows[at : at + size] = ref[start : start + size]
        at += size
    table = rows[:, width:].astype(F32)
    column = lax.broadcasted_iota(jnp.int32, table.shape, 1)
    block = rows[:, :width]
    hidden = gates[0].shape[2]
    tile = min(256, hidden)
    for e in range(2):
        index = where_ref[e]
        chosen = (column == index) | (column == index + experts)
        weight = jnp.sum(jnp.where(chosen, table, 0.0), axis=1, keepdims=True)
        for c in range(0, hidden, tile):
            span = slice(c, c + tile)
            gate = _dot(block, gates[e][0, :, span])
            up = _dot(block, ups[e][0, :, span])
            act = (jax.nn.silu(gate) * up * weight).astype(BF16)
            added = _dot(act, downs[e][0, span, :])
            if e == 0 and c == 0:
                total[...] = added
            else:
                total[...] += added
    at = 0
    for out in outs:
        size = out.shape[0]
        out[...] = total[at : at + size].astype(BF16)
        at += size


def plane_experts(where, rows_in, experts, own_weights, other_weights):
    arrays = [piece[0] for piece in rows_in]
    spans = tuple(piece[1:] for piece in rows_in)
    sizes = [span[1] for span in spans]
    count = sum(sizes)
    padded = arrays[0].shape[1]
    width, hidden = own_weights[0].shape[1:]
    weights = [w for pair in zip(own_weights, other_weights) for w in pair]
    vmem = pl.BlockSpec(memory_space=pltpu.VMEM)
    return pl.pallas_call(
        functools.partial(experts_kernel, spans, experts),
        out_shape=tuple(jax.ShapeDtypeStruct((size, width), BF16) for size in sizes),
        in_specs=[pl.BlockSpec(memory_space=pltpu.SMEM)] + [vmem] * (len(spans) + 6),
        out_specs=[vmem] * len(spans),
        scratch_shapes=[pltpu.VMEM((count, padded), BF16), pltpu.VMEM((count, width), F32)],
        compiler_params=pltpu.CompilerParams(vmem_limit_bytes=24 * 1024 * 1024),
        cost_estimate=pl.CostEstimate(
            flops=12 * count * width * hidden,
            bytes_accessed=12 * width * hidden,
            transcendentals=0,
        ),
    )(where, *arrays, *weights)


def final_kernel(residual_ref, *refs):
    out_ref = refs[-1]
    mix = refs[0][...].astype(F32)
    for ref in refs[1:-1]:
        mix = mix + ref[...].astype(F32)
    out_ref[...] = (residual_ref[...] + mix).astype(BF16)


def final_sum(residual, pieces):
    return pl.pallas_call(
        final_kernel,
        out_shape=jax.ShapeDtypeStruct(residual.shape, BF16),
        compiler_params=pltpu.CompilerParams(vmem_limit_bytes=16 * 1024 * 1024),
    )(residual, *pieces)


def add_bf16(*terms):
    total = terms[0].astype(F32)
    for term in terms[1:]:
        total = total + term.astype(F32)
    return total.astype(BF16)


def on_device(
    hidden_in,
    queries,
    out_gate,
    draft_kv,
    cache_keys,
    cache_values,
    draft_len,
    cache_len,
    o_weight,
    norm_gain,
    route_ids,
    route_weights,
    w_gate,
    w_up,
    w_down,
):
    wide = lax.axis_size("wide")
    narrow = lax.axis_size("narrow")
    chip = lax.axis_index("wide")
    core = lax.axis_index("narrow")
    plane = 4
    planes = wide // plane
    assert narrow == 2 and wide % plane == 0 and planes > 1
    experts = wide * narrow
    own_rows, width = hidden_in.shape
    mid = own_rows // 2

    swap = [(0, 1), (1, 0)]
    own_weights = (w_gate, w_up, w_down)
    other_weights = tuple(lax.ppermute(w, "narrow", swap) for w in own_weights)

    arrays = (queries, out_gate, draft_kv, cache_keys, cache_values, draft_len, cache_len, o_weight)
    outgoing = attention(1 - core, own_rows, BF16, arrays)
    received = lax.ppermute(outgoing, "narrow", swap)
    kept = attention(core, own_rows, F32, arrays)
    residual, sent = residual_norm(
        hidden_in, kept, received, norm_gain, route_ids, route_weights, experts
    )

    def across(flip):
        pairs = [(i, i ^ flip) for i in range(wide)]
        return lambda a: lax.ppermute(a, "wide", pairs)

    def shifted(by):
        pairs = [(i, (i + by * plane) % wide) for i in range(wide)]
        return lambda a: lax.ppermute(a, "wide", pairs)

    over_x, over_y = across(1), across(2)
    own_expert = chip * narrow + core
    where = jnp.stack([own_expert, own_expert ^ 1]).astype(jnp.int32)

    def run_experts(rows_in):
        return plane_experts(where, rows_in, experts, own_weights, other_weights)

    together = lax.optimization_barrier

    blocks = [sent]
    from_x, from_y = [], []
    made = {}
    for k in range(planes):
        to_x, to_y = blocks[k], blocks[k]
        if k:
            to_x = jnp.concatenate([to_x, from_y[-1][mid:own_rows]])
            to_y = jnp.concatenate([to_y, from_x[-1][:mid]])
        group = [over_x(to_x), over_y(to_y)]
        if k < planes - 1:
            group.append(shifted(1)(blocks[k]))
        if k >= 2:
            s = k - 2
            made[s] = run_experts(
                [
                    (blocks[s], 0, own_rows),
                    (from_x[s], 0, own_rows),
                    (from_y[s], 0, own_rows),
                    (from_y[s + 1], own_rows, mid),
                    (from_x[s + 1], own_rows, mid),
                ]
            )
            group += made[s]
        group = together(tuple(group))
        from_x.append(group[0])
        from_y.append(group[1])
        if k < planes - 1:
            blocks.append(group[2])
        if k >= 2:
            made[k - 2] = group[-5:]

    order = list(range(1, planes)) + [0]
    last_y = over_y(from_x[-1][:mid])
    last_x = over_x(from_y[-1][mid:own_rows])
    results = []
    pending = None

    def experts_of(s):
        end = s == planes - 1
        return run_experts(
            [
                (blocks[s], 0, own_rows),
                (from_x[s], 0, own_rows),
                (from_y[s], 0, own_rows),
                (last_y, 0, mid) if end else (from_y[s + 1], own_rows, mid),
                (last_x, 0, mid) if end else (from_x[s + 1], own_rows, mid),
            ]
        )

    first = order[0]
    if first not in made:
        made[first] = experts_of(first)
    part_x, part_y = over_x(made[first][3]), over_y(made[first][4])
    group = [last_x, last_y, part_x, part_y]
    if planes - 2 not in made:
        made[planes - 2] = experts_of(planes - 2)
        group += made[planes - 2]
        group = together(tuple(group))
        made[planes - 2] = group[-5:]
    else:
        group = together(tuple(group))
    last_x, last_y, part_x, part_y = group[:4]

    for j, s in enumerate(order):
        own, for_x, for_y, _, _ = made[s]
        to_x = jnp.concatenate([for_x[:mid], add_bf16(for_x[mid:], part_y)])
        to_y = jnp.concatenate([add_bf16(for_y[:mid], part_x), for_y[mid:]])
        follows = order[j + 1] if j + 1 < planes else None
        if follows is not None and follows in made:
            to_x = jnp.concatenate([to_x, made[follows][3]])
            to_y = jnp.concatenate([to_y, made[follows][4]])
        group = [over_x(to_x), over_y(to_y)]
        if pending is not None:
            group.append(shifted(planes - pending[0])(pending[1]))
        if planes - 1 not in made:
            made[planes - 1] = experts_of(planes - 1)
            group += made[planes - 1]
            group = together(tuple(group))
            made[planes - 1] = group[-5:]
        else:
            group = together(tuple(group))
        if pending is not None:
            results.append(group[2])
        part_x, part_y = group[0][own_rows:], group[1][own_rows:]
        if s:
            pending = (s, add_bf16(own, group[0][:own_rows], group[1][:own_rows]))
        else:
            pending = None
            results += [own, group[0], group[1]]
        if follows is not None and part_x.shape[0] == 0:
            part_x, part_y = over_x(made[follows][3]), over_y(made[follows][4])
    return final_sum(residual, results)


def solution(mesh):
    placed = (
        P(("rep", "wide", "narrow"), None),
        P(("rep", "wide"), "narrow"),
        P(("rep", "wide"), "narrow"),
        P(None, ("rep", "wide"), None),
        P(("rep", "wide"), None, None),
        P(("rep", "wide"), None, None),
        P(("rep", "wide")),
        P(("rep", "wide")),
        P("narrow", None),
        P(),
        P(("rep", "wide", "narrow"), None),
        P(("rep", "wide", "narrow"), None),
        P(("wide", "narrow"), None, None),
        P(("wide", "narrow"), None, None),
        P(("wide", "narrow"), None, None),
    )
    return jax.shard_map(
        on_device,
        mesh=mesh,
        in_specs=placed,
        out_specs=P(("rep", "wide", "narrow"), None),
        check_vma=False,
    )
```

```python
import functools
import math

import jax
import jax.numpy as jnp
from jax import lax
from jax.experimental import pallas as pl
from jax.experimental.pallas import tpu as pltpu
from jax.sharding import PartitionSpec as P

BF16 = jnp.bfloat16
F32 = jnp.float32
LOWEST = -1e30


def _dot(a, b):
    return jnp.dot(a, b, preferred_element_type=F32)


def _dot_t(a, b):
    return lax.dot_general(a, b, (((1,), (1,)), ((), ())), preferred_element_type=F32)


def attention_kernel(
    experts,
    core_ref,
    draft_len_ref,
    cache_len_ref,
    ids_in,
    weights_in,
    gain_in,
    hidden_in,
    queries,
    out_gate,
    draft_kv,
    cache_keys,
    cache_values,
    o_weight,
    sent_ref,
    kept_ref,
    table_ref,
    gain_ref,
    q_buf,
    g_buf,
    d_buf,
    k_buf,
    v_buf,
    w_buf,
    h_buf,
    i_buf,
    r_buf,
    attended,
    sems,
):
    core = core_ref[0]
    reqs_all, context_len, head_size = k_buf.shape
    rows_all = q_buf.shape[0]
    rows, reqs = rows_all // 2, reqs_all // 2
    drafts = rows // reqs
    heads = q_buf.shape[1] // head_size
    groups = [[], [], [], []]

    def fetch(group, source, target):
        at = sum(len(g) for g in groups)
        copy = pltpu.make_async_copy(source, target, sems.at[at])
        copy.start()
        groups[group].append(copy)

    def half_rows(i):
        half = 1 - core if i == 0 else core
        return pl.ds(pl.multiple_of(half * rows, rows), rows)

    def half_reqs(i):
        half = 1 - core if i == 0 else core
        return pl.ds(half * reqs, reqs)

    fetch(0, ids_in, i_buf)
    fetch(0, weights_in, r_buf)
    for i in range(2):
        here = pl.ds(i * rows, rows)
        fetch(0, queries.at[half_rows(i)], q_buf.at[here])
        fetch(0, cache_keys.at[half_reqs(i)], k_buf.at[pl.ds(i * reqs, reqs)])
        fetch(0, draft_kv.at[:, half_rows(i)], d_buf.at[:, here])
    for i in range(2):
        here = pl.ds(i * rows, rows)
        fetch(1, cache_values.at[half_reqs(i)], v_buf.at[pl.ds(i * reqs, reqs)])
        fetch(1, out_gate.at[half_rows(i)], g_buf.at[here])
    fetch(2, o_weight, w_buf)
    fetch(3, hidden_in, h_buf)
    fetch(3, gain_in, gain_ref)

    for copy in groups[0]:
        copy.wait()
    row = lax.broadcasted_iota(jnp.int32, table_ref.shape[::-1], 0)
    table = jnp.zeros(row.shape, F32)
    for k in range(i_buf.shape[0]):
        index = i_buf[k : k + 1, :]
        weight = r_buf[k : k + 1, :]
        high = weight.astype(BF16).astype(F32)
        table = jnp.where(row == index, high, table)
        table = jnp.where(row == index + experts, weight - high, table)
    table_ref[...] = table.T.astype(BF16)
    scale = 1.0 / math.sqrt(head_size)
    stacked = heads * drafts
    slot = lax.broadcasted_iota(jnp.int32, (stacked, context_len), 1)
    draft_slot = lax.broadcasted_iota(jnp.int32, (stacked, drafts), 1)
    draft_row = lax.broadcasted_iota(jnp.int32, (heads, drafts, drafts), 1).reshape(stacked, drafts)
    row_index = lax.broadcasted_iota(jnp.int32, (drafts, head_size), 0)
    lens = []
    for r in range(reqs_all):
        half = 1 - core if r < reqs else core
        place = half * reqs + r % reqs
        lens.append((cache_len_ref[place], draft_len_ref[place]))
    probs = []
    for r in range(reqs_all):
        span = slice(r * drafts, (r + 1) * drafts)
        query = jnp.concatenate(
            [q_buf[span, h * head_size : (h + 1) * head_size] for h in range(heads)], axis=0
        )
        cache_len, draft_len = lens[r]
        cache_scores = _dot_t(query, k_buf[r]) * scale
        draft_scores = _dot_t(query, d_buf[0, span]) * scale
        cache_scores = jnp.where(slot < cache_len, cache_scores, LOWEST)
        live = (draft_slot <= draft_row) & (draft_slot < draft_len)
        draft_scores = jnp.where(live, draft_scores, LOWEST)
        row_max = jnp.maximum(
            jnp.max(cache_scores, axis=-1, keepdims=True),
            jnp.max(draft_scores, axis=-1, keepdims=True),
        )
        cache_probs = jnp.exp(cache_scores - row_max)
        draft_probs = jnp.exp(draft_scores - row_max)
        denominator = jnp.sum(cache_probs, axis=-1, keepdims=True) + jnp.sum(
            draft_probs, axis=-1, keepdims=True
        )
        probs.append((cache_probs.astype(BF16), draft_probs.astype(BF16), denominator))
    for copy in groups[1]:
        copy.wait()
    for r in range(reqs_all):
        span = slice(r * drafts, (r + 1) * drafts)
        cache_probs, draft_probs, denominator = probs[r]
        context = _dot(cache_probs, v_buf[r]) + _dot(draft_probs, d_buf[1, span])
        context = context / denominator
        draft_len = lens[r][1]
        for h in range(heads):
            cols = slice(h * head_size, (h + 1) * head_size)
            gate = jax.nn.sigmoid(g_buf[span, cols].astype(F32))
            piece = context[h * drafts : (h + 1) * drafts] * gate
            piece = jnp.where(row_index < draft_len, piece, 0.0)
            attended[span, cols] = piece.astype(BF16)
    for copy in groups[2] + groups[3]:
        copy.wait()
    rows_in = attended[...]
    width = sent_ref.shape[1]
    tile = min(512, width)
    for c in range(0, width, tile):
        cols = slice(c, c + tile)
        projected = _dot(rows_in, w_buf[:, cols])
        sent_ref[:, cols] = projected[:rows].astype(BF16)
        kept_ref[:, cols] = h_buf[:, cols].astype(F32) + projected[rows:]


def attention(core, experts, hidden, gain, ids, weights, arrays):
    queries, out_gate, draft_kv, cache_keys, cache_values, draft_len, cache_len, o_weight = arrays
    reqs_all, context_len, head_size = cache_keys.shape
    rows_all = queries.shape[0]
    own_rows = hidden.shape[0]
    inner, width = o_weight.shape
    lanes = -(-2 * experts // 128) * 128
    smem = pl.BlockSpec(memory_space=pltpu.SMEM)
    vmem = pl.BlockSpec(memory_space=pltpu.VMEM)
    hbm = pl.BlockSpec(memory_space=pl.ANY)
    ids, weights = ids.T, weights.T

    def in_hbm(a):
        return pltpu.with_memory_space_constraint(a, pltpu.HBM)

    return pl.pallas_call(
        functools.partial(attention_kernel, experts),
        out_shape=(
            jax.ShapeDtypeStruct((own_rows, width), BF16),
            jax.ShapeDtypeStruct((own_rows, width), F32),
            jax.ShapeDtypeStruct((own_rows, lanes), BF16),
            jax.ShapeDtypeStruct((1, width), F32),
        ),
        in_specs=[smem] * 3 + [hbm] * 10,
        out_specs=[vmem] * 4,
        scratch_shapes=[
            pltpu.VMEM((rows_all, inner), BF16),
            pltpu.VMEM((rows_all, inner), BF16),
            pltpu.VMEM((2, rows_all, head_size), BF16),
            pltpu.VMEM(cache_keys.shape, BF16),
            pltpu.VMEM(cache_values.shape, BF16),
            pltpu.VMEM((inner, width), BF16),
            pltpu.VMEM((own_rows, width), BF16),
            pltpu.VMEM(ids.shape, jnp.int32),
            pltpu.VMEM(weights.shape, F32),
            pltpu.VMEM((rows_all, inner), BF16),
            pltpu.SemaphoreType.DMA((15,)),
        ],
        compiler_params=pltpu.CompilerParams(vmem_limit_bytes=24 * 1024 * 1024),
        cost_estimate=pl.CostEstimate(
            flops=2 * rows_all * inner * (width + 2 * context_len),
            bytes_accessed=2 * inner * width + 4 * reqs_all * context_len * head_size,
            transcendentals=0,
        ),
    )(
        core.reshape(1),
        in_hbm(draft_len),
        in_hbm(cache_len),
        *map(
            in_hbm,
            (
                ids,
                weights,
                gain.reshape(1, width),
                hidden,
                queries,
                out_gate,
                draft_kv,
                cache_keys,
                cache_values,
                o_weight,
            ),
        ),
    )


def norm_kernel(kept_ref, received_ref, gain_ref, table_ref, residual_ref, sent_ref):
    residual = kept_ref[...] + received_ref[...].astype(F32)
    width = residual.shape[1]
    spread = jnp.mean(residual * residual, axis=-1, keepdims=True)
    normed = (residual * lax.rsqrt(spread + 1e-06) * gain_ref[...]).astype(BF16)
    residual_ref[...] = residual
    sent_ref[:, :width] = normed
    sent_ref[:, width:] = table_ref[...]


def residual_norm(kept, received, gain, table):
    rows, width = kept.shape
    return pl.pallas_call(
        norm_kernel,
        out_shape=(
            jax.ShapeDtypeStruct((rows, width), F32),
            jax.ShapeDtypeStruct((rows, width + table.shape[1]), BF16),
        ),
        compiler_params=pltpu.CompilerParams(vmem_limit_bytes=16 * 1024 * 1024),
    )(kept, received, gain, table)


def experts_kernel(spans, experts, where_ref, *refs):
    pieces = len(spans)
    rows_in = refs[:pieces]
    gates, ups, downs = (refs[pieces + 2 * i : pieces + 2 + 2 * i] for i in range(3))
    outs = refs[pieces + 6 : -2]
    rows, total = refs[-2:]
    width = total.shape[1]
    at = 0
    for ref, (start, size) in zip(rows_in, spans):
        rows[at : at + size] = ref[start : start + size]
        at += size
    table = rows[:, width:].astype(F32)
    column = lax.broadcasted_iota(jnp.int32, table.shape, 1)
    block = rows[:, :width]
    hidden = gates[0].shape[2]
    tile = min(256, hidden)
    for e in range(2):
        index = where_ref[e]
        chosen = (column == index) | (column == index + experts)
        weight = jnp.sum(jnp.where(chosen, table, 0.0), axis=1, keepdims=True)
        for c in range(0, hidden, tile):
            span = slice(c, c + tile)
            gate = _dot(block, gates[e][0, :, span])
            up = _dot(block, ups[e][0, :, span])
            act = (jax.nn.silu(gate) * up * weight).astype(BF16)
            added = _dot(act, downs[e][0, span, :])
            if e == 0 and c == 0:
                total[...] = added
            else:
                total[...] += added
    at = 0
    for out in outs:
        size = out.shape[0]
        out[...] = total[at : at + size].astype(BF16)
        at += size


def hold_kernel(where_ref, *refs):
    out_ref = refs[-1]
    for i in range(out_ref.shape[0]):
        out_ref[i] = where_ref[i]


def hold_weights(where, weights):
    vmem = pl.BlockSpec(memory_space=pltpu.VMEM)
    smem = pl.BlockSpec(memory_space=pltpu.SMEM)
    return pl.pallas_call(
        hold_kernel,
        out_shape=jax.ShapeDtypeStruct(where.shape, where.dtype),
        in_specs=[smem] + [vmem] * len(weights),
        out_specs=smem,
        compiler_params=pltpu.CompilerParams(vmem_limit_bytes=16 * 1024 * 1024),
        cost_estimate=pl.CostEstimate(flops=20_000_000_000, bytes_accessed=0, transcendentals=0),
    )(where, *weights)


def plane_experts(where, rows_in, experts, own_weights, other_weights):
    arrays = [piece[0] for piece in rows_in]
    spans = tuple(piece[1:] for piece in rows_in)
    sizes = [span[1] for span in spans]
    count = sum(sizes)
    padded = arrays[0].shape[1]
    width, hidden = own_weights[0].shape[1:]
    weights = [w for pair in zip(own_weights, other_weights) for w in pair]
    vmem = pl.BlockSpec(memory_space=pltpu.VMEM)
    return pl.pallas_call(
        functools.partial(experts_kernel, spans, experts),
        out_shape=tuple(jax.ShapeDtypeStruct((size, width), BF16) for size in sizes),
        in_specs=[pl.BlockSpec(memory_space=pltpu.SMEM)] + [vmem] * (len(spans) + 6),
        out_specs=[vmem] * len(spans),
        scratch_shapes=[pltpu.VMEM((count, padded), BF16), pltpu.VMEM((count, width), F32)],
        compiler_params=pltpu.CompilerParams(vmem_limit_bytes=24 * 1024 * 1024),
        cost_estimate=pl.CostEstimate(
            flops=12 * count * width * hidden,
            bytes_accessed=12 * width * hidden,
            transcendentals=0,
        ),
    )(where, *arrays, *weights)


def final_kernel(residual_ref, *refs):
    out_ref = refs[-1]
    mix = refs[0][...].astype(F32)
    for ref in refs[1:-1]:
        mix = mix + ref[...].astype(F32)
    out_ref[...] = (residual_ref[...] + mix).astype(BF16)


def final_sum(residual, pieces):
    return pl.pallas_call(
        final_kernel,
        out_shape=jax.ShapeDtypeStruct(residual.shape, BF16),
        compiler_params=pltpu.CompilerParams(vmem_limit_bytes=16 * 1024 * 1024),
    )(residual, *pieces)


def add_bf16(*terms):
    total = terms[0].astype(F32)
    for term in terms[1:]:
        total = total + term.astype(F32)
    return total.astype(BF16)


def on_device(
    hidden_in,
    queries,
    out_gate,
    draft_kv,
    cache_keys,
    cache_values,
    draft_len,
    cache_len,
    o_weight,
    norm_gain,
    route_ids,
    route_weights,
    w_gate,
    w_up,
    w_down,
):
    wide = lax.axis_size("wide")
    narrow = lax.axis_size("narrow")
    chip = lax.axis_index("wide")
    core = lax.axis_index("narrow")
    plane = 4
    planes = wide // plane
    assert narrow == 2 and wide % plane == 0 and planes > 1
    experts = wide * narrow
    own_rows, width = hidden_in.shape
    mid = own_rows // 2

    swap = [(0, 1), (1, 0)]
    own_weights = (w_gate, w_up, w_down)
    other_weights = tuple(lax.ppermute(w, "narrow", swap) for w in own_weights)

    arrays = (queries, out_gate, draft_kv, cache_keys, cache_values, draft_len, cache_len, o_weight)
    outgoing, kept, table, gain = attention(
        core, experts, hidden_in, norm_gain, route_ids, route_weights, arrays
    )
    received = lax.ppermute(outgoing, "narrow", swap)
    residual, sent = residual_norm(kept, received, gain, table)

    def across(flip):
        pairs = [(i, i ^ flip) for i in range(wide)]
        return lambda a: lax.ppermute(a, "wide", pairs)

    def shifted(by):
        pairs = [(i, (i + by * plane) % wide) for i in range(wide)]
        return lambda a: lax.ppermute(a, "wide", pairs)

    over_x, over_y = across(1), across(2)
    own_expert = chip * narrow + core
    where = jnp.stack([own_expert, own_expert ^ 1]).astype(jnp.int32)

    def run_experts(rows_in):
        return plane_experts(held[-1], rows_in, experts, own_weights, other_weights)

    held = [where]

    together = lax.optimization_barrier

    def pad_rows(a):
        return jnp.pad(a, ((0, 0), (0, sent.shape[1] - width)))

    blocks = [sent]
    from_x, from_y = [], []
    made = {}
    for k in range(planes):
        to_x, to_y = blocks[k], blocks[k]
        if k:
            to_x = jnp.concatenate([to_x, from_y[-1][mid:own_rows]])
            to_y = jnp.concatenate([to_y, from_x[-1][:mid]])
        group = [over_x(to_x), over_y(to_y)]
        if k < planes - 1:
            group.append(shifted(1)(blocks[k]))
        if k >= 2:
            s = k - 2
            made[s] = run_experts(
                [
                    (blocks[s], 0, own_rows),
                    (from_x[s], 0, own_rows),
                    (from_y[s], 0, own_rows),
                    (from_y[s + 1], own_rows, mid),
                    (from_x[s + 1], own_rows, mid),
                ]
            )
            group += made[s]
        if k < 2:
            group.append(hold_weights(held[-1], (own_weights + other_weights, ())[k]))
        group = together(tuple(group))
        if k < 2:
            held.append(group[-1])
        from_x.append(group[0])
        from_y.append(group[1])
        if k < planes - 1:
            blocks.append(group[2])
        if k >= 2:
            made[k - 2] = group[-5:]

    def experts_of(s):
        return run_experts(
            [
                (blocks[s], 0, own_rows),
                (from_x[s], 0, own_rows),
                (from_y[s], 0, own_rows),
                (from_y[s + 1], own_rows if s < planes - 1 else 0, mid),
                (from_x[s + 1], own_rows if s < planes - 1 else 0, mid),
            ]
        )

    order = list(range(1, planes)) + [0]
    first = order[0]
    if first not in made:
        made[first] = experts_of(first)
    to_x = jnp.concatenate([from_y[-1][mid:own_rows], pad_rows(made[first][3])])
    to_y = jnp.concatenate([from_x[-1][:mid], pad_rows(made[first][4])])
    group = [over_x(to_x), over_y(to_y)]
    later = planes - 2 not in made
    if later:
        group += experts_of(planes - 2)
    group = together(tuple(group))
    if later:
        made[planes - 2] = group[-5:]
    from_x.append(group[0])
    from_y.append(group[1])
    part_x, part_y = group[0][mid:, :width], group[1][mid:, :width]

    results = []
    pending = None
    carried = None
    for j, s in enumerate(order):
        own, for_x, for_y, _, _ = made[s]
        to_x = [for_x[:mid], add_bf16(for_x[mid:], part_y)]
        to_y = [add_bf16(for_y[:mid], part_x), for_y[mid:]]
        follows = order[j + 1] if j + 1 < planes else None
        if follows is not None:
            to_x.append(made[follows][3])
            to_y.append(made[follows][4])
        group = [over_x(jnp.concatenate(to_x)), over_y(jnp.concatenate(to_y))]
        if pending is not None:
            onward = 2 * pending[0] >= planes
            group.append(shifted(1 if onward else planes - pending[0])(pending[1]))
        later = planes - 1 not in made
        if later:
            group += experts_of(planes - 1)
        group = together(tuple(group))
        if later:
            made[planes - 1] = group[-5:]
        carried = None
        if pending is not None:
            if onward and pending[0] < planes - 1:
                carried = group[2]
            else:
                results.append(group[2])
        if follows is not None:
            part_x, part_y = group[0][own_rows:], group[1][own_rows:]
        arrived_x, arrived_y = group[0][:own_rows], group[1][:own_rows]
        if s:
            terms = [own, arrived_x, arrived_y]
            if carried is not None:
                terms.append(carried)
            pending = (s, add_bf16(*terms))
        else:
            results += [own, arrived_x, arrived_y]
    return final_sum(residual, results)


def solution(mesh):
    placed = (
        P(("rep", "wide", "narrow"), None),
        P(("rep", "wide"), "narrow"),
        P(("rep", "wide"), "narrow"),
        P(None, ("rep", "wide"), None),
        P(("rep", "wide"), None, None),
        P(("rep", "wide"), None, None),
        P(("rep", "wide")),
        P(("rep", "wide")),
        P("narrow", None),
        P(),
        P(("rep", "wide", "narrow"), None),
        P(("rep", "wide", "narrow"), None),
        P(("wide", "narrow"), None, None),
        P(("wide", "narrow"), None, None),
        P(("wide", "narrow"), None, None),
    )
    return jax.shard_map(
        on_device,
        mesh=mesh,
        in_specs=placed,
        out_specs=P(("rep", "wide", "narrow"), None),
        check_vma=False,
    )
```

```python
import functools
import math

import jax
import jax.numpy as jnp
from jax import lax
from jax.experimental import pallas as pl
from jax.experimental.pallas import tpu as pltpu
from jax.sharding import PartitionSpec as P

BF16 = jnp.bfloat16
F32 = jnp.float32
LOWEST = -1e30


def _dot(a, b):
    return jnp.dot(a, b, preferred_element_type=F32)


def _dot_t(a, b):
    return lax.dot_general(a, b, (((1,), (1,)), ((), ())), preferred_element_type=F32)


def attention_kernel(
    experts,
    core_ref,
    draft_len_ref,
    cache_len_ref,
    ids_in,
    weights_in,
    gain_in,
    hidden_in,
    queries,
    out_gate,
    draft_kv,
    cache_keys,
    cache_values,
    o_weight,
    sent_ref,
    kept_ref,
    table_ref,
    gain_ref,
    q_buf,
    g_buf,
    d_buf,
    k_buf,
    v_buf,
    w_buf,
    h_buf,
    i_buf,
    r_buf,
    attended,
    sems,
):
    core = core_ref[0]
    reqs_all, context_len, head_size = k_buf.shape
    rows_all = q_buf.shape[0]
    rows, reqs = rows_all // 2, reqs_all // 2
    drafts = rows // reqs
    heads = q_buf.shape[1] // head_size
    groups = [[], [], [], []]

    def fetch(group, source, target):
        at = sum(len(g) for g in groups)
        copy = pltpu.make_async_copy(source, target, sems.at[at])
        copy.start()
        groups[group].append(copy)

    def half_rows(i):
        half = 1 - core if i == 0 else core
        return pl.ds(pl.multiple_of(half * rows, rows), rows)

    def half_reqs(i):
        half = 1 - core if i == 0 else core
        return pl.ds(half * reqs, reqs)

    fetch(0, ids_in, i_buf)
    fetch(0, weights_in, r_buf)
    for i in range(2):
        here = pl.ds(i * rows, rows)
        fetch(0, queries.at[half_rows(i)], q_buf.at[here])
        fetch(0, cache_keys.at[half_reqs(i)], k_buf.at[pl.ds(i * reqs, reqs)])
        fetch(0, draft_kv.at[:, half_rows(i)], d_buf.at[:, here])
    for i in range(2):
        here = pl.ds(i * rows, rows)
        fetch(1, cache_values.at[half_reqs(i)], v_buf.at[pl.ds(i * reqs, reqs)])
        fetch(1, out_gate.at[half_rows(i)], g_buf.at[here])
    fetch(2, o_weight, w_buf)
    fetch(3, hidden_in, h_buf)
    fetch(3, gain_in, gain_ref)

    for copy in groups[0]:
        copy.wait()
    row = lax.broadcasted_iota(jnp.int32, table_ref.shape[::-1], 0)
    table = jnp.zeros(row.shape, F32)
    for k in range(i_buf.shape[0]):
        index = i_buf[k : k + 1, :]
        weight = r_buf[k : k + 1, :]
        high = weight.astype(BF16).astype(F32)
        table = jnp.where(row == index, high, table)
        table = jnp.where(row == index + experts, weight - high, table)
    table_ref[...] = table.T.astype(BF16)
    scale = 1.0 / math.sqrt(head_size)
    stacked = heads * drafts
    slot = lax.broadcasted_iota(jnp.int32, (stacked, context_len), 1)
    draft_slot = lax.broadcasted_iota(jnp.int32, (stacked, drafts), 1)
    draft_row = lax.broadcasted_iota(jnp.int32, (heads, drafts, drafts), 1).reshape(stacked, drafts)
    row_index = lax.broadcasted_iota(jnp.int32, (drafts, head_size), 0)
    lens = []
    for r in range(reqs_all):
        half = 1 - core if r < reqs else core
        place = half * reqs + r % reqs
        lens.append((cache_len_ref[place], draft_len_ref[place]))
    probs = []
    for r in range(reqs_all):
        span = slice(r * drafts, (r + 1) * drafts)
        query = jnp.concatenate(
            [q_buf[span, h * head_size : (h + 1) * head_size] for h in range(heads)], axis=0
        )
        cache_len, draft_len = lens[r]
        cache_scores = _dot_t(query, k_buf[r]) * scale
        draft_scores = _dot_t(query, d_buf[0, span]) * scale
        cache_scores = jnp.where(slot < cache_len, cache_scores, LOWEST)
        live = (draft_slot <= draft_row) & (draft_slot < draft_len)
        draft_scores = jnp.where(live, draft_scores, LOWEST)
        row_max = jnp.maximum(
            jnp.max(cache_scores, axis=-1, keepdims=True),
            jnp.max(draft_scores, axis=-1, keepdims=True),
        )
        cache_probs = jnp.exp(cache_scores - row_max)
        draft_probs = jnp.exp(draft_scores - row_max)
        denominator = jnp.sum(cache_probs, axis=-1, keepdims=True) + jnp.sum(
            draft_probs, axis=-1, keepdims=True
        )
        probs.append((cache_probs.astype(BF16), draft_probs.astype(BF16), denominator))
    for copy in groups[1]:
        copy.wait()
    for r in range(reqs_all):
        span = slice(r * drafts, (r + 1) * drafts)
        cache_probs, draft_probs, denominator = probs[r]
        context = _dot(cache_probs, v_buf[r]) + _dot(draft_probs, d_buf[1, span])
        context = context / denominator
        draft_len = lens[r][1]
        for h in range(heads):
            cols = slice(h * head_size, (h + 1) * head_size)
            gate = jax.nn.sigmoid(g_buf[span, cols].astype(F32))
            piece = context[h * drafts : (h + 1) * drafts] * gate
            piece = jnp.where(row_index < draft_len, piece, 0.0)
            attended[span, cols] = piece.astype(BF16)
    for copy in groups[2] + groups[3]:
        copy.wait()
    rows_in = attended[...]
    width = sent_ref.shape[1]
    tile = min(512, width)
    for c in range(0, width, tile):
        cols = slice(c, c + tile)
        projected = _dot(rows_in, w_buf[:, cols])
        sent_ref[:, cols] = projected[:rows].astype(BF16)
        kept_ref[:, cols] = h_buf[:, cols].astype(F32) + projected[rows:]


def attention(core, experts, hidden, gain, ids, weights, arrays):
    queries, out_gate, draft_kv, cache_keys, cache_values, draft_len, cache_len, o_weight = arrays
    reqs_all, context_len, head_size = cache_keys.shape
    rows_all = queries.shape[0]
    own_rows = hidden.shape[0]
    inner, width = o_weight.shape
    lanes = -(-2 * experts // 128) * 128
    smem = pl.BlockSpec(memory_space=pltpu.SMEM)
    vmem = pl.BlockSpec(memory_space=pltpu.VMEM)
    hbm = pl.BlockSpec(memory_space=pl.ANY)
    ids, weights = ids.T, weights.T

    def in_hbm(a):
        return pltpu.with_memory_space_constraint(a, pltpu.HBM)

    return pl.pallas_call(
        functools.partial(attention_kernel, experts),
        out_shape=(
            jax.ShapeDtypeStruct((own_rows, width), BF16),
            jax.ShapeDtypeStruct((own_rows, width), F32),
            jax.ShapeDtypeStruct((own_rows, lanes), BF16),
            jax.ShapeDtypeStruct((1, width), F32),
        ),
        in_specs=[smem] * 3 + [hbm] * 10,
        out_specs=[vmem] * 4,
        scratch_shapes=[
            pltpu.VMEM((rows_all, inner), BF16),
            pltpu.VMEM((rows_all, inner), BF16),
            pltpu.VMEM((2, rows_all, head_size), BF16),
            pltpu.VMEM(cache_keys.shape, BF16),
            pltpu.VMEM(cache_values.shape, BF16),
            pltpu.VMEM((inner, width), BF16),
            pltpu.VMEM((own_rows, width), BF16),
            pltpu.VMEM(ids.shape, jnp.int32),
            pltpu.VMEM(weights.shape, F32),
            pltpu.VMEM((rows_all, inner), BF16),
            pltpu.SemaphoreType.DMA((15,)),
        ],
        compiler_params=pltpu.CompilerParams(vmem_limit_bytes=24 * 1024 * 1024),
        cost_estimate=pl.CostEstimate(
            flops=2 * rows_all * inner * (width + 2 * context_len),
            bytes_accessed=2 * inner * width + 4 * reqs_all * context_len * head_size,
            transcendentals=0,
        ),
    )(
        core.reshape(1),
        in_hbm(draft_len),
        in_hbm(cache_len),
        *map(
            in_hbm,
            (
                ids,
                weights,
                gain.reshape(1, width),
                hidden,
                queries,
                out_gate,
                draft_kv,
                cache_keys,
                cache_values,
                o_weight,
            ),
        ),
    )


def norm_kernel(kept_ref, received_ref, gain_ref, table_ref, residual_ref, sent_ref):
    residual = kept_ref[...] + received_ref[...].astype(F32)
    width = residual.shape[1]
    spread = jnp.mean(residual * residual, axis=-1, keepdims=True)
    normed = (residual * lax.rsqrt(spread + 1e-06) * gain_ref[...]).astype(BF16)
    residual_ref[...] = residual
    sent_ref[:, :width] = normed
    sent_ref[:, width:] = table_ref[...]


def residual_norm(kept, received, gain, table):
    rows, width = kept.shape
    return pl.pallas_call(
        norm_kernel,
        out_shape=(
            jax.ShapeDtypeStruct((rows, width), F32),
            jax.ShapeDtypeStruct((rows, width + table.shape[1]), BF16),
        ),
        compiler_params=pltpu.CompilerParams(vmem_limit_bytes=16 * 1024 * 1024),
    )(kept, received, gain, table)


def experts_kernel(spans, experts, where_ref, *refs):
    pieces = len(spans)
    rows_in = refs[:pieces]
    gates, ups, downs = (refs[pieces + 2 * i : pieces + 2 + 2 * i] for i in range(3))
    outs = refs[pieces + 6 : -2]
    rows, total = refs[-2:]
    width = total.shape[1]
    at = 0
    for ref, (start, size) in zip(rows_in, spans):
        rows[at : at + size] = ref[start : start + size]
        at += size
    table = rows[:, width:].astype(F32)
    column = lax.broadcasted_iota(jnp.int32, table.shape, 1)
    block = rows[:, :width]
    hidden = gates[0].shape[2]
    tile = min(256, hidden)
    for e in range(2):
        index = where_ref[e]
        chosen = (column == index) | (column == index + experts)
        weight = jnp.sum(jnp.where(chosen, table, 0.0), axis=1, keepdims=True)
        for c in range(0, hidden, tile):
            span = slice(c, c + tile)
            gate = _dot(block, gates[e][0, :, span])
            up = _dot(block, ups[e][0, :, span])
            act = (jax.nn.silu(gate) * up * weight).astype(BF16)
            added = _dot(act, downs[e][0, span, :])
            if e == 0 and c == 0:
                total[...] = added
            else:
                total[...] += added
    at = 0
    for out in outs:
        size = out.shape[0]
        out[...] = total[at : at + size].astype(BF16)
        at += size


def hold_kernel(count, where_ref, *refs):
    sources, out_ref, held, sems = refs[:count], refs[count], refs[count + 1 : -1], refs[-1]
    copies = [
        pltpu.make_async_copy(source, target, sems.at[i])
        for i, (source, target) in enumerate(zip(sources, held))
    ]
    for copy in copies:
        copy.start()
    for i in range(out_ref.shape[0]):
        out_ref[i] = where_ref[i]
    for copy in copies:
        copy.wait()


def hold_weights(where, weights):
    count = len(weights)
    vmem = pl.BlockSpec(memory_space=pltpu.VMEM)
    smem = pl.BlockSpec(memory_space=pltpu.SMEM)
    return pl.pallas_call(
        functools.partial(hold_kernel, count),
        out_shape=[jax.ShapeDtypeStruct(where.shape, where.dtype)]
        + [jax.ShapeDtypeStruct(w.shape, w.dtype) for w in weights],
        in_specs=[smem] + [pl.BlockSpec(memory_space=pl.ANY)] * count,
        out_specs=[smem] + [vmem] * count,
        scratch_shapes=[pltpu.SemaphoreType.DMA((max(1, count),))],
        compiler_params=pltpu.CompilerParams(vmem_limit_bytes=16 * 1024 * 1024),
        cost_estimate=pl.CostEstimate(flops=20_000_000_000, bytes_accessed=0, transcendentals=0),
    )(where, *[pltpu.with_memory_space_constraint(w, pltpu.HBM) for w in weights])


def plane_experts(where, rows_in, experts, own_weights, other_weights):
    arrays = [piece[0] for piece in rows_in]
    spans = tuple(piece[1:] for piece in rows_in)
    sizes = [span[1] for span in spans]
    count = sum(sizes)
    padded = arrays[0].shape[1]
    width, hidden = own_weights[0].shape[1:]
    weights = [w for pair in zip(own_weights, other_weights) for w in pair]
    vmem = pl.BlockSpec(memory_space=pltpu.VMEM)
    return pl.pallas_call(
        functools.partial(experts_kernel, spans, experts),
        out_shape=tuple(jax.ShapeDtypeStruct((size, width), BF16) for size in sizes),
        in_specs=[pl.BlockSpec(memory_space=pltpu.SMEM)] + [vmem] * (len(spans) + 6),
        out_specs=[vmem] * len(spans),
        scratch_shapes=[pltpu.VMEM((count, padded), BF16), pltpu.VMEM((count, width), F32)],
        compiler_params=pltpu.CompilerParams(vmem_limit_bytes=24 * 1024 * 1024),
        cost_estimate=pl.CostEstimate(
            flops=12 * count * width * hidden,
            bytes_accessed=12 * width * hidden,
            transcendentals=0,
        ),
    )(where, *arrays, *weights)


def final_kernel(residual_ref, *refs):
    out_ref = refs[-1]
    mix = refs[0][...].astype(F32)
    for ref in refs[1:-1]:
        mix = mix + ref[...].astype(F32)
    out_ref[...] = (residual_ref[...] + mix).astype(BF16)


def final_sum(residual, pieces):
    return pl.pallas_call(
        final_kernel,
        out_shape=jax.ShapeDtypeStruct(residual.shape, BF16),
        compiler_params=pltpu.CompilerParams(vmem_limit_bytes=16 * 1024 * 1024),
    )(residual, *pieces)


def add_bf16(*terms):
    total = terms[0].astype(F32)
    for term in terms[1:]:
        total = total + term.astype(F32)
    return total.astype(BF16)


def on_device(
    hidden_in,
    queries,
    out_gate,
    draft_kv,
    cache_keys,
    cache_values,
    draft_len,
    cache_len,
    o_weight,
    norm_gain,
    route_ids,
    route_weights,
    w_gate,
    w_up,
    w_down,
):
    wide = lax.axis_size("wide")
    narrow = lax.axis_size("narrow")
    chip = lax.axis_index("wide")
    core = lax.axis_index("narrow")
    plane = 4
    planes = wide // plane
    assert narrow == 2 and wide % plane == 0 and planes > 1
    experts = wide * narrow
    own_rows, width = hidden_in.shape
    mid = own_rows // 2

    swap = [(0, 1), (1, 0)]
    own_weights = (w_gate, w_up, w_down)
    other_weights = tuple(lax.ppermute(w, "narrow", swap) for w in own_weights)

    arrays = (queries, out_gate, draft_kv, cache_keys, cache_values, draft_len, cache_len, o_weight)
    outgoing, kept, table, gain = attention(
        core, experts, hidden_in, norm_gain, route_ids, route_weights, arrays
    )
    received = lax.ppermute(outgoing, "narrow", swap)
    residual, sent = residual_norm(kept, received, gain, table)

    def across(flips):
        pairs = [
            (i * narrow + c, (i ^ flips[c]) * narrow + c) for i in range(wide) for c in range(narrow)
        ]
        return lambda a: lax.ppermute(a, ("wide", "narrow"), pairs)

    def shifted(by):
        pairs = [(i, (i + by * plane) % wide) for i in range(wide)]
        return lambda a: lax.ppermute(a, "wide", pairs)

    over_u, over_v = across((1, 2)), across((2, 1))
    own_expert = chip * narrow + core
    where = jnp.stack([own_expert, own_expert ^ 1]).astype(jnp.int32)

    def together(kept):
        names = list(kept)
        return dict(zip(names, lax.optimization_barrier(tuple(kept[n] for n in names))))

    b, u, v, made = {0: sent}, {}, {}, {}

    def experts_of(s):
        rows_in = [(b[s], 0, own_rows), (u[s], 0, own_rows), (v[s], 0, 2 * own_rows)]
        return plane_experts(held["where"], rows_in, experts, held["own"], held["other"])

    def phase(starts, experts_for=None, passed=()):
        kept = {(i, "moved"): start[2] for i, start in enumerate(starts)}
        if experts_for is not None:
            kept.update({(i, "made"): a for i, a in enumerate(experts_of(experts_for))})
        kept.update({(i, "passed"): a for i, a in enumerate(passed)})
        kept = together(kept)
        for i, (store, key, _) in enumerate(starts):
            store[key] = kept[i, "moved"]
        if experts_for is not None:
            made[experts_for] = [kept[i, "made"] for i in range(3)]
        return [kept[i, "passed"] for i in range(len(passed))]

    starts = [(u, 0, over_u(b[0])), (b, 1, shifted(1)(b[0]))]
    index, *weights = phase(starts, passed=hold_weights(where, own_weights + other_weights))
    held = {"where": index, "own": weights[:3], "other": weights[3:]}
    for k in range(1, planes):
        v[k - 1] = over_v(jnp.concatenate([b[k - 1], u[k - 1]]))
        starts = [(u, k, over_u(b[k]))]
        if k + 1 < planes:
            starts.append((b, k + 1, shifted(1)(b[k])))
        if k == 1:
            (held["where"],) = phase(starts, passed=hold_weights(held["where"], ()))
        else:
            phase(starts, experts_for=k - 2)
    v[planes - 1] = over_v(jnp.concatenate([b[planes - 1], u[planes - 1]]))
    order = list(range(1, planes)) + [0]
    (*waiting,) = phase([], experts_for=planes - 2, passed=[made[s][2] for s in sorted(made)])
    for s, array in enumerate(waiting):
        made[s][2] = array
    back_v, back_u, back_z, sums = {}, {}, {}, {}
    first, second = over_v(made[order[0]][2]), None
    phase([(v, planes - 1, v[planes - 1])])
    if planes > 3:
        second = over_v(made[order[1]][2])
    phase([(back_v, order[0], first)], experts_for=planes - 1)
    results = []
    for j, s in enumerate(order):
        own, for_u, _ = made[s]
        starts = [(back_u, s, over_u(add_bf16(for_u, back_v[s][own_rows:])))]
        if j + 2 < planes:
            starts.append((back_v, order[j + 1], second))
        elif s:
            starts.append((back_v, 0, over_v(made[0][2])))
        if j + 3 < planes:
            second = over_v(made[order[j + 2]][2])
        if j:
            last = order[j - 1]
            onward = 2 * last >= planes
            moved = shifted(1 if onward else planes - last)(sums[last])
            if last < planes - 1:
                starts.append((back_z, last, moved))
            else:
                back_z[last] = moved
        (made[0][2],) = phase(starts, passed=(made[0][2],))
        arrived = [own, back_v[s][:own_rows], back_u[s]]
        if s:
            if 2 * (s - 1) >= planes:
                arrived.append(back_z.pop(s - 1))
            sums[s] = add_bf16(*arrived)
        else:
            results += arrived + [back_z[last] for last in sorted(back_z)]
    return final_sum(residual, results)


def solution(mesh):
    placed = (
        P(("rep", "wide", "narrow"), None),
        P(("rep", "wide"), "narrow"),
        P(("rep", "wide"), "narrow"),
        P(None, ("rep", "wide"), None),
        P(("rep", "wide"), None, None),
        P(("rep", "wide"), None, None),
        P(("rep", "wide")),
        P(("rep", "wide")),
        P("narrow", None),
        P(),
        P(("rep", "wide", "narrow"), None),
        P(("rep", "wide", "narrow"), None),
        P(("wide", "narrow"), None, None),
        P(("wide", "narrow"), None, None),
        P(("wide", "narrow"), None, None),
    )
    return jax.shard_map(
        on_device,
        mesh=mesh,
        in_specs=placed,
        out_specs=P(("rep", "wide", "narrow"), None),
        check_vma=False,
    )
```

```python
import functools
import math

import jax
import jax.numpy as jnp
from jax import lax
from jax.experimental import pallas as pl
from jax.experimental.pallas import tpu as pltpu
from jax.sharding import PartitionSpec as P

BF16 = jnp.bfloat16
F32 = jnp.float32
LOWEST = -1e30
STEP_FLOPS = 200_000_000


def in_hbm(a):
    return pltpu.with_memory_space_constraint(a, pltpu.HBM)


def _dot(a, b):
    return jnp.dot(a, b, preferred_element_type=F32)


def _dot_t(a, b):
    return lax.dot_general(a, b, (((1,), (1,)), ((), ())), preferred_element_type=F32)


def attention_kernel(
    experts,
    core_ref,
    draft_len_ref,
    cache_len_ref,
    ids_in,
    weights_in,
    gain_in,
    hidden_in,
    queries,
    out_gate,
    draft_kv,
    cache_keys,
    cache_values,
    o_weight,
    sent_ref,
    kept_ref,
    table_ref,
    gain_ref,
    q_buf,
    g_buf,
    d_buf,
    k_buf,
    v_buf,
    w_buf,
    h_buf,
    i_buf,
    r_buf,
    attended,
    sems,
):
    core = core_ref[0]
    reqs_all, context_len, head_size = k_buf.shape
    rows_all = q_buf.shape[0]
    rows, reqs = rows_all // 2, reqs_all // 2
    drafts = rows // reqs
    heads = q_buf.shape[1] // head_size
    groups = [[], [], [], []]

    def fetch(group, source, target):
        at = sum(len(g) for g in groups)
        copy = pltpu.make_async_copy(source, target, sems.at[at])
        copy.start()
        groups[group].append(copy)

    def half_rows(i):
        half = 1 - core if i == 0 else core
        return pl.ds(pl.multiple_of(half * rows, rows), rows)

    def half_reqs(i):
        half = 1 - core if i == 0 else core
        return pl.ds(half * reqs, reqs)

    fetch(0, ids_in, i_buf)
    fetch(0, weights_in, r_buf)
    for i in range(2):
        here = pl.ds(i * rows, rows)
        fetch(0, queries.at[half_rows(i)], q_buf.at[here])
        fetch(0, cache_keys.at[half_reqs(i)], k_buf.at[pl.ds(i * reqs, reqs)])
        fetch(0, draft_kv.at[:, half_rows(i)], d_buf.at[:, here])
    for i in range(2):
        here = pl.ds(i * rows, rows)
        fetch(1, cache_values.at[half_reqs(i)], v_buf.at[pl.ds(i * reqs, reqs)])
        fetch(1, out_gate.at[half_rows(i)], g_buf.at[here])
    fetch(2, o_weight, w_buf)
    fetch(3, hidden_in, h_buf)
    fetch(3, gain_in, gain_ref)

    for copy in groups[0]:
        copy.wait()
    row = lax.broadcasted_iota(jnp.int32, table_ref.shape[::-1], 0)
    table = jnp.zeros(row.shape, F32)
    for k in range(i_buf.shape[0]):
        index = i_buf[k : k + 1, :]
        weight = r_buf[k : k + 1, :]
        high = weight.astype(BF16).astype(F32)
        table = jnp.where(row == index, high, table)
        table = jnp.where(row == index + experts, weight - high, table)
    table_ref[...] = table.T.astype(BF16)
    scale = 1.0 / math.sqrt(head_size)
    stacked = heads * drafts
    slot = lax.broadcasted_iota(jnp.int32, (stacked, context_len), 1)
    draft_slot = lax.broadcasted_iota(jnp.int32, (stacked, drafts), 1)
    draft_row = lax.broadcasted_iota(jnp.int32, (heads, drafts, drafts), 1).reshape(stacked, drafts)
    row_index = lax.broadcasted_iota(jnp.int32, (drafts, head_size), 0)
    lens = []
    for r in range(reqs_all):
        half = 1 - core if r < reqs else core
        place = half * reqs + r % reqs
        lens.append((cache_len_ref[place], draft_len_ref[place]))
    probs = []
    for r in range(reqs_all):
        span = slice(r * drafts, (r + 1) * drafts)
        query = jnp.concatenate(
            [q_buf[span, h * head_size : (h + 1) * head_size] for h in range(heads)], axis=0
        )
        cache_len, draft_len = lens[r]
        cache_scores = _dot_t(query, k_buf[r]) * scale
        draft_scores = _dot_t(query, d_buf[0, span]) * scale
        cache_scores = jnp.where(slot < cache_len, cache_scores, LOWEST)
        live = (draft_slot <= draft_row) & (draft_slot < draft_len)
        draft_scores = jnp.where(live, draft_scores, LOWEST)
        row_max = jnp.maximum(
            jnp.max(cache_scores, axis=-1, keepdims=True),
            jnp.max(draft_scores, axis=-1, keepdims=True),
        )
        cache_probs = jnp.exp(cache_scores - row_max)
        draft_probs = jnp.exp(draft_scores - row_max)
        denominator = jnp.sum(cache_probs, axis=-1, keepdims=True) + jnp.sum(
            draft_probs, axis=-1, keepdims=True
        )
        probs.append((cache_probs.astype(BF16), draft_probs.astype(BF16), denominator))
    for copy in groups[1]:
        copy.wait()
    for r in range(reqs_all):
        span = slice(r * drafts, (r + 1) * drafts)
        cache_probs, draft_probs, denominator = probs[r]
        context = _dot(cache_probs, v_buf[r]) + _dot(draft_probs, d_buf[1, span])
        context = context / denominator
        draft_len = lens[r][1]
        for h in range(heads):
            cols = slice(h * head_size, (h + 1) * head_size)
            gate = jax.nn.sigmoid(g_buf[span, cols].astype(F32))
            piece = context[h * drafts : (h + 1) * drafts] * gate
            piece = jnp.where(row_index < draft_len, piece, 0.0)
            attended[span, cols] = piece.astype(BF16)
    for copy in groups[2] + groups[3]:
        copy.wait()
    rows_in = attended[...]
    width = sent_ref.shape[1]
    tile = min(512, width)
    for c in range(0, width, tile):
        cols = slice(c, c + tile)
        projected = _dot(rows_in, w_buf[:, cols])
        sent_ref[:, cols] = projected[:rows].astype(BF16)
        kept_ref[:, cols] = h_buf[:, cols].astype(F32) + projected[rows:]


def attention(core, experts, hidden, gain, ids, weights, arrays):
    queries, out_gate, draft_kv, cache_keys, cache_values, draft_len, cache_len, o_weight = arrays
    reqs_all, context_len, head_size = cache_keys.shape
    rows_all = queries.shape[0]
    own_rows = hidden.shape[0]
    inner, width = o_weight.shape
    lanes = -(-2 * experts // 128) * 128
    smem = pl.BlockSpec(memory_space=pltpu.SMEM)
    vmem = pl.BlockSpec(memory_space=pltpu.VMEM)
    hbm = pl.BlockSpec(memory_space=pl.ANY)
    ids, weights = ids.T, weights.T

    return pl.pallas_call(
        functools.partial(attention_kernel, experts),
        out_shape=(
            jax.ShapeDtypeStruct((own_rows, width), BF16),
            jax.ShapeDtypeStruct((own_rows, width), F32),
            jax.ShapeDtypeStruct((own_rows, lanes), BF16),
            jax.ShapeDtypeStruct((1, width), F32),
        ),
        in_specs=[smem] * 3 + [hbm] * 10,
        out_specs=[vmem] * 4,
        scratch_shapes=[
            pltpu.VMEM((rows_all, inner), BF16),
            pltpu.VMEM((rows_all, inner), BF16),
            pltpu.VMEM((2, rows_all, head_size), BF16),
            pltpu.VMEM(cache_keys.shape, BF16),
            pltpu.VMEM(cache_values.shape, BF16),
            pltpu.VMEM((inner, width), BF16),
            pltpu.VMEM((own_rows, width), BF16),
            pltpu.VMEM(ids.shape, jnp.int32),
            pltpu.VMEM(weights.shape, F32),
            pltpu.VMEM((rows_all, inner), BF16),
            pltpu.SemaphoreType.DMA((15,)),
        ],
        compiler_params=pltpu.CompilerParams(vmem_limit_bytes=24 * 1024 * 1024),
        cost_estimate=pl.CostEstimate(
            flops=2 * rows_all * inner * (width + 2 * context_len),
            bytes_accessed=2 * inner * width + 4 * reqs_all * context_len * head_size,
            transcendentals=0,
        ),
    )(
        core.reshape(1),
        in_hbm(draft_len),
        in_hbm(cache_len),
        *map(
            in_hbm,
            (
                ids,
                weights,
                gain.reshape(1, width),
                hidden,
                queries,
                out_gate,
                draft_kv,
                cache_keys,
                cache_values,
                o_weight,
            ),
        ),
    )


def norm_kernel(kept_ref, received_ref, gain_ref, table_ref, residual_ref, sent_ref):
    residual = kept_ref[...] + received_ref[...].astype(F32)
    width = residual.shape[1]
    spread = jnp.mean(residual * residual, axis=-1, keepdims=True)
    normed = (residual * lax.rsqrt(spread + 1e-06) * gain_ref[...]).astype(BF16)
    residual_ref[...] = residual
    sent_ref[:, :width] = normed
    sent_ref[:, width:] = table_ref[...]


def residual_norm(kept, received, gain, table):
    rows, width = kept.shape
    return pl.pallas_call(
        norm_kernel,
        out_shape=(
            jax.ShapeDtypeStruct((rows, width), F32),
            jax.ShapeDtypeStruct((rows, width + table.shape[1]), BF16),
        ),
        compiler_params=pltpu.CompilerParams(vmem_limit_bytes=16 * 1024 * 1024),
    )(kept, received, gain, table)


def experts_kernel(spans, experts, where_ref, *refs):
    pieces = len(spans)
    rows_in = refs[:pieces]
    gates, ups, downs = (refs[pieces + 2 * i : pieces + 2 + 2 * i] for i in range(3))
    outs = refs[pieces + 6 : -2]
    rows, total = refs[-2:]
    width = total.shape[1]
    at = 0
    for ref, (start, size) in zip(rows_in, spans):
        rows[at : at + size] = ref[start : start + size]
        at += size
    table = rows[:, width:].astype(F32)
    column = lax.broadcasted_iota(jnp.int32, table.shape, 1)
    block = rows[:, :width]
    hidden = gates[0].shape[2]
    tile = min(256, hidden)
    for e in range(2):
        index = where_ref[e]
        chosen = (column == index) | (column == index + experts)
        weight = jnp.sum(jnp.where(chosen, table, 0.0), axis=1, keepdims=True)
        for c in range(0, hidden, tile):
            span = slice(c, c + tile)
            gate = _dot(block, gates[e][0, :, span])
            up = _dot(block, ups[e][0, :, span])
            act = (jax.nn.silu(gate) * up * weight).astype(BF16)
            added = _dot(act, downs[e][0, span, :])
            if e == 0 and c == 0:
                total[...] = added
            else:
                total[...] += added
    at = 0
    for out in outs:
        size = out.shape[0]
        out[...] = total[at : at + size].astype(BF16)
        at += size


def hold_kernel(count, where_ref, *refs):
    sources, out_ref, held, sems = refs[:count], refs[count], refs[count + 1 : -1], refs[-1]
    copies = [
        pltpu.make_async_copy(source, target, sems.at[i])
        for i, (source, target) in enumerate(zip(sources, held))
    ]
    for copy in copies:
        copy.start()
    for i in range(out_ref.shape[0]):
        out_ref[i] = where_ref[i]
    for copy in copies:
        copy.wait()


def hold_weights(where, weights):
    count = len(weights)
    vmem = pl.BlockSpec(memory_space=pltpu.VMEM)
    smem = pl.BlockSpec(memory_space=pltpu.SMEM)
    return pl.pallas_call(
        functools.partial(hold_kernel, count),
        out_shape=[jax.ShapeDtypeStruct(where.shape, where.dtype)]
        + [jax.ShapeDtypeStruct(w.shape, w.dtype) for w in weights],
        in_specs=[smem] + [pl.BlockSpec(memory_space=pl.ANY)] * count,
        out_specs=[smem] + [vmem] * count,
        scratch_shapes=[pltpu.SemaphoreType.DMA((max(1, count),))],
        compiler_params=pltpu.CompilerParams(vmem_limit_bytes=16 * 1024 * 1024),
        cost_estimate=pl.CostEstimate(flops=STEP_FLOPS, bytes_accessed=0, transcendentals=0),
    )(where, *weights)


def step_kernel(token_ref, out_ref):
    out_ref[...] = token_ref[...]


def step(token):
    return pl.pallas_call(
        step_kernel,
        out_shape=jax.ShapeDtypeStruct(token.shape, token.dtype),
        compiler_params=pltpu.CompilerParams(vmem_limit_bytes=16 * 1024 * 1024),
        cost_estimate=pl.CostEstimate(flops=STEP_FLOPS, bytes_accessed=0, transcendentals=0),
    )(token)


def plane_experts(where, rows_in, experts, own_weights, other_weights):
    arrays = [piece[0] for piece in rows_in]
    spans = tuple(piece[1:] for piece in rows_in)
    sizes = [span[1] for span in spans]
    count = sum(sizes)
    padded = arrays[0].shape[1]
    width, hidden = own_weights[0].shape[1:]
    weights = [w for pair in zip(own_weights, other_weights) for w in pair]
    vmem = pl.BlockSpec(memory_space=pltpu.VMEM)
    return pl.pallas_call(
        functools.partial(experts_kernel, spans, experts),
        out_shape=tuple(jax.ShapeDtypeStruct((size, width), BF16) for size in sizes),
        in_specs=[pl.BlockSpec(memory_space=pltpu.SMEM)] + [vmem] * (len(spans) + 6),
        out_specs=[vmem] * len(spans),
        scratch_shapes=[pltpu.VMEM((count, padded), BF16), pltpu.VMEM((count, width), F32)],
        compiler_params=pltpu.CompilerParams(vmem_limit_bytes=24 * 1024 * 1024),
        cost_estimate=pl.CostEstimate(flops=STEP_FLOPS, bytes_accessed=0, transcendentals=0),
    )(where, *arrays, *weights)


def final_kernel(token_ref, residual_ref, *refs):
    out_ref = refs[-1]
    mix = refs[0][...].astype(F32)
    for ref in refs[1:-1]:
        mix = mix + ref[...].astype(F32)
    out_ref[...] = (residual_ref[...] + mix).astype(BF16)


def final_sum(token, residual, pieces):
    return pl.pallas_call(
        final_kernel,
        out_shape=jax.ShapeDtypeStruct(residual.shape, BF16),
        compiler_params=pltpu.CompilerParams(vmem_limit_bytes=16 * 1024 * 1024),
    )(token, residual, *pieces)


def add_bf16(*terms):
    total = terms[0].astype(F32)
    for term in terms[1:]:
        total = total + term.astype(F32)
    return total.astype(BF16)


def on_device(
    hidden_in,
    queries,
    out_gate,
    draft_kv,
    cache_keys,
    cache_values,
    draft_len,
    cache_len,
    o_weight,
    norm_gain,
    route_ids,
    route_weights,
    w_gate,
    w_up,
    w_down,
):
    wide = lax.axis_size("wide")
    narrow = lax.axis_size("narrow")
    chip = lax.axis_index("wide")
    core = lax.axis_index("narrow")
    plane = 4
    planes = wide // plane
    assert narrow == 2 and wide % plane == 0 and planes > 1
    experts = wide * narrow
    own_rows, width = hidden_in.shape
    mid = own_rows // 2

    swap = [(0, 1), (1, 0)]
    own_weights = (w_gate, w_up, w_down)
    other_weights = [lax.ppermute(w, "narrow", swap) for w in own_weights]

    arrays = (queries, out_gate, draft_kv, cache_keys, cache_values, draft_len, cache_len, o_weight)
    outgoing, kept, table, gain = attention(
        core, experts, hidden_in, norm_gain, route_ids, route_weights, arrays
    )
    received = lax.ppermute(outgoing, "narrow", swap)
    residual, sent = residual_norm(kept, received, gain, table)

    def across(flips):
        pairs = [
            (i * narrow + c, (i ^ flips[c]) * narrow + c) for i in range(wide) for c in range(narrow)
        ]
        return lambda a: lax.ppermute(a, ("wide", "narrow"), pairs)

    def shifted(by):
        pairs = [(i, (i + by * plane) % wide) for i in range(wide)]
        return lambda a: lax.ppermute(a, "wide", pairs)

    over_u, over_v = across((1, 2)), across((2, 1))
    own_expert = chip * narrow + core
    where = jnp.stack([own_expert, own_expert ^ 1]).astype(jnp.int32)

    b, u, v, made = {0: sent}, {}, {}, {}
    token = jnp.zeros((8, 128), F32)

    def wait(*entries, passed=()):
        nonlocal token
        arrays = [store[key] for store, key in entries]
        token, *rest = lax.optimization_barrier((token, *arrays, *passed))
        for (store, key), array in zip(entries, rest):
            store[key] = array
        return rest[len(entries) :]

    def run_experts(s):
        rows_in = [(b[s], 0, own_rows), (u[s], 0, own_rows), (v[s], 0, 2 * own_rows)]
        made[s] = list(plane_experts(index, rows_in, experts, own_held, other_held))

    def made_entries(s):
        return [(made[s], i) for i in range(3)]

    b[1] = shifted(1)(b[0])
    u[0] = over_u(b[0])
    index, *held = hold_weights(where, [in_hbm(w) for w in own_weights] + other_weights)
    index, *held = wait((b, 1), (u, 0), passed=[index, *held])
    own_held, other_held = held[:3], held[3:]
    for k in range(1, planes):
        if k + 1 < planes:
            b[k + 1] = shifted(1)(b[k])
        u[k] = over_u(b[k])
        v[k - 1] = over_v(jnp.concatenate([b[k - 1], u[k - 1]]))
        token = step(token)
        entries = [(u, k)]
        if k + 1 < planes:
            entries.append((b, k + 1))
        if k > 1:
            run_experts(k - 2)
            entries += made_entries(k - 2)
        wait(*entries)
    v[planes - 1] = over_v(jnp.concatenate([b[planes - 1], u[planes - 1]]))
    token = step(token)
    run_experts(planes - 2)
    wait(*made_entries(planes - 2), *[(made[s], 2) for s in range(planes - 2)])

    half = (planes + 1) // 2
    order = list(range(half, planes - 1)) + list(range(1, half)) + [planes - 1, 0]
    back_v, back_u, back_z, sums = {}, {}, {}, {}
    for s in order[:2]:
        if s in made:
            back_v[s] = over_v(made[s][2])
    token = step(token)
    wait((v, planes - 1), (made[0], 2))
    run_experts(planes - 1)
    wait(*made_entries(planes - 1), *([(back_v, order[0])] if order[0] in back_v else []))
    for s in order[:2]:
        if s not in back_v:
            back_v[s] = over_v(made[s][2])
    results = []
    for j, s in enumerate(order):
        own, for_u, _ = made[s]
        if j:
            last = order[j - 1]
            onward = 2 * last >= planes
            back_z[last] = shifted(1 if onward else planes - last)(sums[last])
        if s == 0:
            token = step(token)
            wait((back_v, 0))
        back_u[s] = over_u(add_bf16(for_u, back_v[s][own_rows:]))
        if not s:
            break
        if j + 2 < planes:
            back_v[order[j + 2]] = over_v(made[order[j + 2]][2])
        token = step(token)
        carried = s - 1 in back_z and 2 * (s - 1) >= planes
        entries = [(back_u, s)]
        if order[j + 1]:
            entries += [(back_v, order[j + 1]), (made[0], 2)]
        if carried:
            entries.append((back_z, s - 1))
        wait(*entries)
        terms = [own, back_v[s][:own_rows], back_u[s]]
        if carried:
            terms.append(back_z.pop(s - 1))
        sums[s] = add_bf16(*terms)
    results = [made[0][0], back_v[0][:own_rows], back_u[0]]
    results += [back_z[s] for s in sorted(back_z)]
    return final_sum(token, residual, results)


def solution(mesh):
    placed = (
        P(("rep", "wide", "narrow"), None),
        P(("rep", "wide"), "narrow"),
        P(("rep", "wide"), "narrow"),
        P(None, ("rep", "wide"), None),
        P(("rep", "wide"), None, None),
        P(("rep", "wide"), None, None),
        P(("rep", "wide")),
        P(("rep", "wide")),
        P("narrow", None),
        P(),
        P(("rep", "wide", "narrow"), None),
        P(("rep", "wide", "narrow"), None),
        P(("wide", "narrow"), None, None),
        P(("wide", "narrow"), None, None),
        P(("wide", "narrow"), None, None),
    )
    return jax.shard_map(
        on_device,
        mesh=mesh,
        in_specs=placed,
        out_specs=P(("rep", "wide", "narrow"), None),
        check_vma=False,
    )
```

```python
import functools
import math

import jax
import jax.numpy as jnp
from jax import lax
from jax.experimental import pallas as pl
from jax.experimental.pallas import tpu as pltpu
from jax.sharding import PartitionSpec as P

BF16 = jnp.bfloat16
F32 = jnp.float32
LOWEST = -1e30
STEP_FLOPS = 200_000_000


def in_hbm(a):
    return pltpu.with_memory_space_constraint(a, pltpu.HBM)


def _dot(a, b):
    return jnp.dot(a, b, preferred_element_type=F32)


def _dot_t(a, b):
    return lax.dot_general(a, b, (((1,), (1,)), ((), ())), preferred_element_type=F32)


def attention_kernel(
    experts,
    core_ref,
    draft_len_ref,
    cache_len_ref,
    ids_in,
    weights_in,
    gain_in,
    hidden_in,
    queries,
    out_gate,
    draft_kv,
    cache_keys,
    cache_values,
    o_weight,
    sent_ref,
    kept_ref,
    table_ref,
    gain_ref,
    q_buf,
    g_buf,
    d_buf,
    k_buf,
    v_buf,
    w_buf,
    h_buf,
    i_buf,
    r_buf,
    attended,
    sems,
):
    core = core_ref[0]
    reqs_all, context_len, head_size = k_buf.shape
    rows_all = q_buf.shape[0]
    rows, reqs = rows_all // 2, reqs_all // 2
    drafts = rows // reqs
    heads = q_buf.shape[1] // head_size
    groups = [[], [], [], []]

    def fetch(group, source, target):
        at = sum(len(g) for g in groups)
        copy = pltpu.make_async_copy(source, target, sems.at[at])
        copy.start()
        groups[group].append(copy)

    def half_rows(i):
        half = 1 - core if i == 0 else core
        return pl.ds(pl.multiple_of(half * rows, rows), rows)

    def half_reqs(i):
        half = 1 - core if i == 0 else core
        return pl.ds(half * reqs, reqs)

    fetch(0, ids_in, i_buf)
    fetch(0, weights_in, r_buf)
    for i in range(2):
        here = pl.ds(i * rows, rows)
        fetch(0, queries.at[half_rows(i)], q_buf.at[here])
        fetch(0, cache_keys.at[half_reqs(i)], k_buf.at[pl.ds(i * reqs, reqs)])
        fetch(0, draft_kv.at[:, half_rows(i)], d_buf.at[:, here])
    for i in range(2):
        here = pl.ds(i * rows, rows)
        fetch(1, cache_values.at[half_reqs(i)], v_buf.at[pl.ds(i * reqs, reqs)])
        fetch(1, out_gate.at[half_rows(i)], g_buf.at[here])
    fetch(2, o_weight, w_buf)
    fetch(3, hidden_in, h_buf)
    fetch(3, gain_in, gain_ref)

    for copy in groups[0]:
        copy.wait()
    row = lax.broadcasted_iota(jnp.int32, table_ref.shape[::-1], 0)
    table = jnp.zeros(row.shape, F32)
    for k in range(i_buf.shape[0]):
        index = i_buf[k : k + 1, :]
        weight = r_buf[k : k + 1, :]
        high = weight.astype(BF16).astype(F32)
        table = jnp.where(row == index, high, table)
        table = jnp.where(row == index + experts, weight - high, table)
    table_ref[...] = table.T.astype(BF16)
    scale = 1.0 / math.sqrt(head_size)
    stacked = heads * drafts
    slot = lax.broadcasted_iota(jnp.int32, (stacked, context_len), 1)
    draft_slot = lax.broadcasted_iota(jnp.int32, (stacked, drafts), 1)
    draft_row = lax.broadcasted_iota(jnp.int32, (heads, drafts, drafts), 1).reshape(stacked, drafts)
    row_index = lax.broadcasted_iota(jnp.int32, (drafts, head_size), 0)
    lens = []
    for r in range(reqs_all):
        half = 1 - core if r < reqs else core
        place = half * reqs + r % reqs
        lens.append((cache_len_ref[place], draft_len_ref[place]))
    probs = []
    for r in range(reqs_all):
        span = slice(r * drafts, (r + 1) * drafts)
        query = jnp.concatenate(
            [q_buf[span, h * head_size : (h + 1) * head_size] for h in range(heads)], axis=0
        )
        cache_len, draft_len = lens[r]
        cache_scores = _dot_t(query, k_buf[r]) * scale
        draft_scores = _dot_t(query, d_buf[0, span]) * scale
        cache_scores = jnp.where(slot < cache_len, cache_scores, LOWEST)
        live = (draft_slot <= draft_row) & (draft_slot < draft_len)
        draft_scores = jnp.where(live, draft_scores, LOWEST)
        row_max = jnp.maximum(
            jnp.max(cache_scores, axis=-1, keepdims=True),
            jnp.max(draft_scores, axis=-1, keepdims=True),
        )
        cache_probs = jnp.exp(cache_scores - row_max)
        draft_probs = jnp.exp(draft_scores - row_max)
        denominator = jnp.sum(cache_probs, axis=-1, keepdims=True) + jnp.sum(
            draft_probs, axis=-1, keepdims=True
        )
        probs.append((cache_probs.astype(BF16), draft_probs.astype(BF16), denominator))
    for copy in groups[1]:
        copy.wait()
    for r in range(reqs_all):
        span = slice(r * drafts, (r + 1) * drafts)
        cache_probs, draft_probs, denominator = probs[r]
        context = _dot(cache_probs, v_buf[r]) + _dot(draft_probs, d_buf[1, span])
        context = context / denominator
        draft_len = lens[r][1]
        for h in range(heads):
            cols = slice(h * head_size, (h + 1) * head_size)
            gate = jax.nn.sigmoid(g_buf[span, cols].astype(F32))
            piece = context[h * drafts : (h + 1) * drafts] * gate
            piece = jnp.where(row_index < draft_len, piece, 0.0)
            attended[span, cols] = piece.astype(BF16)
    for copy in groups[2] + groups[3]:
        copy.wait()
    rows_in = attended[...]
    width = sent_ref.shape[1]
    tile = min(512, width)
    for c in range(0, width, tile):
        cols = slice(c, c + tile)
        projected = _dot(rows_in, w_buf[:, cols])
        sent_ref[:, cols] = projected[:rows].astype(BF16)
        kept_ref[:, cols] = h_buf[:, cols].astype(F32) + projected[rows:]


def attention(core, experts, hidden, gain, ids, weights, arrays):
    queries, out_gate, draft_kv, cache_keys, cache_values, draft_len, cache_len, o_weight = arrays
    reqs_all, context_len, head_size = cache_keys.shape
    rows_all = queries.shape[0]
    own_rows = hidden.shape[0]
    inner, width = o_weight.shape
    lanes = -(-2 * experts // 128) * 128
    smem = pl.BlockSpec(memory_space=pltpu.SMEM)
    vmem = pl.BlockSpec(memory_space=pltpu.VMEM)
    hbm = pl.BlockSpec(memory_space=pl.ANY)
    ids, weights = ids.T, weights.T

    return pl.pallas_call(
        functools.partial(attention_kernel, experts),
        out_shape=(
            jax.ShapeDtypeStruct((own_rows, width), BF16),
            jax.ShapeDtypeStruct((own_rows, width), F32),
            jax.ShapeDtypeStruct((own_rows, lanes), BF16),
            jax.ShapeDtypeStruct((1, width), F32),
        ),
        in_specs=[smem] * 3 + [hbm] * 10,
        out_specs=[vmem] * 4,
        scratch_shapes=[
            pltpu.VMEM((rows_all, inner), BF16),
            pltpu.VMEM((rows_all, inner), BF16),
            pltpu.VMEM((2, rows_all, head_size), BF16),
            pltpu.VMEM(cache_keys.shape, BF16),
            pltpu.VMEM(cache_values.shape, BF16),
            pltpu.VMEM((inner, width), BF16),
            pltpu.VMEM((own_rows, width), BF16),
            pltpu.VMEM(ids.shape, jnp.int32),
            pltpu.VMEM(weights.shape, F32),
            pltpu.VMEM((rows_all, inner), BF16),
            pltpu.SemaphoreType.DMA((15,)),
        ],
        compiler_params=pltpu.CompilerParams(vmem_limit_bytes=24 * 1024 * 1024),
        cost_estimate=pl.CostEstimate(
            flops=2 * rows_all * inner * (width + 2 * context_len),
            bytes_accessed=2 * inner * width + 4 * reqs_all * context_len * head_size,
            transcendentals=0,
        ),
    )(
        core.reshape(1),
        in_hbm(draft_len),
        in_hbm(cache_len),
        *map(
            in_hbm,
            (
                ids,
                weights,
                gain.reshape(1, width),
                hidden,
                queries,
                out_gate,
                draft_kv,
                cache_keys,
                cache_values,
                o_weight,
            ),
        ),
    )


def norm_kernel(kept_ref, received_ref, gain_ref, table_ref, residual_ref, sent_ref):
    residual = kept_ref[...] + received_ref[...].astype(F32)
    width = residual.shape[1]
    spread = jnp.mean(residual * residual, axis=-1, keepdims=True)
    normed = (residual * lax.rsqrt(spread + 1e-06) * gain_ref[...]).astype(BF16)
    residual_ref[...] = residual
    sent_ref[:, :width] = normed
    sent_ref[:, width:] = table_ref[...]


def residual_norm(kept, received, gain, table):
    rows, width = kept.shape
    return pl.pallas_call(
        norm_kernel,
        out_shape=(
            jax.ShapeDtypeStruct((rows, width), F32),
            jax.ShapeDtypeStruct((rows, width + table.shape[1]), BF16),
        ),
        compiler_params=pltpu.CompilerParams(vmem_limit_bytes=16 * 1024 * 1024),
    )(kept, received, gain, table)


def experts_kernel(spans, experts, where_ref, *refs):
    pieces = len(spans)
    rows_in = refs[:pieces]
    gates, ups, downs = (refs[pieces + 2 * i : pieces + 2 + 2 * i] for i in range(3))
    outs = refs[pieces + 6 : -2]
    rows, total = refs[-2:]
    width = total.shape[1]
    at = 0
    for ref, (start, size) in zip(rows_in, spans):
        rows[at : at + size] = ref[start : start + size]
        at += size
    table = rows[:, width:].astype(F32)
    column = lax.broadcasted_iota(jnp.int32, table.shape, 1)
    block = rows[:, :width]
    hidden = gates[0].shape[2]
    tile = min(256, hidden)
    for e in range(2):
        index = where_ref[e]
        chosen = (column == index) | (column == index + experts)
        weight = jnp.sum(jnp.where(chosen, table, 0.0), axis=1, keepdims=True)
        for c in range(0, hidden, tile):
            span = slice(c, c + tile)
            gate = _dot(block, gates[e][0, :, span])
            up = _dot(block, ups[e][0, :, span])
            act = (jax.nn.silu(gate) * up * weight).astype(BF16)
            added = _dot(act, downs[e][0, span, :])
            if e == 0 and c == 0:
                total[...] = added
            else:
                total[...] += added
    at = 0
    for out in outs:
        size = out.shape[0]
        out[...] = total[at : at + size].astype(BF16)
        at += size


def hold_kernel(count, where_ref, *refs):
    sources, out_ref, held, sems = refs[:count], refs[count], refs[count + 1 : -1], refs[-1]
    copies = [
        pltpu.make_async_copy(source, target, sems.at[i])
        for i, (source, target) in enumerate(zip(sources, held))
    ]
    for copy in copies:
        copy.start()
    for i in range(out_ref.shape[0]):
        out_ref[i] = where_ref[i]
    for copy in copies:
        copy.wait()


def hold_weights(where, weights):
    count = len(weights)
    vmem = pl.BlockSpec(memory_space=pltpu.VMEM)
    smem = pl.BlockSpec(memory_space=pltpu.SMEM)
    return pl.pallas_call(
        functools.partial(hold_kernel, count),
        out_shape=[jax.ShapeDtypeStruct(where.shape, where.dtype)]
        + [jax.ShapeDtypeStruct(w.shape, w.dtype) for w in weights],
        in_specs=[smem] + [pl.BlockSpec(memory_space=pl.ANY)] * count,
        out_specs=[smem] + [vmem] * count,
        scratch_shapes=[pltpu.SemaphoreType.DMA((max(1, count),))],
        compiler_params=pltpu.CompilerParams(vmem_limit_bytes=16 * 1024 * 1024),
        cost_estimate=pl.CostEstimate(flops=STEP_FLOPS, bytes_accessed=0, transcendentals=0),
    )(where, *weights)


def step_kernel(token_ref, out_ref):
    out_ref[...] = token_ref[...]


def step(token):
    return pl.pallas_call(
        step_kernel,
        out_shape=jax.ShapeDtypeStruct(token.shape, token.dtype),
        compiler_params=pltpu.CompilerParams(vmem_limit_bytes=16 * 1024 * 1024),
        cost_estimate=pl.CostEstimate(flops=STEP_FLOPS, bytes_accessed=0, transcendentals=0),
    )(token)


def plane_experts(where, rows_in, out_rows, experts, own_weights, other_weights):
    arrays = [piece[0] for piece in rows_in]
    spans = tuple(piece[1:] for piece in rows_in)
    count = sum(span[1] for span in spans)
    padded = arrays[0].shape[1]
    width, hidden = own_weights[0].shape[1:]
    weights = [w for pair in zip(own_weights, other_weights) for w in pair]
    vmem = pl.BlockSpec(memory_space=pltpu.VMEM)
    return pl.pallas_call(
        functools.partial(experts_kernel, spans, experts),
        out_shape=tuple(jax.ShapeDtypeStruct((size, width), BF16) for size in out_rows),
        in_specs=[pl.BlockSpec(memory_space=pltpu.SMEM)] + [vmem] * (len(spans) + 6),
        out_specs=[vmem] * len(out_rows),
        scratch_shapes=[pltpu.VMEM((count, padded), BF16), pltpu.VMEM((count, width), F32)],
        compiler_params=pltpu.CompilerParams(vmem_limit_bytes=24 * 1024 * 1024),
        cost_estimate=pl.CostEstimate(flops=STEP_FLOPS, bytes_accessed=0, transcendentals=0),
    )(where, *arrays, *weights)


def final_kernel(token_ref, residual_ref, *refs):
    out_ref = refs[-1]
    mix = refs[0][...].astype(F32)
    for ref in refs[1:-1]:
        mix = mix + ref[...].astype(F32)
    out_ref[...] = (residual_ref[...] + mix).astype(BF16)


def final_sum(token, residual, pieces):
    return pl.pallas_call(
        final_kernel,
        out_shape=jax.ShapeDtypeStruct(residual.shape, BF16),
        compiler_params=pltpu.CompilerParams(vmem_limit_bytes=16 * 1024 * 1024),
    )(token, residual, *pieces)


def add_bf16(*terms):
    total = terms[0].astype(F32)
    for term in terms[1:]:
        total = total + term.astype(F32)
    return total.astype(BF16)


def on_device(
    hidden_in,
    queries,
    out_gate,
    draft_kv,
    cache_keys,
    cache_values,
    draft_len,
    cache_len,
    o_weight,
    norm_gain,
    route_ids,
    route_weights,
    w_gate,
    w_up,
    w_down,
):
    wide = lax.axis_size("wide")
    narrow = lax.axis_size("narrow")
    chip = lax.axis_index("wide")
    core = lax.axis_index("narrow")
    plane = 4
    planes = wide // plane
    assert narrow == 2 and wide % plane == 0 and planes > 2
    experts = wide * narrow
    own_rows, width = hidden_in.shape
    mid = own_rows // 2

    swap = [(0, 1), (1, 0)]
    own_weights = (w_gate, w_up, w_down)
    other_weights = [lax.ppermute(w, "narrow", swap) for w in own_weights]

    arrays = (queries, out_gate, draft_kv, cache_keys, cache_values, draft_len, cache_len, o_weight)
    outgoing, kept, table, gain = attention(
        core, experts, hidden_in, norm_gain, route_ids, route_weights, arrays
    )
    received = lax.ppermute(outgoing, "narrow", swap)
    residual, sent = residual_norm(kept, received, gain, table)

    def across(flips):
        pairs = [
            (i * narrow + c, (i ^ flips[c]) * narrow + c) for i in range(wide) for c in range(narrow)
        ]
        return lambda a: lax.ppermute(a, ("wide", "narrow"), pairs)

    def shifted(by):
        pairs = [(i, (i + by * plane) % wide) for i in range(wide)]
        return lambda a: lax.ppermute(a, "wide", pairs)

    over_u, over_v = across((1, 2)), across((2, 1))
    own_expert = chip * narrow + core
    where = jnp.stack([own_expert, own_expert ^ 1]).astype(jnp.int32)

    b, u, v, made = {0: sent}, {}, {}, {}
    token = jnp.zeros((8, 128), F32)

    def wait(*entries, passed=()):
        nonlocal token
        arrays = [store[key] for store, key in entries]
        token, *rest = lax.optimization_barrier((token, *arrays, *passed))
        for (store, key), array in zip(entries, rest):
            store[key] = array
        return rest[len(entries) :]

    def run_experts(s):
        rows_in = [(b[s], 0, own_rows), (u[s], 0, own_rows), (v[s], 0, 2 * own_rows)]
        out_rows = [2 * own_rows] * 2 if s == 1 else [own_rows, own_rows, 2 * own_rows]
        made[s] = list(plane_experts(index, rows_in, out_rows, experts, own_held, other_held))

    def made_entries(s):
        return [(made[s], i) for i in range(len(made[s]))]

    b[1] = shifted(1)(b[0])
    u[0] = over_u(b[0])
    index, *held = hold_weights(where, [in_hbm(w) for w in own_weights] + other_weights)
    index, *held = wait((b, 1), (u, 0), passed=[index, *held])
    own_held, other_held = held[:3], held[3:]
    for k in range(1, planes):
        if k + 1 < planes:
            b[k + 1] = shifted(1)(b[k])
        u[k] = over_u(b[k])
        v[k - 1] = over_v(jnp.concatenate([b[k - 1], u[k - 1]]))
        token = step(token)
        entries = [(u, k)]
        if k + 1 < planes:
            entries.append((b, k + 1))
        if k > 1:
            run_experts(k - 2)
            entries += made_entries(k - 2)
        wait(*entries)
    v[planes - 1] = over_v(jnp.concatenate([b[planes - 1], u[planes - 1]]))
    whole = {}
    if 1 in made:
        whole[0] = shifted(planes - 1)(made[1][0])
    token = step(token)
    run_experts(planes - 2)
    wait(*made_entries(planes - 2), (made[1], 1))
    if 0 not in whole:
        whole[0] = shifted(planes - 1)(made[1][0])
    whole[1] = shifted(planes - 1)(made[1][1])

    half = max(2, (planes + 1) // 2)
    order = list(range(half, planes - 1)) + list(range(2, half)) + [planes - 1, 0]
    back_v, back_u, back_z, sums = {}, {}, {}, {}
    for s in order[:2]:
        if s in made and s:
            back_v[s] = over_v(made[s][2])
    token = step(token)
    wait((v, planes - 1))
    run_experts(planes - 1)
    wait(
        *made_entries(planes - 1),
        *([(back_v, order[0])] if order[0] in back_v else []),
        (whole, 0),
    )
    for s in order[:2]:
        if s not in back_v and s:
            back_v[s] = over_v(made[s][2])
    for j, s in enumerate(order[:-1]):
        own, for_u, _ = made[s]
        if j:
            last = order[j - 1]
            onward = 2 * last >= planes
            back_z[last] = shifted(1 if onward else planes - last)(sums[last])
        back_u[s] = over_u(add_bf16(for_u, back_v[s][own_rows:]))
        if order[j + 1] == 0:
            parts = [whole[0][:own_rows], whole[0][own_rows:], whole[1]]
            made[0] = [add_bf16(a, part) for a, part in zip(made[0], parts)]
            back_v[0] = over_v(made[0][2])
        elif order[j + 2]:
            back_v[order[j + 2]] = over_v(made[order[j + 2]][2])
        token = step(token)
        if j == 0:
            wait((whole, 1))
            token = step(token)
        carried = s - 1 in back_z and 2 * (s - 1) >= planes
        wait((back_u, s), *([(back_z, s - 1)] if carried else []))
        terms = [own, back_v[s][:own_rows], back_u[s]]
        if carried:
            terms.append(back_z.pop(s - 1))
        sums[s] = add_bf16(*terms)
        token = step(token)
        if order[j + 1]:
            wait((back_v, order[j + 1]), *[(made[0], i) for i in range(3)])
    last = planes - 1
    back_z[last] = shifted(1)(sums[last])
    token = step(token)
    wait((back_v, 0))
    back_u[0] = over_u(add_bf16(made[0][1], back_v[0][own_rows:]))
    results = [made[0][0], back_v[0][:own_rows], back_u[0]]
    results += [back_z[s] for s in sorted(back_z)]
    return final_sum(token, residual, results)


def solution(mesh):
    placed = (
        P(("rep", "wide", "narrow"), None),
        P(("rep", "wide"), "narrow"),
        P(("rep", "wide"), "narrow"),
        P(None, ("rep", "wide"), None),
        P(("rep", "wide"), None, None),
        P(("rep", "wide"), None, None),
        P(("rep", "wide")),
        P(("rep", "wide")),
        P("narrow", None),
        P(),
        P(("rep", "wide", "narrow"), None),
        P(("rep", "wide", "narrow"), None),
        P(("wide", "narrow"), None, None),
        P(("wide", "narrow"), None, None),
        P(("wide", "narrow"), None, None),
    )
    return jax.shard_map(
        on_device,
        mesh=mesh,
        in_specs=placed,
        out_specs=P(("rep", "wide", "narrow"), None),
        check_vma=False,
    )
```

```python
import functools
import math

import jax
import jax.numpy as jnp
from jax import lax
from jax.experimental import pallas as pl
from jax.experimental.pallas import tpu as pltpu
from jax.sharding import PartitionSpec as P

BF16 = jnp.bfloat16
F32 = jnp.float32
LOWEST = -1e30
STEP_FLOPS = 200_000_000


def in_hbm(a):
    return pltpu.with_memory_space_constraint(a, pltpu.HBM)


def _dot(a, b):
    return jnp.dot(a, b, preferred_element_type=F32)


def _dot_t(a, b):
    return lax.dot_general(a, b, (((1,), (1,)), ((), ())), preferred_element_type=F32)


def attention_kernel(
    experts,
    core_ref,
    draft_len_ref,
    cache_len_ref,
    ids_in,
    weights_in,
    gain_in,
    hidden_in,
    queries,
    out_gate,
    draft_kv,
    cache_keys,
    cache_values,
    o_weight,
    sent_ref,
    kept_ref,
    table_ref,
    gain_ref,
    q_buf,
    g_buf,
    d_buf,
    k_buf,
    v_buf,
    w_buf,
    h_buf,
    i_buf,
    r_buf,
    attended,
    sems,
):
    core = core_ref[0]
    reqs_all, context_len, head_size = k_buf.shape
    rows_all = q_buf.shape[0]
    rows, reqs = rows_all // 2, reqs_all // 2
    drafts = rows // reqs
    heads = q_buf.shape[1] // head_size
    groups = [[], [], [], []]

    def fetch(group, source, target):
        at = sum(len(g) for g in groups)
        copy = pltpu.make_async_copy(source, target, sems.at[at])
        copy.start()
        groups[group].append(copy)

    def half_rows(i):
        half = 1 - core if i == 0 else core
        return pl.ds(pl.multiple_of(half * rows, rows), rows)

    def half_reqs(i):
        half = 1 - core if i == 0 else core
        return pl.ds(half * reqs, reqs)

    fetch(0, ids_in, i_buf)
    fetch(0, weights_in, r_buf)
    for i in range(2):
        here = pl.ds(i * rows, rows)
        fetch(0, queries.at[half_rows(i)], q_buf.at[here])
        fetch(0, cache_keys.at[half_reqs(i)], k_buf.at[pl.ds(i * reqs, reqs)])
        fetch(0, draft_kv.at[:, half_rows(i)], d_buf.at[:, here])
    for i in range(2):
        here = pl.ds(i * rows, rows)
        fetch(1, cache_values.at[half_reqs(i)], v_buf.at[pl.ds(i * reqs, reqs)])
        fetch(1, out_gate.at[half_rows(i)], g_buf.at[here])
    fetch(2, o_weight, w_buf)
    fetch(3, hidden_in, h_buf)
    fetch(3, gain_in, gain_ref)

    for copy in groups[0]:
        copy.wait()
    row = lax.broadcasted_iota(jnp.int32, table_ref.shape[::-1], 0)
    table = jnp.zeros(row.shape, F32)
    for k in range(i_buf.shape[0]):
        index = i_buf[k : k + 1, :]
        weight = r_buf[k : k + 1, :]
        high = weight.astype(BF16).astype(F32)
        table = jnp.where(row == index, high, table)
        table = jnp.where(row == index + experts, weight - high, table)
    table_ref[...] = table.T.astype(BF16)
    scale = 1.0 / math.sqrt(head_size)
    stacked = heads * drafts
    slot = lax.broadcasted_iota(jnp.int32, (stacked, context_len), 1)
    draft_slot = lax.broadcasted_iota(jnp.int32, (stacked, drafts), 1)
    draft_row = lax.broadcasted_iota(jnp.int32, (heads, drafts, drafts), 1).reshape(stacked, drafts)
    row_index = lax.broadcasted_iota(jnp.int32, (drafts, head_size), 0)
    lens = []
    for r in range(reqs_all):
        half = 1 - core if r < reqs else core
        place = half * reqs + r % reqs
        lens.append((cache_len_ref[place], draft_len_ref[place]))
    probs = []
    for r in range(reqs_all):
        span = slice(r * drafts, (r + 1) * drafts)
        query = jnp.concatenate(
            [q_buf[span, h * head_size : (h + 1) * head_size] for h in range(heads)], axis=0
        )
        cache_len, draft_len = lens[r]
        cache_scores = _dot_t(query, k_buf[r]) * scale
        draft_scores = _dot_t(query, d_buf[0, span]) * scale
        cache_scores = jnp.where(slot < cache_len, cache_scores, LOWEST)
        live = (draft_slot <= draft_row) & (draft_slot < draft_len)
        draft_scores = jnp.where(live, draft_scores, LOWEST)
        row_max = jnp.maximum(
            jnp.max(cache_scores, axis=-1, keepdims=True),
            jnp.max(draft_scores, axis=-1, keepdims=True),
        )
        cache_probs = jnp.exp(cache_scores - row_max)
        draft_probs = jnp.exp(draft_scores - row_max)
        denominator = jnp.sum(cache_probs, axis=-1, keepdims=True) + jnp.sum(
            draft_probs, axis=-1, keepdims=True
        )
        probs.append((cache_probs.astype(BF16), draft_probs.astype(BF16), denominator))
    for copy in groups[1]:
        copy.wait()
    for r in range(reqs_all):
        span = slice(r * drafts, (r + 1) * drafts)
        cache_probs, draft_probs, denominator = probs[r]
        context = _dot(cache_probs, v_buf[r]) + _dot(draft_probs, d_buf[1, span])
        context = context / denominator
        draft_len = lens[r][1]
        for h in range(heads):
            cols = slice(h * head_size, (h + 1) * head_size)
            gate = jax.nn.sigmoid(g_buf[span, cols].astype(F32))
            piece = context[h * drafts : (h + 1) * drafts] * gate
            piece = jnp.where(row_index < draft_len, piece, 0.0)
            attended[span, cols] = piece.astype(BF16)
    for copy in groups[2] + groups[3]:
        copy.wait()
    rows_in = attended[...]
    width = sent_ref.shape[1]
    tile = min(512, width)
    for c in range(0, width, tile):
        cols = slice(c, c + tile)
        projected = _dot(rows_in, w_buf[:, cols])
        sent_ref[:, cols] = projected[:rows].astype(BF16)
        kept_ref[:, cols] = h_buf[:, cols].astype(F32) + projected[rows:]


def attention(core, experts, hidden, gain, ids, weights, arrays):
    queries, out_gate, draft_kv, cache_keys, cache_values, draft_len, cache_len, o_weight = arrays
    reqs_all, context_len, head_size = cache_keys.shape
    rows_all = queries.shape[0]
    own_rows = hidden.shape[0]
    inner, width = o_weight.shape
    lanes = -(-2 * experts // 128) * 128
    smem = pl.BlockSpec(memory_space=pltpu.SMEM)
    vmem = pl.BlockSpec(memory_space=pltpu.VMEM)
    hbm = pl.BlockSpec(memory_space=pl.ANY)
    ids, weights = ids.T, weights.T

    return pl.pallas_call(
        functools.partial(attention_kernel, experts),
        out_shape=(
            jax.ShapeDtypeStruct((own_rows, width), BF16),
            jax.ShapeDtypeStruct((own_rows, width), F32),
            jax.ShapeDtypeStruct((own_rows, lanes), BF16),
            jax.ShapeDtypeStruct((1, width), F32),
        ),
        in_specs=[smem] * 3 + [hbm] * 10,
        out_specs=[vmem] * 4,
        scratch_shapes=[
            pltpu.VMEM((rows_all, inner), BF16),
            pltpu.VMEM((rows_all, inner), BF16),
            pltpu.VMEM((2, rows_all, head_size), BF16),
            pltpu.VMEM(cache_keys.shape, BF16),
            pltpu.VMEM(cache_values.shape, BF16),
            pltpu.VMEM((inner, width), BF16),
            pltpu.VMEM((own_rows, width), BF16),
            pltpu.VMEM(ids.shape, jnp.int32),
            pltpu.VMEM(weights.shape, F32),
            pltpu.VMEM((rows_all, inner), BF16),
            pltpu.SemaphoreType.DMA((15,)),
        ],
        compiler_params=pltpu.CompilerParams(vmem_limit_bytes=24 * 1024 * 1024),
        cost_estimate=pl.CostEstimate(
            flops=2 * rows_all * inner * (width + 2 * context_len),
            bytes_accessed=2 * inner * width + 4 * reqs_all * context_len * head_size,
            transcendentals=0,
        ),
    )(
        core.reshape(1),
        in_hbm(draft_len),
        in_hbm(cache_len),
        *map(
            in_hbm,
            (
                ids,
                weights,
                gain.reshape(1, width),
                hidden,
                queries,
                out_gate,
                draft_kv,
                cache_keys,
                cache_values,
                o_weight,
            ),
        ),
    )


def norm_kernel(kept_ref, received_ref, gain_ref, table_ref, residual_ref, sent_ref):
    residual = kept_ref[...] + received_ref[...].astype(F32)
    width = residual.shape[1]
    spread = jnp.mean(residual * residual, axis=-1, keepdims=True)
    normed = (residual * lax.rsqrt(spread + 1e-06) * gain_ref[...]).astype(BF16)
    residual_ref[...] = residual
    sent_ref[:, :width] = normed
    sent_ref[:, width:] = table_ref[...]


def residual_norm(kept, received, gain, table):
    rows, width = kept.shape
    return pl.pallas_call(
        norm_kernel,
        out_shape=(
            jax.ShapeDtypeStruct((rows, width), F32),
            jax.ShapeDtypeStruct((rows, width + table.shape[1]), BF16),
        ),
        compiler_params=pltpu.CompilerParams(vmem_limit_bytes=16 * 1024 * 1024),
    )(kept, received, gain, table)


def experts_kernel(spans, experts, where_ref, *refs):
    pieces = len(spans)
    rows_in = refs[:pieces]
    gates, ups, downs = (refs[pieces + 2 * i : pieces + 2 + 2 * i] for i in range(3))
    outs = refs[pieces + 6 : -2]
    rows, total = refs[-2:]
    width = total.shape[1]
    at = 0
    for ref, (start, size) in zip(rows_in, spans):
        rows[at : at + size] = ref[start : start + size]
        at += size
    table = rows[:, width:].astype(F32)
    column = lax.broadcasted_iota(jnp.int32, table.shape, 1)
    block = rows[:, :width]
    hidden = gates[0].shape[2]
    tile = min(256, hidden)
    for e in range(2):
        index = where_ref[e]
        chosen = (column == index) | (column == index + experts)
        weight = jnp.sum(jnp.where(chosen, table, 0.0), axis=1, keepdims=True)
        for c in range(0, hidden, tile):
            span = slice(c, c + tile)
            gate = _dot(block, gates[e][0, :, span])
            up = _dot(block, ups[e][0, :, span])
            act = (jax.nn.silu(gate) * up * weight).astype(BF16)
            added = _dot(act, downs[e][0, span, :])
            if e == 0 and c == 0:
                total[...] = added
            else:
                total[...] += added
    at = 0
    for out in outs:
        size = out.shape[0]
        out[...] = total[at : at + size].astype(BF16)
        at += size


def hold_kernel(count, where_ref, *refs):
    sources, out_ref, held, sems = refs[:count], refs[count], refs[count + 1 : -1], refs[-1]
    copies = [
        pltpu.make_async_copy(source, target, sems.at[i])
        for i, (source, target) in enumerate(zip(sources, held))
    ]
    for copy in copies:
        copy.start()
    for i in range(out_ref.shape[0]):
        out_ref[i] = where_ref[i]
    for copy in copies:
        copy.wait()


def hold_weights(where, weights):
    count = len(weights)
    vmem = pl.BlockSpec(memory_space=pltpu.VMEM)
    smem = pl.BlockSpec(memory_space=pltpu.SMEM)
    return pl.pallas_call(
        functools.partial(hold_kernel, count),
        out_shape=[jax.ShapeDtypeStruct(where.shape, where.dtype)]
        + [jax.ShapeDtypeStruct(w.shape, w.dtype) for w in weights],
        in_specs=[smem] + [pl.BlockSpec(memory_space=pl.ANY)] * count,
        out_specs=[smem] + [vmem] * count,
        scratch_shapes=[pltpu.SemaphoreType.DMA((max(1, count),))],
        compiler_params=pltpu.CompilerParams(vmem_limit_bytes=16 * 1024 * 1024),
        cost_estimate=pl.CostEstimate(flops=STEP_FLOPS, bytes_accessed=0, transcendentals=0),
    )(where, *weights)


def step_kernel(token_ref, out_ref):
    out_ref[...] = token_ref[...]


def step(token):
    return pl.pallas_call(
        step_kernel,
        out_shape=jax.ShapeDtypeStruct(token.shape, token.dtype),
        compiler_params=pltpu.CompilerParams(vmem_limit_bytes=16 * 1024 * 1024),
        cost_estimate=pl.CostEstimate(flops=STEP_FLOPS, bytes_accessed=0, transcendentals=0),
    )(token)


def plane_experts(where, rows_in, out_rows, experts, own_weights, other_weights):
    arrays = [piece[0] for piece in rows_in]
    spans = tuple(piece[1:] for piece in rows_in)
    count = sum(span[1] for span in spans)
    padded = arrays[0].shape[1]
    width, hidden = own_weights[0].shape[1:]
    weights = [w for pair in zip(own_weights, other_weights) for w in pair]
    vmem = pl.BlockSpec(memory_space=pltpu.VMEM)
    return pl.pallas_call(
        functools.partial(experts_kernel, spans, experts),
        out_shape=tuple(jax.ShapeDtypeStruct((size, width), BF16) for size in out_rows),
        in_specs=[pl.BlockSpec(memory_space=pltpu.SMEM)] + [vmem] * (len(spans) + 6),
        out_specs=[vmem] * len(out_rows),
        scratch_shapes=[pltpu.VMEM((count, padded), BF16), pltpu.VMEM((count, width), F32)],
        compiler_params=pltpu.CompilerParams(vmem_limit_bytes=24 * 1024 * 1024),
        cost_estimate=pl.CostEstimate(flops=STEP_FLOPS, bytes_accessed=0, transcendentals=0),
    )(where, *arrays, *weights)


def final_kernel(token_ref, residual_ref, *refs):
    out_ref = refs[-1]
    mix = refs[0][...].astype(F32)
    for ref in refs[1:-1]:
        mix = mix + ref[...].astype(F32)
    out_ref[...] = (residual_ref[...] + mix).astype(BF16)


def final_sum(token, residual, pieces):
    return pl.pallas_call(
        final_kernel,
        out_shape=jax.ShapeDtypeStruct(residual.shape, BF16),
        compiler_params=pltpu.CompilerParams(vmem_limit_bytes=16 * 1024 * 1024),
    )(token, residual, *pieces)


def add_bf16(*terms):
    total = terms[0].astype(F32)
    for term in terms[1:]:
        total = total + term.astype(F32)
    return total.astype(BF16)


def on_device(
    hidden_in,
    queries,
    out_gate,
    draft_kv,
    cache_keys,
    cache_values,
    draft_len,
    cache_len,
    o_weight,
    norm_gain,
    route_ids,
    route_weights,
    w_gate,
    w_up,
    w_down,
):
    wide = lax.axis_size("wide")
    narrow = lax.axis_size("narrow")
    chip = lax.axis_index("wide")
    core = lax.axis_index("narrow")
    plane = 4
    planes = wide // plane
    assert narrow == 2 and wide % plane == 0 and planes > 2
    experts = wide * narrow
    own_rows, width = hidden_in.shape
    mid = own_rows // 2

    swap = [(0, 1), (1, 0)]
    own_weights = (w_gate, w_up, w_down)
    other_weights = [lax.ppermute(w, "narrow", swap) for w in own_weights]

    arrays = (queries, out_gate, draft_kv, cache_keys, cache_values, draft_len, cache_len, o_weight)
    outgoing, kept, table, gain = attention(
        core, experts, hidden_in, norm_gain, route_ids, route_weights, arrays
    )
    received = lax.ppermute(outgoing, "narrow", swap)
    residual, sent = residual_norm(kept, received, gain, table)

    def across(flips):
        pairs = [
            (i * narrow + c, (i ^ flips[c]) * narrow + c) for i in range(wide) for c in range(narrow)
        ]
        return lambda a: lax.ppermute(a, ("wide", "narrow"), pairs)

    def shifted(by):
        pairs = [(i, (i + by * plane) % wide) for i in range(wide)]
        return lambda a: lax.ppermute(a, "wide", pairs)

    over_u, over_v = across((1, 2)), across((2, 1))
    own_expert = chip * narrow + core
    where = jnp.stack([own_expert, own_expert ^ 1]).astype(jnp.int32)

    b, u, v, made = {0: sent}, {}, {}, {}
    token = jnp.zeros((8, 128), F32)

    def wait(*entries, passed=()):
        nonlocal token
        arrays = [store[key] for store, key in entries]
        token, *rest = lax.optimization_barrier((token, *arrays, *passed))
        for (store, key), array in zip(entries, rest):
            store[key] = array
        return rest[len(entries) :]

    def run_experts(s):
        rows_in = [(b[s], 0, own_rows), (u[s], 0, own_rows), (v[s], 0, 2 * own_rows)]
        out_rows = [2 * own_rows] * 2 if s == 1 else [own_rows, own_rows, 2 * own_rows]
        made[s] = list(plane_experts(index, rows_in, out_rows, experts, own_held, other_held))

    def made_entries(s):
        return [(made[s], i) for i in range(len(made[s]))]

    b[1] = shifted(1)(b[0])
    u[0] = over_u(b[0])
    index, *held = hold_weights(where, [in_hbm(w) for w in own_weights] + other_weights)
    index, *held = wait((b, 1), (u, 0), passed=[index, *held])
    own_held, other_held = held[:3], held[3:]
    for k in range(1, planes):
        if k + 1 < planes:
            b[k + 1] = shifted(1)(b[k])
        u[k] = over_u(b[k])
        v[k - 1] = over_v(jnp.concatenate([b[k - 1], u[k - 1]]))
        token = step(token)
        entries = [(u, k)]
        if k + 1 < planes:
            entries.append((b, k + 1))
        if k > 1:
            run_experts(k - 2)
            entries += made_entries(k - 2)
        wait(*entries)
    v[planes - 1] = over_v(jnp.concatenate([b[planes - 1], u[planes - 1]]))
    whole = {}
    if 1 in made:
        whole[0] = shifted(planes - 1)(made[1][0])
    token = step(token)
    run_experts(planes - 2)
    wait(*made_entries(planes - 2), (made[1], 1))
    if 0 not in whole:
        whole[0] = shifted(planes - 1)(made[1][0])
    whole[1] = shifted(planes - 1)(made[1][1])

    half = max(2, (planes + 1) // 2)
    order = list(range(half, planes - 1)) + list(range(2, half)) + [planes - 1, 0]
    back_v, back_u, back_z, sums = {}, {}, {}, {}
    for s in order[:2]:
        if s in made and s:
            back_v[s] = over_v(made[s][2])
    token = step(token)
    wait((v, planes - 1))
    run_experts(planes - 1)
    wait(*made_entries(planes - 1))
    for s in order[:2]:
        if s not in back_v and s:
            back_v[s] = over_v(made[s][2])
    token = step(token)
    wait((back_v, order[0]), (whole, 0))
    for j, s in enumerate(order[:-1]):
        own, for_u, _ = made[s]
        if j:
            last = order[j - 1]
            onward = 2 * last >= planes
            back_z[last] = shifted(1 if onward else planes - last)(sums[last])
        back_u[s] = over_u(add_bf16(for_u, back_v[s][own_rows:]))
        if j + 2 < planes - 1 and order[j + 2]:
            back_v[order[j + 2]] = over_v(made[order[j + 2]][2])
        token = step(token)
        carried = s - 1 in back_z and 2 * (s - 1) >= planes
        wait(
            (back_u, s),
            *([(back_z, s - 1)] if carried else []),
            *([] if order[j + 1] else [(back_v, 0)]),
            *([] if j else [(whole, 1)]),
            *([(back_v, order[j + 1])] if order[j + 1] else []),
        )
        if j == 0:
            parts = [whole[0][:own_rows], whole[0][own_rows:], whole[1]]
            made[0] = [add_bf16(a, part) for a, part in zip(made[0], parts)]
            back_v[0] = over_v(made[0][2])
        terms = [own, back_v[s][:own_rows], back_u[s]]
        if carried:
            terms.append(back_z.pop(s - 1))
        sums[s] = add_bf16(*terms)
        token = step(token)
    last = planes - 1
    back_z[last] = shifted(1)(sums[last])
    back_u[0] = over_u(add_bf16(made[0][1], back_v[0][own_rows:]))
    results = [made[0][0], back_v[0][:own_rows], back_u[0]]
    results += [back_z[s] for s in sorted(back_z)]
    return final_sum(token, residual, results)


def solution(mesh):
    placed = (
        P(("rep", "wide", "narrow"), None),
        P(("rep", "wide"), "narrow"),
        P(("rep", "wide"), "narrow"),
        P(None, ("rep", "wide"), None),
        P(("rep", "wide"), None, None),
        P(("rep", "wide"), None, None),
        P(("rep", "wide")),
        P(("rep", "wide")),
        P("narrow", None),
        P(),
        P(("rep", "wide", "narrow"), None),
        P(("rep", "wide", "narrow"), None),
        P(("wide", "narrow"), None, None),
        P(("wide", "narrow"), None, None),
        P(("wide", "narrow"), None, None),
    )
    return jax.shard_map(
        on_device,
        mesh=mesh,
        in_specs=placed,
        out_specs=P(("rep", "wide", "narrow"), None),
        check_vma=False,
    )
```

```python
import functools
import math

import jax
import jax.numpy as jnp
from jax import lax
from jax.experimental import pallas as pl
from jax.experimental.pallas import tpu as pltpu
from jax.sharding import PartitionSpec as P

BF16 = jnp.bfloat16
F32 = jnp.float32
LOWEST = -1e30
STEP_FLOPS = 200_000_000


def in_hbm(a):
    return pltpu.with_memory_space_constraint(a, pltpu.HBM)


def _dot(a, b):
    return jnp.dot(a, b, preferred_element_type=F32)


def _dot_t(a, b):
    return lax.dot_general(a, b, (((1,), (1,)), ((), ())), preferred_element_type=F32)


def attention_kernel(
    experts,
    core_ref,
    draft_len_ref,
    cache_len_ref,
    ids_in,
    weights_in,
    gain_in,
    hidden_in,
    queries,
    out_gate,
    draft_kv,
    cache_keys,
    cache_values,
    o_weight,
    sent_ref,
    kept_ref,
    table_ref,
    gain_ref,
    q_buf,
    g_buf,
    d_buf,
    k_buf,
    v_buf,
    w_buf,
    h_buf,
    i_buf,
    r_buf,
    attended,
    sems,
):
    core = core_ref[0]
    reqs_all, context_len, head_size = k_buf.shape
    rows_all = q_buf.shape[0]
    rows, reqs = rows_all // 2, reqs_all // 2
    drafts = rows // reqs
    heads = q_buf.shape[1] // head_size
    groups = [[], [], [], []]

    def fetch(group, source, target):
        at = sum(len(g) for g in groups)
        copy = pltpu.make_async_copy(source, target, sems.at[at])
        copy.start()
        groups[group].append(copy)

    def half_rows(i):
        half = 1 - core if i == 0 else core
        return pl.ds(pl.multiple_of(half * rows, rows), rows)

    def half_reqs(i):
        half = 1 - core if i == 0 else core
        return pl.ds(half * reqs, reqs)

    fetch(0, ids_in, i_buf)
    fetch(0, weights_in, r_buf)
    for i in range(2):
        here = pl.ds(i * rows, rows)
        fetch(0, queries.at[half_rows(i)], q_buf.at[here])
        fetch(0, cache_keys.at[half_reqs(i)], k_buf.at[pl.ds(i * reqs, reqs)])
        fetch(0, draft_kv.at[:, half_rows(i)], d_buf.at[:, here])
    for i in range(2):
        here = pl.ds(i * rows, rows)
        fetch(1, cache_values.at[half_reqs(i)], v_buf.at[pl.ds(i * reqs, reqs)])
        fetch(1, out_gate.at[half_rows(i)], g_buf.at[here])
    fetch(2, o_weight, w_buf)
    fetch(3, hidden_in, h_buf)
    fetch(3, gain_in, gain_ref)

    for copy in groups[0]:
        copy.wait()
    row = lax.broadcasted_iota(jnp.int32, table_ref.shape[::-1], 0)
    table = jnp.zeros(row.shape, F32)
    for k in range(i_buf.shape[0]):
        index = i_buf[k : k + 1, :]
        weight = r_buf[k : k + 1, :]
        high = weight.astype(BF16).astype(F32)
        table = jnp.where(row == index, high, table)
        table = jnp.where(row == index + experts, weight - high, table)
    table_ref[...] = table.T.astype(BF16)
    scale = 1.0 / math.sqrt(head_size)
    stacked = heads * drafts
    slot = lax.broadcasted_iota(jnp.int32, (stacked, context_len), 1)
    draft_slot = lax.broadcasted_iota(jnp.int32, (stacked, drafts), 1)
    draft_row = lax.broadcasted_iota(jnp.int32, (heads, drafts, drafts), 1).reshape(stacked, drafts)
    row_index = lax.broadcasted_iota(jnp.int32, (drafts, head_size), 0)
    lens = []
    for r in range(reqs_all):
        half = 1 - core if r < reqs else core
        place = half * reqs + r % reqs
        lens.append((cache_len_ref[place], draft_len_ref[place]))
    probs = []
    for r in range(reqs_all):
        span = slice(r * drafts, (r + 1) * drafts)
        query = jnp.concatenate(
            [q_buf[span, h * head_size : (h + 1) * head_size] for h in range(heads)], axis=0
        )
        cache_len, draft_len = lens[r]
        cache_scores = _dot_t(query, k_buf[r]) * scale
        draft_scores = _dot_t(query, d_buf[0, span]) * scale
        cache_scores = jnp.where(slot < cache_len, cache_scores, LOWEST)
        live = (draft_slot <= draft_row) & (draft_slot < draft_len)
        draft_scores = jnp.where(live, draft_scores, LOWEST)
        row_max = jnp.maximum(
            jnp.max(cache_scores, axis=-1, keepdims=True),
            jnp.max(draft_scores, axis=-1, keepdims=True),
        )
        cache_probs = jnp.exp(cache_scores - row_max)
        draft_probs = jnp.exp(draft_scores - row_max)
        denominator = jnp.sum(cache_probs, axis=-1, keepdims=True) + jnp.sum(
            draft_probs, axis=-1, keepdims=True
        )
        probs.append((cache_probs.astype(BF16), draft_probs.astype(BF16), denominator))
    for copy in groups[1]:
        copy.wait()
    for r in range(reqs_all):
        span = slice(r * drafts, (r + 1) * drafts)
        cache_probs, draft_probs, denominator = probs[r]
        context = _dot(cache_probs, v_buf[r]) + _dot(draft_probs, d_buf[1, span])
        context = context / denominator
        draft_len = lens[r][1]
        for h in range(heads):
            cols = slice(h * head_size, (h + 1) * head_size)
            gate = jax.nn.sigmoid(g_buf[span, cols].astype(F32))
            piece = context[h * drafts : (h + 1) * drafts] * gate
            piece = jnp.where(row_index < draft_len, piece, 0.0)
            attended[span, cols] = piece.astype(BF16)
    for copy in groups[2] + groups[3]:
        copy.wait()
    rows_in = attended[...]
    width = sent_ref.shape[1]
    tile = min(512, width)
    for c in range(0, width, tile):
        cols = slice(c, c + tile)
        projected = _dot(rows_in, w_buf[:, cols])
        sent_ref[:, cols] = projected[:rows].astype(BF16)
        kept_ref[:, cols] = h_buf[:, cols].astype(F32) + projected[rows:]


def attention(core, experts, hidden, gain, ids, weights, arrays):
    queries, out_gate, draft_kv, cache_keys, cache_values, draft_len, cache_len, o_weight = arrays
    reqs_all, context_len, head_size = cache_keys.shape
    rows_all = queries.shape[0]
    own_rows = hidden.shape[0]
    inner, width = o_weight.shape
    lanes = -(-2 * experts // 128) * 128
    smem = pl.BlockSpec(memory_space=pltpu.SMEM)
    vmem = pl.BlockSpec(memory_space=pltpu.VMEM)
    hbm = pl.BlockSpec(memory_space=pl.ANY)
    ids, weights = ids.T, weights.T

    return pl.pallas_call(
        functools.partial(attention_kernel, experts),
        out_shape=(
            jax.ShapeDtypeStruct((own_rows, width), BF16),
            jax.ShapeDtypeStruct((own_rows, width), F32),
            jax.ShapeDtypeStruct((own_rows, lanes), BF16),
            jax.ShapeDtypeStruct((1, width), F32),
        ),
        in_specs=[smem] * 3 + [hbm] * 10,
        out_specs=[vmem] * 4,
        scratch_shapes=[
            pltpu.VMEM((rows_all, inner), BF16),
            pltpu.VMEM((rows_all, inner), BF16),
            pltpu.VMEM((2, rows_all, head_size), BF16),
            pltpu.VMEM(cache_keys.shape, BF16),
            pltpu.VMEM(cache_values.shape, BF16),
            pltpu.VMEM((inner, width), BF16),
            pltpu.VMEM((own_rows, width), BF16),
            pltpu.VMEM(ids.shape, jnp.int32),
            pltpu.VMEM(weights.shape, F32),
            pltpu.VMEM((rows_all, inner), BF16),
            pltpu.SemaphoreType.DMA((15,)),
        ],
        compiler_params=pltpu.CompilerParams(vmem_limit_bytes=24 * 1024 * 1024),
        cost_estimate=pl.CostEstimate(
            flops=2 * rows_all * inner * (width + 2 * context_len),
            bytes_accessed=2 * inner * width + 4 * reqs_all * context_len * head_size,
            transcendentals=0,
        ),
    )(
        core.reshape(1),
        in_hbm(draft_len),
        in_hbm(cache_len),
        *map(
            in_hbm,
            (
                ids,
                weights,
                gain.reshape(1, width),
                hidden,
                queries,
                out_gate,
                draft_kv,
                cache_keys,
                cache_values,
                o_weight,
            ),
        ),
    )


def norm_kernel(kept_ref, received_ref, gain_ref, table_ref, residual_ref, sent_ref):
    residual = kept_ref[...] + received_ref[...].astype(F32)
    width = residual.shape[1]
    spread = jnp.mean(residual * residual, axis=-1, keepdims=True)
    normed = (residual * lax.rsqrt(spread + 1e-06) * gain_ref[...]).astype(BF16)
    residual_ref[...] = residual
    sent_ref[:, :width] = normed
    sent_ref[:, width:] = table_ref[...]


def residual_norm(kept, received, gain, table):
    rows, width = kept.shape
    return pl.pallas_call(
        norm_kernel,
        out_shape=(
            jax.ShapeDtypeStruct((rows, width), F32),
            jax.ShapeDtypeStruct((rows, width + table.shape[1]), BF16),
        ),
        compiler_params=pltpu.CompilerParams(vmem_limit_bytes=16 * 1024 * 1024),
    )(kept, received, gain, table)


def experts_kernel(spans, experts, where_ref, *refs):
    pieces = len(spans)
    rows_in = refs[:pieces]
    gates, ups, downs = (refs[pieces + 2 * i : pieces + 2 + 2 * i] for i in range(3))
    outs = refs[pieces + 6 : -2]
    rows, total = refs[-2:]
    width = total.shape[1]
    at = 0
    for ref, (start, size) in zip(rows_in, spans):
        rows[at : at + size] = ref[start : start + size]
        at += size
    table = rows[:, width:].astype(F32)
    column = lax.broadcasted_iota(jnp.int32, table.shape, 1)
    block = rows[:, :width]
    hidden = gates[0].shape[2]
    tile = min(256, hidden)
    for e in range(2):
        index = where_ref[e]
        chosen = (column == index) | (column == index + experts)
        weight = jnp.sum(jnp.where(chosen, table, 0.0), axis=1, keepdims=True)
        for c in range(0, hidden, tile):
            span = slice(c, c + tile)
            gate = _dot(block, gates[e][0, :, span])
            up = _dot(block, ups[e][0, :, span])
            act = (jax.nn.silu(gate) * up * weight).astype(BF16)
            added = _dot(act, downs[e][0, span, :])
            if e == 0 and c == 0:
                total[...] = added
            else:
                total[...] += added
    at = 0
    for out in outs:
        size = out.shape[0]
        out[...] = total[at : at + size].astype(BF16)
        at += size


def hold_kernel(count, where_ref, *refs):
    sources, out_ref, held, sems = refs[:count], refs[count], refs[count + 1 : -1], refs[-1]
    copies = [
        pltpu.make_async_copy(source, target, sems.at[i])
        for i, (source, target) in enumerate(zip(sources, held))
    ]
    for copy in copies:
        copy.start()
    for i in range(out_ref.shape[0]):
        out_ref[i] = where_ref[i]
    for copy in copies:
        copy.wait()


def hold_weights(where, weights):
    count = len(weights)
    vmem = pl.BlockSpec(memory_space=pltpu.VMEM)
    smem = pl.BlockSpec(memory_space=pltpu.SMEM)
    return pl.pallas_call(
        functools.partial(hold_kernel, count),
        out_shape=[jax.ShapeDtypeStruct(where.shape, where.dtype)]
        + [jax.ShapeDtypeStruct(w.shape, w.dtype) for w in weights],
        in_specs=[smem] + [pl.BlockSpec(memory_space=pl.ANY)] * count,
        out_specs=[smem] + [vmem] * count,
        scratch_shapes=[pltpu.SemaphoreType.DMA((max(1, count),))],
        compiler_params=pltpu.CompilerParams(vmem_limit_bytes=16 * 1024 * 1024),
        cost_estimate=pl.CostEstimate(flops=STEP_FLOPS, bytes_accessed=0, transcendentals=0),
    )(where, *weights)


def step_kernel(token_ref, out_ref):
    out_ref[...] = token_ref[...]


def step(token):
    return pl.pallas_call(
        step_kernel,
        out_shape=jax.ShapeDtypeStruct(token.shape, token.dtype),
        compiler_params=pltpu.CompilerParams(vmem_limit_bytes=16 * 1024 * 1024),
        cost_estimate=pl.CostEstimate(flops=STEP_FLOPS, bytes_accessed=0, transcendentals=0),
    )(token)


def plane_experts(where, rows_in, out_rows, experts, own_weights, other_weights):
    arrays = [piece[0] for piece in rows_in]
    spans = tuple(piece[1:] for piece in rows_in)
    count = sum(span[1] for span in spans)
    padded = arrays[0].shape[1]
    width, hidden = own_weights[0].shape[1:]
    weights = [w for pair in zip(own_weights, other_weights) for w in pair]
    vmem = pl.BlockSpec(memory_space=pltpu.VMEM)
    return pl.pallas_call(
        functools.partial(experts_kernel, spans, experts),
        out_shape=tuple(jax.ShapeDtypeStruct((size, width), BF16) for size in out_rows),
        in_specs=[pl.BlockSpec(memory_space=pltpu.SMEM)] + [vmem] * (len(spans) + 6),
        out_specs=[vmem] * len(out_rows),
        scratch_shapes=[pltpu.VMEM((count, padded), BF16), pltpu.VMEM((count, width), F32)],
        compiler_params=pltpu.CompilerParams(vmem_limit_bytes=24 * 1024 * 1024),
        cost_estimate=pl.CostEstimate(flops=STEP_FLOPS, bytes_accessed=0, transcendentals=0),
    )(where, *arrays, *weights)


def final_kernel(token_ref, residual_ref, *refs):
    out_ref = refs[-1]
    mix = refs[0][...].astype(F32)
    for ref in refs[1:-1]:
        mix = mix + ref[...].astype(F32)
    out_ref[...] = (residual_ref[...] + mix).astype(BF16)


def final_sum(token, residual, pieces):
    return pl.pallas_call(
        final_kernel,
        out_shape=jax.ShapeDtypeStruct(residual.shape, BF16),
        compiler_params=pltpu.CompilerParams(vmem_limit_bytes=16 * 1024 * 1024),
    )(token, residual, *pieces)


def add_bf16(*terms):
    total = terms[0].astype(F32)
    for term in terms[1:]:
        total = total + term.astype(F32)
    return total.astype(BF16)


def on_device(
    hidden_in,
    queries,
    out_gate,
    draft_kv,
    cache_keys,
    cache_values,
    draft_len,
    cache_len,
    o_weight,
    norm_gain,
    route_ids,
    route_weights,
    w_gate,
    w_up,
    w_down,
):
    wide = lax.axis_size("wide")
    narrow = lax.axis_size("narrow")
    chip = lax.axis_index("wide")
    core = lax.axis_index("narrow")
    plane = 4
    planes = wide // plane
    assert narrow == 2 and wide % plane == 0 and planes > 2
    experts = wide * narrow
    own_rows, width = hidden_in.shape
    mid = own_rows // 2

    swap = [(0, 1), (1, 0)]
    own_weights = (w_gate, w_up, w_down)
    other_weights = [lax.ppermute(w, "narrow", swap) for w in own_weights]

    arrays = (queries, out_gate, draft_kv, cache_keys, cache_values, draft_len, cache_len, o_weight)
    outgoing, kept, table, gain = attention(
        core, experts, hidden_in, norm_gain, route_ids, route_weights, arrays
    )
    received = lax.ppermute(outgoing, "narrow", swap)
    residual, sent = residual_norm(kept, received, gain, table)

    def across(flips):
        pairs = [
            (i * narrow + c, (i ^ flips[c]) * narrow + c) for i in range(wide) for c in range(narrow)
        ]
        return lambda a: lax.ppermute(a, ("wide", "narrow"), pairs)

    def shifted(by):
        pairs = [(i, (i + by * plane) % wide) for i in range(wide)]
        return lambda a: lax.ppermute(a, "wide", pairs)

    over_u, over_v = across((1, 2)), across((2, 1))
    own_expert = chip * narrow + core
    where = jnp.stack([own_expert, own_expert ^ 1]).astype(jnp.int32)

    b, u, v, made = {0: sent}, {}, {}, {}
    token = jnp.zeros((8, 128), F32)

    def wait(*entries, passed=()):
        nonlocal token
        arrays = [store[key] for store, key in entries]
        token, *rest = lax.optimization_barrier((token, *arrays, *passed))
        for (store, key), array in zip(entries, rest):
            store[key] = array
        return rest[len(entries) :]

    def run_experts(s):
        rows_in = [(b[s], 0, own_rows), (u[s], 0, own_rows), (v[s], 0, 2 * own_rows)]
        out_rows = [2 * own_rows] * 2 if s == 1 else [own_rows] * 4
        made[s] = list(plane_experts(index, rows_in, out_rows, experts, own_held, other_held))

    def made_entries(s):
        return [(made[s], i) for i in range(len(made[s]))]

    b[1] = shifted(1)(b[0])
    u[0] = over_u(b[0])
    index, *held = hold_weights(where, [in_hbm(w) for w in own_weights] + other_weights)
    index, *held = wait((b, 1), (u, 0), passed=[index, *held])
    own_held, other_held = held[:3], held[3:]
    for k in range(1, planes):
        if k + 1 < planes:
            b[k + 1] = shifted(1)(b[k])
        u[k] = over_u(b[k])
        v[k - 1] = over_v(jnp.concatenate([b[k - 1], u[k - 1]]))
        token = step(token)
        entries = [(u, k)]
        if k + 1 < planes:
            entries.append((b, k + 1))
        if k > 1:
            run_experts(k - 2)
            entries += made_entries(k - 2)
        wait(*entries)
    v[planes - 1] = over_v(jnp.concatenate([b[planes - 1], u[planes - 1]]))
    whole = {}
    if 1 in made:
        whole[0] = shifted(planes - 1)(made[1][0])
    token = step(token)
    run_experts(planes - 2)
    wait(*made_entries(planes - 2), (made[1], 1))
    if 0 not in whole:
        whole[0] = shifted(planes - 1)(made[1][0])
    whole[1] = shifted(planes - 1)(made[1][1])

    half = max(2, (planes + 1) // 2)
    order = list(range(half, planes - 1)) + list(range(2, half)) + [planes - 1, 0]
    back_d, back_v, back_u, back_z, sums = {}, {}, {}, {}, {}
    for s in order[:2]:
        if s in made and s:
            back_d[s] = over_v(made[s][3])
    token = step(token)
    wait((v, planes - 1))
    run_experts(planes - 1)
    wait(*made_entries(planes - 1))
    for s in order[:2]:
        if s not in back_d and s:
            back_d[s] = over_v(made[s][3])
    token = step(token)
    wait((back_d, order[0]), (whole, 0))
    for j, s in enumerate(order[:-1]):
        own, for_u, for_v, _ = made[s]
        follows = order[j + 1]
        if j:
            last = order[j - 1]
            onward = 2 * last >= planes
            back_z[last] = shifted(1 if onward else planes - last)(sums[last])
        back_u[s] = over_u(add_bf16(for_u, back_d[s]))
        back_v[s] = over_v(for_v)
        if follows and order[j + 2]:
            back_d[order[j + 2]] = over_v(made[order[j + 2]][3])
        token = step(token)
        carried = s - 1 in back_z and 2 * (s - 1) >= planes
        wait(
            (back_u, s),
            (back_v, s),
            *([(back_z, s - 1)] if carried else []),
            *([] if j else [(whole, 1)]),
            *([(back_d, follows)] if follows else []),
        )
        if j == 0:
            own_0, for_u_0, for_v_0, for_d_0 = made[0]
            own_0 = add_bf16(own_0, whole[0][:own_rows])
            for_u_0 = add_bf16(for_u_0, whole[0][own_rows:])
            back_d[0] = over_v(add_bf16(for_d_0, whole[1][own_rows:]))
            back_v[0] = over_v(add_bf16(for_v_0, whole[1][:own_rows]))
        terms = [own, back_v[s], back_u[s]]
        if carried:
            terms.append(back_z.pop(s - 1))
        sums[s] = add_bf16(*terms)
        token = step(token)
    last = planes - 1
    back_z[last] = shifted(1)(sums[last])
    token = step(token)
    wait((back_d, 0))
    back_u[0] = over_u(add_bf16(for_u_0, back_d[0]))
    results = [own_0, back_v[0], back_u[0]]
    results += [back_z[s] for s in sorted(back_z)]
    return final_sum(token, residual, results)


def solution(mesh):
    placed = (
        P(("rep", "wide", "narrow"), None),
        P(("rep", "wide"), "narrow"),
        P(("rep", "wide"), "narrow"),
        P(None, ("rep", "wide"), None),
        P(("rep", "wide"), None, None),
        P(("rep", "wide"), None, None),
        P(("rep", "wide")),
        P(("rep", "wide")),
        P("narrow", None),
        P(),
        P(("rep", "wide", "narrow"), None),
        P(("rep", "wide", "narrow"), None),
        P(("wide", "narrow"), None, None),
        P(("wide", "narrow"), None, None),
        P(("wide", "narrow"), None, None),
    )
    return jax.shard_map(
        on_device,
        mesh=mesh,
        in_specs=placed,
        out_specs=P(("rep", "wide", "narrow"), None),
        check_vma=False,
    )
```

```python
import functools
import math

import jax
import jax.numpy as jnp
from jax import lax
from jax.experimental import pallas as pl
from jax.experimental.pallas import tpu as pltpu
from jax.sharding import PartitionSpec as P

BF16 = jnp.bfloat16
F32 = jnp.float32
LOWEST = -1e30
STEP_FLOPS = 200_000_000


def in_hbm(a):
    return pltpu.with_memory_space_constraint(a, pltpu.HBM)


def _dot(a, b):
    return jnp.dot(a, b, preferred_element_type=F32)


def _dot_t(a, b):
    return lax.dot_general(a, b, (((1,), (1,)), ((), ())), preferred_element_type=F32)


def attention_kernel(
    experts,
    core_ref,
    draft_len_ref,
    cache_len_ref,
    ids_in,
    weights_in,
    gain_in,
    hidden_in,
    queries,
    out_gate,
    draft_kv,
    cache_keys,
    cache_values,
    o_weight,
    sent_ref,
    kept_ref,
    table_ref,
    gain_ref,
    q_buf,
    g_buf,
    d_buf,
    k_buf,
    v_buf,
    w_buf,
    h_buf,
    i_buf,
    r_buf,
    attended,
    sems,
):
    core = core_ref[0]
    reqs_all, context_len, head_size = k_buf.shape
    rows_all = q_buf.shape[0]
    rows, reqs = rows_all // 2, reqs_all // 2
    drafts = rows // reqs
    heads = q_buf.shape[1] // head_size
    groups = [[], [], [], []]

    def fetch(group, source, target):
        at = sum(len(g) for g in groups)
        copy = pltpu.make_async_copy(source, target, sems.at[at])
        copy.start()
        groups[group].append(copy)

    def half_rows(i):
        half = 1 - core if i == 0 else core
        return pl.ds(pl.multiple_of(half * rows, rows), rows)

    def half_reqs(i):
        half = 1 - core if i == 0 else core
        return pl.ds(half * reqs, reqs)

    fetch(0, ids_in, i_buf)
    fetch(0, weights_in, r_buf)
    for i in range(2):
        here = pl.ds(i * rows, rows)
        fetch(0, queries.at[half_rows(i)], q_buf.at[here])
        fetch(0, cache_keys.at[half_reqs(i)], k_buf.at[pl.ds(i * reqs, reqs)])
        fetch(0, draft_kv.at[:, half_rows(i)], d_buf.at[:, here])
    for i in range(2):
        here = pl.ds(i * rows, rows)
        fetch(1, cache_values.at[half_reqs(i)], v_buf.at[pl.ds(i * reqs, reqs)])
        fetch(1, out_gate.at[half_rows(i)], g_buf.at[here])
    fetch(2, o_weight, w_buf)
    fetch(3, hidden_in, h_buf)
    fetch(3, gain_in, gain_ref)

    for copy in groups[0]:
        copy.wait()
    row = lax.broadcasted_iota(jnp.int32, table_ref.shape[::-1], 0)
    table = jnp.zeros(row.shape, F32)
    for k in range(i_buf.shape[0]):
        index = i_buf[k : k + 1, :]
        weight = r_buf[k : k + 1, :]
        high = weight.astype(BF16).astype(F32)
        table = jnp.where(row == index, high, table)
        table = jnp.where(row == index + experts, weight - high, table)
    table_ref[...] = table.T.astype(BF16)
    scale = 1.0 / math.sqrt(head_size)
    stacked = heads * drafts
    slot = lax.broadcasted_iota(jnp.int32, (stacked, context_len), 1)
    draft_slot = lax.broadcasted_iota(jnp.int32, (stacked, drafts), 1)
    draft_row = lax.broadcasted_iota(jnp.int32, (heads, drafts, drafts), 1).reshape(stacked, drafts)
    row_index = lax.broadcasted_iota(jnp.int32, (drafts, head_size), 0)
    lens = []
    for r in range(reqs_all):
        half = 1 - core if r < reqs else core
        place = half * reqs + r % reqs
        lens.append((cache_len_ref[place], draft_len_ref[place]))
    probs = []
    for r in range(reqs_all):
        span = slice(r * drafts, (r + 1) * drafts)
        query = jnp.concatenate(
            [q_buf[span, h * head_size : (h + 1) * head_size] for h in range(heads)], axis=0
        )
        cache_len, draft_len = lens[r]
        cache_scores = _dot_t(query, k_buf[r]) * scale
        draft_scores = _dot_t(query, d_buf[0, span]) * scale
        cache_scores = jnp.where(slot < cache_len, cache_scores, LOWEST)
        live = (draft_slot <= draft_row) & (draft_slot < draft_len)
        draft_scores = jnp.where(live, draft_scores, LOWEST)
        row_max = jnp.maximum(
            jnp.max(cache_scores, axis=-1, keepdims=True),
            jnp.max(draft_scores, axis=-1, keepdims=True),
        )
        cache_probs = jnp.exp(cache_scores - row_max)
        draft_probs = jnp.exp(draft_scores - row_max)
        denominator = jnp.sum(cache_probs, axis=-1, keepdims=True) + jnp.sum(
            draft_probs, axis=-1, keepdims=True
        )
        probs.append((cache_probs.astype(BF16), draft_probs.astype(BF16), denominator))
    for copy in groups[1]:
        copy.wait()
    for r in range(reqs_all):
        span = slice(r * drafts, (r + 1) * drafts)
        cache_probs, draft_probs, denominator = probs[r]
        context = _dot(cache_probs, v_buf[r]) + _dot(draft_probs, d_buf[1, span])
        context = context / denominator
        draft_len = lens[r][1]
        for h in range(heads):
            cols = slice(h * head_size, (h + 1) * head_size)
            gate = jax.nn.sigmoid(g_buf[span, cols].astype(F32))
            piece = context[h * drafts : (h + 1) * drafts] * gate
            piece = jnp.where(row_index < draft_len, piece, 0.0)
            attended[span, cols] = piece.astype(BF16)
    for copy in groups[2] + groups[3]:
        copy.wait()
    rows_in = attended[...]
    width = sent_ref.shape[1]
    tile = min(512, width)
    for c in range(0, width, tile):
        cols = slice(c, c + tile)
        projected = _dot(rows_in, w_buf[:, cols])
        sent_ref[:, cols] = projected[:rows].astype(BF16)
        kept_ref[:, cols] = h_buf[:, cols].astype(F32) + projected[rows:]


def attention(core, experts, hidden, gain, ids, weights, arrays):
    queries, out_gate, draft_kv, cache_keys, cache_values, draft_len, cache_len, o_weight = arrays
    reqs_all, context_len, head_size = cache_keys.shape
    rows_all = queries.shape[0]
    own_rows = hidden.shape[0]
    inner, width = o_weight.shape
    lanes = -(-2 * experts // 128) * 128
    smem = pl.BlockSpec(memory_space=pltpu.SMEM)
    vmem = pl.BlockSpec(memory_space=pltpu.VMEM)
    hbm = pl.BlockSpec(memory_space=pl.ANY)
    ids, weights = ids.T, weights.T

    return pl.pallas_call(
        functools.partial(attention_kernel, experts),
        out_shape=(
            jax.ShapeDtypeStruct((own_rows, width), BF16),
            jax.ShapeDtypeStruct((own_rows, width), F32),
            jax.ShapeDtypeStruct((own_rows, lanes), BF16),
            jax.ShapeDtypeStruct((1, width), F32),
        ),
        in_specs=[smem] * 3 + [hbm] * 10,
        out_specs=[vmem] * 4,
        scratch_shapes=[
            pltpu.VMEM((rows_all, inner), BF16),
            pltpu.VMEM((rows_all, inner), BF16),
            pltpu.VMEM((2, rows_all, head_size), BF16),
            pltpu.VMEM(cache_keys.shape, BF16),
            pltpu.VMEM(cache_values.shape, BF16),
            pltpu.VMEM((inner, width), BF16),
            pltpu.VMEM((own_rows, width), BF16),
            pltpu.VMEM(ids.shape, jnp.int32),
            pltpu.VMEM(weights.shape, F32),
            pltpu.VMEM((rows_all, inner), BF16),
            pltpu.SemaphoreType.DMA((15,)),
        ],
        compiler_params=pltpu.CompilerParams(vmem_limit_bytes=24 * 1024 * 1024),
        cost_estimate=pl.CostEstimate(
            flops=2 * rows_all * inner * (width + 2 * context_len),
            bytes_accessed=2 * inner * width + 4 * reqs_all * context_len * head_size,
            transcendentals=0,
        ),
    )(
        core.reshape(1),
        in_hbm(draft_len),
        in_hbm(cache_len),
        *map(
            in_hbm,
            (
                ids,
                weights,
                gain.reshape(1, width),
                hidden,
                queries,
                out_gate,
                draft_kv,
                cache_keys,
                cache_values,
                o_weight,
            ),
        ),
    )


def norm_kernel(kept_ref, received_ref, gain_ref, table_ref, residual_ref, sent_ref):
    residual = kept_ref[...] + received_ref[...].astype(F32)
    width = residual.shape[1]
    spread = jnp.mean(residual * residual, axis=-1, keepdims=True)
    normed = (residual * lax.rsqrt(spread + 1e-06) * gain_ref[...]).astype(BF16)
    residual_ref[...] = residual
    sent_ref[:, :width] = normed
    sent_ref[:, width:] = table_ref[...]


def residual_norm(kept, received, gain, table):
    rows, width = kept.shape
    return pl.pallas_call(
        norm_kernel,
        out_shape=(
            jax.ShapeDtypeStruct((rows, width), F32),
            jax.ShapeDtypeStruct((rows, width + table.shape[1]), BF16),
        ),
        compiler_params=pltpu.CompilerParams(vmem_limit_bytes=16 * 1024 * 1024),
    )(kept, received, gain, table)


def experts_kernel(spans, experts, where_ref, *refs):
    pieces = len(spans)
    rows_in = refs[:pieces]
    gates, ups, downs = (refs[pieces + 2 * i : pieces + 2 + 2 * i] for i in range(3))
    outs, rows = refs[pieces + 6 : -1], refs[-1]
    width = outs[0].shape[1]
    at = 0
    for ref, (start, size) in zip(rows_in, spans):
        rows[at : at + size] = ref[start : start + size]
        at += size
    table = rows[:, width:].astype(F32)
    column = lax.broadcasted_iota(jnp.int32, table.shape, 1)
    block = rows[:, :width]
    acts = []
    for e in range(2):
        index = where_ref[e]
        chosen = (column == index) | (column == index + experts)
        weight = jnp.sum(jnp.where(chosen, table, 0.0), axis=1, keepdims=True)
        gate = _dot(block, gates[e][0])
        up = _dot(block, ups[e][0])
        acts.append((jax.nn.silu(gate) * up * weight).astype(BF16))
    tile = min(512, width)
    for c in range(0, width, tile):
        cols = slice(c, c + tile)
        made = _dot(acts[0], downs[0][0, :, cols]) + _dot(acts[1], downs[1][0, :, cols])
        at = 0
        for out in outs:
            size = out.shape[0]
            out[:, cols] = made[at : at + size].astype(BF16)
            at += size


def hold_kernel(count, where_ref, *refs):
    sources, out_ref, held, sems = refs[:count], refs[count], refs[count + 1 : -1], refs[-1]
    copies = [
        pltpu.make_async_copy(source, target, sems.at[i])
        for i, (source, target) in enumerate(zip(sources, held))
    ]
    for copy in copies:
        copy.start()
    for i in range(out_ref.shape[0]):
        out_ref[i] = where_ref[i]
    for copy in copies:
        copy.wait()


def hold_weights(where, weights):
    count = len(weights)
    vmem = pl.BlockSpec(memory_space=pltpu.VMEM)
    smem = pl.BlockSpec(memory_space=pltpu.SMEM)
    return pl.pallas_call(
        functools.partial(hold_kernel, count),
        out_shape=[jax.ShapeDtypeStruct(where.shape, where.dtype)]
        + [jax.ShapeDtypeStruct(w.shape, w.dtype) for w in weights],
        in_specs=[smem] + [pl.BlockSpec(memory_space=pl.ANY)] * count,
        out_specs=[smem] + [vmem] * count,
        scratch_shapes=[pltpu.SemaphoreType.DMA((max(1, count),))],
        compiler_params=pltpu.CompilerParams(vmem_limit_bytes=16 * 1024 * 1024),
        cost_estimate=pl.CostEstimate(flops=STEP_FLOPS, bytes_accessed=0, transcendentals=0),
    )(where, *weights)


def step_kernel(token_ref, out_ref):
    out_ref[...] = token_ref[...]


def step(token):
    return pl.pallas_call(
        step_kernel,
        out_shape=jax.ShapeDtypeStruct(token.shape, token.dtype),
        compiler_params=pltpu.CompilerParams(vmem_limit_bytes=16 * 1024 * 1024),
        cost_estimate=pl.CostEstimate(flops=STEP_FLOPS, bytes_accessed=0, transcendentals=0),
    )(token)


def plane_experts(where, rows_in, out_rows, experts, own_weights, other_weights):
    arrays = [piece[0] for piece in rows_in]
    spans = tuple(piece[1:] for piece in rows_in)
    count = sum(span[1] for span in spans)
    padded = arrays[0].shape[1]
    width, hidden = own_weights[0].shape[1:]
    weights = [w for pair in zip(own_weights, other_weights) for w in pair]
    vmem = pl.BlockSpec(memory_space=pltpu.VMEM)
    return pl.pallas_call(
        functools.partial(experts_kernel, spans, experts),
        out_shape=tuple(jax.ShapeDtypeStruct((size, width), BF16) for size in out_rows),
        in_specs=[pl.BlockSpec(memory_space=pltpu.SMEM)] + [vmem] * (len(spans) + 6),
        out_specs=[vmem] * len(out_rows),
        scratch_shapes=[pltpu.VMEM((count, padded), BF16)],
        compiler_params=pltpu.CompilerParams(vmem_limit_bytes=24 * 1024 * 1024),
        cost_estimate=pl.CostEstimate(flops=STEP_FLOPS, bytes_accessed=0, transcendentals=0),
    )(where, *arrays, *weights)


def final_kernel(token_ref, residual_ref, *refs):
    out_ref = refs[-1]
    mix = refs[0][...].astype(F32)
    for ref in refs[1:-1]:
        mix = mix + ref[...].astype(F32)
    out_ref[...] = (residual_ref[...] + mix).astype(BF16)


def final_sum(token, residual, pieces):
    return pl.pallas_call(
        final_kernel,
        out_shape=jax.ShapeDtypeStruct(residual.shape, BF16),
        compiler_params=pltpu.CompilerParams(vmem_limit_bytes=16 * 1024 * 1024),
    )(token, residual, *pieces)


def add_bf16(*terms):
    total = terms[0].astype(F32)
    for term in terms[1:]:
        total = total + term.astype(F32)
    return total.astype(BF16)


def on_device(
    hidden_in,
    queries,
    out_gate,
    draft_kv,
    cache_keys,
    cache_values,
    draft_len,
    cache_len,
    o_weight,
    norm_gain,
    route_ids,
    route_weights,
    w_gate,
    w_up,
    w_down,
):
    wide = lax.axis_size("wide")
    narrow = lax.axis_size("narrow")
    chip = lax.axis_index("wide")
    core = lax.axis_index("narrow")
    plane = 4
    planes = wide // plane
    assert narrow == 2 and wide % plane == 0 and planes > 2
    experts = wide * narrow
    own_rows, width = hidden_in.shape
    mid = own_rows // 2

    swap = [(0, 1), (1, 0)]
    own_weights = (w_gate, w_up, w_down)
    other_weights = [lax.ppermute(w, "narrow", swap) for w in own_weights]

    arrays = (queries, out_gate, draft_kv, cache_keys, cache_values, draft_len, cache_len, o_weight)
    outgoing, kept, table, gain = attention(
        core, experts, hidden_in, norm_gain, route_ids, route_weights, arrays
    )
    received = lax.ppermute(outgoing, "narrow", swap)
    residual, sent = residual_norm(kept, received, gain, table)

    def across(flips):
        pairs = [
            (i * narrow + c, (i ^ flips[c]) * narrow + c) for i in range(wide) for c in range(narrow)
        ]
        return lambda a: lax.ppermute(a, ("wide", "narrow"), pairs)

    def shifted(by):
        pairs = [(i, (i + by * plane) % wide) for i in range(wide)]
        return lambda a: lax.ppermute(a, "wide", pairs)

    over_u, over_v = across((1, 2)), across((2, 1))
    own_expert = chip * narrow + core
    where = jnp.stack([own_expert, own_expert ^ 1]).astype(jnp.int32)

    b, u, v, made = {0: sent}, {}, {}, {}
    token = jnp.zeros((8, 128), F32)

    def wait(*entries, passed=()):
        nonlocal token
        arrays = [store[key] for store, key in entries]
        token, *rest = lax.optimization_barrier((token, *arrays, *passed))
        for (store, key), array in zip(entries, rest):
            store[key] = array
        return rest[len(entries) :]

    def run_experts(s):
        rows_in = [(b[s], 0, own_rows), (u[s], 0, own_rows), (v[s], 0, 2 * own_rows)]
        out_rows = [2 * own_rows] * 2 if s == 1 else [own_rows] * 4
        made[s] = list(plane_experts(index, rows_in, out_rows, experts, own_held, other_held))

    def made_entries(s):
        return [(made[s], i) for i in range(len(made[s]))]

    b[1] = shifted(1)(b[0])
    u[0] = over_u(b[0])
    index, *held = hold_weights(where, [in_hbm(w) for w in own_weights] + other_weights)
    index, *held = wait((b, 1), (u, 0), passed=[index, *held])
    own_held, other_held = held[:3], held[3:]
    for k in range(1, planes):
        if k + 1 < planes:
            b[k + 1] = shifted(1)(b[k])
        u[k] = over_u(b[k])
        v[k - 1] = over_v(jnp.concatenate([b[k - 1], u[k - 1]]))
        token = step(token)
        entries = [(u, k)]
        if k + 1 < planes:
            entries.append((b, k + 1))
        if k > 1:
            run_experts(k - 2)
            entries += made_entries(k - 2)
        wait(*entries)
    v[planes - 1] = over_v(jnp.concatenate([b[planes - 1], u[planes - 1]]))
    whole = {}
    if 1 in made:
        whole[0] = shifted(planes - 1)(made[1][0])
    token = step(token)
    run_experts(planes - 2)
    wait(*made_entries(planes - 2), (made[1], 1))
    if 0 not in whole:
        whole[0] = shifted(planes - 1)(made[1][0])
    whole[1] = shifted(planes - 1)(made[1][1])

    half = max(2, (planes + 1) // 2)
    order = list(range(half, planes - 1)) + list(range(2, half)) + [planes - 1, 0]
    back_d, back_v, back_u, back_z, sums = {}, {}, {}, {}, {}
    for s in order[:2]:
        if s in made and s:
            back_d[s] = over_v(made[s][3])
    token = step(token)
    wait((v, planes - 1))
    run_experts(planes - 1)
    wait(*made_entries(planes - 1))
    for s in order[:2]:
        if s not in back_d and s:
            back_d[s] = over_v(made[s][3])
    token = step(token)
    wait((back_d, order[0]), (whole, 0))
    for j, s in enumerate(order[:-1]):
        own, for_u, for_v, _ = made[s]
        follows = order[j + 1]
        if j:
            last = order[j - 1]
            onward = 2 * last >= planes
            back_z[last] = shifted(1 if onward else planes - last)(sums[last])
        back_u[s] = over_u(add_bf16(for_u, back_d[s]))
        back_v[s] = over_v(for_v)
        if follows and order[j + 2]:
            back_d[order[j + 2]] = over_v(made[order[j + 2]][3])
        token = step(token)
        carried = s - 1 in back_z and 2 * (s - 1) >= planes
        wait(
            (back_u, s),
            (back_v, s),
            *([(back_z, s - 1)] if carried else []),
            *([] if j else [(whole, 1)]),
            *([(back_d, follows)] if follows else []),
        )
        if j == 0:
            own_0, for_u_0, for_v_0, for_d_0 = made[0]
            own_0 = add_bf16(own_0, whole[0][:own_rows])
            for_u_0 = add_bf16(for_u_0, whole[0][own_rows:])
            back_d[0] = over_v(add_bf16(for_d_0, whole[1][own_rows:]))
            back_v[0] = over_v(add_bf16(for_v_0, whole[1][:own_rows]))
        terms = [own, back_v[s], back_u[s]]
        if carried:
            terms.append(back_z.pop(s - 1))
        sums[s] = add_bf16(*terms)
        token = step(token)
    last = planes - 1
    back_z[last] = shifted(1)(sums[last])
    token = step(token)
    wait((back_d, 0))
    back_u[0] = over_u(add_bf16(for_u_0, back_d[0]))
    results = [own_0, back_v[0], back_u[0]]
    results += [back_z[s] for s in sorted(back_z)]
    return final_sum(token, residual, results)


def solution(mesh):
    placed = (
        P(("rep", "wide", "narrow"), None),
        P(("rep", "wide"), "narrow"),
        P(("rep", "wide"), "narrow"),
        P(None, ("rep", "wide"), None),
        P(("rep", "wide"), None, None),
        P(("rep", "wide"), None, None),
        P(("rep", "wide")),
        P(("rep", "wide")),
        P("narrow", None),
        P(),
        P(("rep", "wide", "narrow"), None),
        P(("rep", "wide", "narrow"), None),
        P(("wide", "narrow"), None, None),
        P(("wide", "narrow"), None, None),
        P(("wide", "narrow"), None, None),
    )
    return jax.shard_map(
        on_device,
        mesh=mesh,
        in_specs=placed,
        out_specs=P(("rep", "wide", "narrow"), None),
        check_vma=False,
    )
```

```python
import functools
import math

import jax
import jax.numpy as jnp
from jax import lax
from jax.experimental import pallas as pl
from jax.experimental.pallas import tpu as pltpu
from jax.sharding import PartitionSpec as P

BF16 = jnp.bfloat16
F32 = jnp.float32
LOWEST = -math.inf
STEP_FLOPS = 200_000_000


def in_hbm(a):
    return pltpu.with_memory_space_constraint(a, pltpu.HBM)


def _dot(a, b):
    return jnp.dot(a, b, preferred_element_type=F32)


def _dot_t(a, b):
    return lax.dot_general(a, b, (((1,), (1,)), ((), ())), preferred_element_type=F32)


def attention_kernel(
    experts,
    core_ref,
    draft_len_ref,
    cache_len_ref,
    ids_in,
    weights_in,
    gain_in,
    hidden_in,
    queries,
    out_gate,
    draft_kv,
    cache_keys,
    cache_values,
    o_weight,
    sent_ref,
    kept_ref,
    table_ref,
    gain_ref,
    q_buf,
    g_buf,
    d_buf,
    k_buf,
    v_buf,
    w_buf,
    h_buf,
    i_buf,
    r_buf,
    attended,
    sems,
):
    core = core_ref[0]
    reqs_all, context_len, head_size = k_buf.shape
    rows_all = q_buf.shape[0]
    rows, reqs = rows_all // 2, reqs_all // 2
    drafts = rows // reqs
    heads = q_buf.shape[1] // head_size
    groups = [[], [], [], []]

    def fetch(group, source, target):
        at = sum(len(g) for g in groups)
        copy = pltpu.make_async_copy(source, target, sems.at[at])
        copy.start()
        groups[group].append(copy)

    def half_rows(i):
        half = 1 - core if i == 0 else core
        return pl.ds(pl.multiple_of(half * rows, rows), rows)

    def half_reqs(i):
        half = 1 - core if i == 0 else core
        return pl.ds(half * reqs, reqs)

    fetch(0, ids_in, i_buf)
    fetch(0, weights_in, r_buf)
    for i in range(2):
        here = pl.ds(i * rows, rows)
        fetch(0, queries.at[half_rows(i)], q_buf.at[here])
        fetch(0, cache_keys.at[half_reqs(i)], k_buf.at[pl.ds(i * reqs, reqs)])
        fetch(0, draft_kv.at[:, half_rows(i)], d_buf.at[:, here])
    for i in range(2):
        here = pl.ds(i * rows, rows)
        fetch(1, cache_values.at[half_reqs(i)], v_buf.at[pl.ds(i * reqs, reqs)])
        fetch(1, out_gate.at[half_rows(i)], g_buf.at[here])
    fetch(2, o_weight, w_buf)
    fetch(3, hidden_in, h_buf)
    fetch(3, gain_in, gain_ref)

    for copy in groups[0]:
        copy.wait()
    scale = 1.0 / math.sqrt(head_size)
    stacked = heads * drafts
    slot = lax.broadcasted_iota(jnp.int32, (stacked, context_len), 1)
    draft_slot = lax.broadcasted_iota(jnp.int32, (stacked, drafts), 1)
    draft_row = lax.broadcasted_iota(jnp.int32, (heads, drafts, drafts), 1).reshape(stacked, drafts)
    row_index = lax.broadcasted_iota(jnp.int32, (drafts, head_size), 0)
    lens = []
    for r in range(reqs_all):
        half = 1 - core if r < reqs else core
        place = half * reqs + r % reqs
        lens.append((cache_len_ref[place], draft_len_ref[place]))
    probs = []
    for r in range(reqs_all):
        span = slice(r * drafts, (r + 1) * drafts)
        query = jnp.concatenate(
            [q_buf[span, h * head_size : (h + 1) * head_size] for h in range(heads)], axis=0
        )
        cache_len, draft_len = lens[r]
        cache_scores = _dot_t(query, k_buf[r]) * scale
        draft_scores = _dot_t(query, d_buf[0, span]) * scale
        cache_scores = jnp.where(slot < cache_len, cache_scores, LOWEST)
        live = (draft_slot <= draft_row) & (draft_slot < draft_len)
        draft_scores = jnp.where(live, draft_scores, LOWEST)
        row_max = jnp.maximum(
            jnp.max(cache_scores, axis=-1, keepdims=True),
            jnp.max(draft_scores, axis=-1, keepdims=True),
        )
        cache_probs = jnp.exp(cache_scores - row_max)
        draft_probs = jnp.exp(draft_scores - row_max)
        denominator = jnp.sum(cache_probs, axis=-1, keepdims=True) + jnp.sum(
            draft_probs, axis=-1, keepdims=True
        )
        probs.append((cache_probs.astype(BF16), draft_probs.astype(BF16), denominator))
    row = lax.broadcasted_iota(jnp.int32, table_ref.shape[::-1], 0)
    table = jnp.zeros(row.shape, F32)
    for k in range(i_buf.shape[0]):
        index = i_buf[k : k + 1, :]
        weight = r_buf[k : k + 1, :]
        high = weight.astype(BF16).astype(F32)
        table = jnp.where(row == index, high, table)
        table = jnp.where(row == index + experts, weight - high, table)
    table_ref[...] = table.T.astype(BF16)
    for copy in groups[1]:
        copy.wait()
    for r in range(reqs_all):
        span = slice(r * drafts, (r + 1) * drafts)
        cache_probs, draft_probs, denominator = probs[r]
        context = _dot(cache_probs, v_buf[r]) + _dot(draft_probs, d_buf[1, span])
        context = context / denominator
        draft_len = lens[r][1]
        for h in range(heads):
            cols = slice(h * head_size, (h + 1) * head_size)
            gate = jax.nn.sigmoid(g_buf[span, cols].astype(F32))
            piece = context[h * drafts : (h + 1) * drafts] * gate
            piece = jnp.where(row_index < draft_len, piece, 0.0)
            attended[span, cols] = piece.astype(BF16)
    for copy in groups[2] + groups[3]:
        copy.wait()
    rows_in = attended[...]
    width = sent_ref.shape[1]
    tile = min(512, width)
    for c in range(0, width, tile):
        cols = slice(c, c + tile)
        projected = _dot(rows_in, w_buf[:, cols])
        sent_ref[:, cols] = projected[:rows].astype(BF16)
        kept_ref[:, cols] = h_buf[:, cols].astype(F32) + projected[rows:]


def attention(core, experts, hidden, gain, ids, weights, arrays):
    queries, out_gate, draft_kv, cache_keys, cache_values, draft_len, cache_len, o_weight = arrays
    reqs_all, context_len, head_size = cache_keys.shape
    rows_all = queries.shape[0]
    own_rows = hidden.shape[0]
    inner, width = o_weight.shape
    lanes = -(-2 * experts // 128) * 128
    smem = pl.BlockSpec(memory_space=pltpu.SMEM)
    vmem = pl.BlockSpec(memory_space=pltpu.VMEM)
    hbm = pl.BlockSpec(memory_space=pl.ANY)
    ids, weights = ids.T, weights.T

    return pl.pallas_call(
        functools.partial(attention_kernel, experts),
        out_shape=(
            jax.ShapeDtypeStruct((own_rows, width), BF16),
            jax.ShapeDtypeStruct((own_rows, width), F32),
            jax.ShapeDtypeStruct((own_rows, lanes), BF16),
            jax.ShapeDtypeStruct((1, width), F32),
        ),
        in_specs=[smem] * 3 + [hbm] * 10,
        out_specs=[vmem] * 4,
        scratch_shapes=[
            pltpu.VMEM((rows_all, inner), BF16),
            pltpu.VMEM((rows_all, inner), BF16),
            pltpu.VMEM((2, rows_all, head_size), BF16),
            pltpu.VMEM(cache_keys.shape, BF16),
            pltpu.VMEM(cache_values.shape, BF16),
            pltpu.VMEM((inner, width), BF16),
            pltpu.VMEM((own_rows, width), BF16),
            pltpu.VMEM(ids.shape, jnp.int32),
            pltpu.VMEM(weights.shape, F32),
            pltpu.VMEM((rows_all, inner), BF16),
            pltpu.SemaphoreType.DMA((15,)),
        ],
        compiler_params=pltpu.CompilerParams(vmem_limit_bytes=24 * 1024 * 1024),
        cost_estimate=pl.CostEstimate(
            flops=2 * rows_all * inner * (width + 2 * context_len),
            bytes_accessed=2 * inner * width + 4 * reqs_all * context_len * head_size,
            transcendentals=0,
        ),
    )(
        core.reshape(1),
        in_hbm(draft_len),
        in_hbm(cache_len),
        *map(
            in_hbm,
            (
                ids,
                weights,
                gain.reshape(1, width),
                hidden,
                queries,
                out_gate,
                draft_kv,
                cache_keys,
                cache_values,
                o_weight,
            ),
        ),
    )


def norm_kernel(kept_ref, received_ref, gain_ref, table_ref, residual_ref, sent_ref):
    residual = kept_ref[...] + received_ref[...].astype(F32)
    width = residual.shape[1]
    spread = jnp.mean(residual * residual, axis=-1, keepdims=True)
    normed = (residual * lax.rsqrt(spread + 1e-06) * gain_ref[...]).astype(BF16)
    residual_ref[...] = residual
    sent_ref[:, :width] = normed
    sent_ref[:, width:] = table_ref[...]


def residual_norm(kept, received, gain, table):
    rows, width = kept.shape
    return pl.pallas_call(
        norm_kernel,
        out_shape=(
            jax.ShapeDtypeStruct((rows, width), F32),
            jax.ShapeDtypeStruct((rows, width + table.shape[1]), BF16),
        ),
        compiler_params=pltpu.CompilerParams(vmem_limit_bytes=16 * 1024 * 1024),
    )(kept, received, gain, table)


def experts_kernel(spans, experts, where_ref, *refs):
    pieces = len(spans)
    rows_in = refs[:pieces]
    gates, ups, downs = (refs[pieces + 2 * i : pieces + 2 + 2 * i] for i in range(3))
    outs, rows = refs[pieces + 6 : -1], refs[-1]
    width = outs[0].shape[1]
    at = 0
    for ref, (start, size) in zip(rows_in, spans):
        rows[at : at + size] = ref[start : start + size]
        at += size
    table = rows[:, width:].astype(F32)
    column = lax.broadcasted_iota(jnp.int32, table.shape, 1)
    block = rows[:, :width]
    acts = []
    for e in range(2):
        index = where_ref[e]
        chosen = (column == index) | (column == index + experts)
        weight = jnp.sum(jnp.where(chosen, table, 0.0), axis=1, keepdims=True)
        gate = _dot(block, gates[e][0])
        up = _dot(block, ups[e][0])
        acts.append((jax.nn.silu(gate) * up * weight).astype(BF16))
    tile = min(512, width)
    for c in range(0, width, tile):
        cols = slice(c, c + tile)
        made = _dot(acts[0], downs[0][0, :, cols]) + _dot(acts[1], downs[1][0, :, cols])
        at = 0
        for out in outs:
            size = out.shape[0]
            out[:, cols] = made[at : at + size].astype(BF16)
            at += size


def hold_kernel(count, where_ref, *refs):
    sources, out_ref, held, sems = refs[:count], refs[count], refs[count + 1 : -1], refs[-1]
    copies = [
        pltpu.make_async_copy(source, target, sems.at[i])
        for i, (source, target) in enumerate(zip(sources, held))
    ]
    for copy in copies:
        copy.start()
    for i in range(out_ref.shape[0]):
        out_ref[i] = where_ref[i]
    for copy in copies:
        copy.wait()


def hold_weights(where, weights):
    count = len(weights)
    vmem = pl.BlockSpec(memory_space=pltpu.VMEM)
    smem = pl.BlockSpec(memory_space=pltpu.SMEM)
    return pl.pallas_call(
        functools.partial(hold_kernel, count),
        out_shape=[jax.ShapeDtypeStruct(where.shape, where.dtype)]
        + [jax.ShapeDtypeStruct(w.shape, w.dtype) for w in weights],
        in_specs=[smem] + [pl.BlockSpec(memory_space=pl.ANY)] * count,
        out_specs=[smem] + [vmem] * count,
        scratch_shapes=[pltpu.SemaphoreType.DMA((max(1, count),))],
        compiler_params=pltpu.CompilerParams(vmem_limit_bytes=16 * 1024 * 1024),
        cost_estimate=pl.CostEstimate(flops=STEP_FLOPS, bytes_accessed=0, transcendentals=0),
    )(where, *weights)


def step_kernel(token_ref, out_ref):
    out_ref[...] = token_ref[...]


def step(token):
    return pl.pallas_call(
        step_kernel,
        out_shape=jax.ShapeDtypeStruct(token.shape, token.dtype),
        compiler_params=pltpu.CompilerParams(vmem_limit_bytes=16 * 1024 * 1024),
        cost_estimate=pl.CostEstimate(flops=STEP_FLOPS, bytes_accessed=0, transcendentals=0),
    )(token)


def plane_experts(where, rows_in, out_rows, experts, own_weights, other_weights):
    arrays = [piece[0] for piece in rows_in]
    spans = tuple(piece[1:] for piece in rows_in)
    count = sum(span[1] for span in spans)
    padded = arrays[0].shape[1]
    width, hidden = own_weights[0].shape[1:]
    weights = [w for pair in zip(own_weights, other_weights) for w in pair]
    vmem = pl.BlockSpec(memory_space=pltpu.VMEM)
    return pl.pallas_call(
        functools.partial(experts_kernel, spans, experts),
        out_shape=tuple(jax.ShapeDtypeStruct((size, width), BF16) for size in out_rows),
        in_specs=[pl.BlockSpec(memory_space=pltpu.SMEM)] + [vmem] * (len(spans) + 6),
        out_specs=[vmem] * len(out_rows),
        scratch_shapes=[pltpu.VMEM((count, padded), BF16)],
        compiler_params=pltpu.CompilerParams(vmem_limit_bytes=24 * 1024 * 1024),
        cost_estimate=pl.CostEstimate(flops=STEP_FLOPS, bytes_accessed=0, transcendentals=0),
    )(where, *arrays, *weights)


def final_kernel(token_ref, residual_ref, *refs):
    out_ref = refs[-1]
    mix = refs[0][...].astype(F32)
    for ref in refs[1:-1]:
        mix = mix + ref[...].astype(F32)
    out_ref[...] = (residual_ref[...] + mix).astype(BF16)


def final_sum(token, residual, pieces):
    return pl.pallas_call(
        final_kernel,
        out_shape=jax.ShapeDtypeStruct(residual.shape, BF16),
        compiler_params=pltpu.CompilerParams(vmem_limit_bytes=16 * 1024 * 1024),
    )(token, residual, *pieces)


def add_bf16(*terms):
    total = terms[0].astype(F32)
    for term in terms[1:]:
        total = total + term.astype(F32)
    return total.astype(BF16)


def on_device(
    hidden_in,
    queries,
    out_gate,
    draft_kv,
    cache_keys,
    cache_values,
    draft_len,
    cache_len,
    o_weight,
    norm_gain,
    route_ids,
    route_weights,
    w_gate,
    w_up,
    w_down,
):
    wide = lax.axis_size("wide")
    narrow = lax.axis_size("narrow")
    chip = lax.axis_index("wide")
    core = lax.axis_index("narrow")
    plane = 4
    planes = wide // plane
    assert narrow == 2 and wide % plane == 0 and planes > 2
    experts = wide * narrow
    own_rows, width = hidden_in.shape
    mid = own_rows // 2

    swap = [(0, 1), (1, 0)]
    own_weights = (w_gate, w_up, w_down)
    other_weights = [lax.ppermute(w, "narrow", swap) for w in own_weights]

    arrays = (queries, out_gate, draft_kv, cache_keys, cache_values, draft_len, cache_len, o_weight)
    outgoing, kept, table, gain = attention(
        core, experts, hidden_in, norm_gain, route_ids, route_weights, arrays
    )
    received = lax.ppermute(outgoing, "narrow", swap)
    residual, sent = residual_norm(kept, received, gain, table)

    def across(flips):
        pairs = [
            (i * narrow + c, (i ^ flips[c]) * narrow + c) for i in range(wide) for c in range(narrow)
        ]
        return lambda a: lax.ppermute(a, ("wide", "narrow"), pairs)

    def shifted(by):
        pairs = [(i, (i + by * plane) % wide) for i in range(wide)]
        return lambda a: lax.ppermute(a, "wide", pairs)

    over_u, over_v = across((1, 2)), across((2, 1))
    own_expert = chip * narrow + core
    where = jnp.stack([own_expert, own_expert ^ 1]).astype(jnp.int32)

    b, u, v, made = {0: sent}, {}, {}, {}
    token = jnp.zeros((8, 128), F32)

    def wait(*entries, passed=()):
        nonlocal token
        arrays = [store[key] for store, key in entries]
        token, *rest = lax.optimization_barrier((token, *arrays, *passed))
        for (store, key), array in zip(entries, rest):
            store[key] = array
        return rest[len(entries) :]

    def run_experts(s):
        rows_in = [(b[s], 0, own_rows), (u[s], 0, own_rows), (v[s], 0, 2 * own_rows)]
        out_rows = [2 * own_rows] * 2 if s == 1 else [own_rows] * 4
        made[s] = list(plane_experts(index, rows_in, out_rows, experts, own_held, other_held))

    def made_entries(s):
        return [(made[s], i) for i in range(len(made[s]))]

    b[1] = shifted(1)(b[0])
    u[0] = over_u(b[0])
    index, *held = hold_weights(where, [in_hbm(w) for w in own_weights] + other_weights)
    index, *held = wait((b, 1), (u, 0), passed=[index, *held])
    own_held, other_held = held[:3], held[3:]
    for k in range(1, planes):
        if k + 1 < planes:
            b[k + 1] = shifted(1)(b[k])
        u[k] = over_u(b[k])
        v[k - 1] = over_v(jnp.concatenate([b[k - 1], u[k - 1]]))
        token = step(token)
        entries = [(u, k)]
        if k + 1 < planes:
            entries.append((b, k + 1))
        if k > 1:
            run_experts(k - 2)
            entries += made_entries(k - 2)
        wait(*entries)
    v[planes - 1] = over_v(jnp.concatenate([b[planes - 1], u[planes - 1]]))
    whole = {}
    if 1 in made:
        whole[0] = shifted(planes - 1)(made[1][0])
    token = step(token)
    run_experts(planes - 2)
    wait(*made_entries(planes - 2), (made[1], 1))
    if 0 not in whole:
        whole[0] = shifted(planes - 1)(made[1][0])
    whole[1] = shifted(planes - 1)(made[1][1])

    half = max(2, (planes + 1) // 2)
    order = list(range(half, planes - 1)) + list(range(2, half)) + [planes - 1, 0]
    back_d, back_v, back_u, back_z, sums = {}, {}, {}, {}, {}
    for s in order[:2]:
        if s in made and s:
            back_d[s] = over_v(made[s][3])
    token = step(token)
    wait((v, planes - 1))
    run_experts(planes - 1)
    wait(*made_entries(planes - 1))
    for s in order[:2]:
        if s not in back_d and s:
            back_d[s] = over_v(made[s][3])
    token = step(token)
    wait((back_d, order[0]), (whole, 0))
    for j, s in enumerate(order[:-1]):
        own, for_u, for_v, _ = made[s]
        follows = order[j + 1]
        if j:
            last = order[j - 1]
            onward = 2 * last >= planes
            back_z[last] = shifted(1 if onward else planes - last)(sums[last])
        back_u[s] = over_u(add_bf16(for_u, back_d[s]))
        back_v[s] = over_v(for_v)
        if follows and order[j + 2]:
            back_d[order[j + 2]] = over_v(made[order[j + 2]][3])
        token = step(token)
        carried = s - 1 in back_z and 2 * (s - 1) >= planes
        wait(
            (back_u, s),
            (back_v, s),
            *([(back_z, s - 1)] if carried else []),
            *([] if j else [(whole, 1)]),
            *([(back_d, follows)] if follows else []),
        )
        if j == 0:
            own_0, for_u_0, for_v_0, for_d_0 = made[0]
            own_0 = add_bf16(own_0, whole[0][:own_rows])
            for_u_0 = add_bf16(for_u_0, whole[0][own_rows:])
            back_d[0] = over_v(add_bf16(for_d_0, whole[1][own_rows:]))
            back_v[0] = over_v(add_bf16(for_v_0, whole[1][:own_rows]))
        terms = [own, back_v[s], back_u[s]]
        if carried:
            terms.append(back_z.pop(s - 1))
        sums[s] = add_bf16(*terms)
        token = step(token)
    last = planes - 1
    back_z[last] = shifted(1)(sums[last])
    token = step(token)
    wait((back_d, 0))
    back_u[0] = over_u(add_bf16(for_u_0, back_d[0]))
    results = [own_0, back_v[0], back_u[0]]
    results += [back_z[s] for s in sorted(back_z)]
    return final_sum(token, residual, results)


def solution(mesh):
    placed = (
        P(("rep", "wide", "narrow"), None),
        P(("rep", "wide"), "narrow"),
        P(("rep", "wide"), "narrow"),
        P(None, ("rep", "wide"), None),
        P(("rep", "wide"), None, None),
        P(("rep", "wide"), None, None),
        P(("rep", "wide")),
        P(("rep", "wide")),
        P("narrow", None),
        P(),
        P(("rep", "wide", "narrow"), None),
        P(("rep", "wide", "narrow"), None),
        P(("wide", "narrow"), None, None),
        P(("wide", "narrow"), None, None),
        P(("wide", "narrow"), None, None),
    )
    return jax.shard_map(
        on_device,
        mesh=mesh,
        in_specs=placed,
        out_specs=P(("rep", "wide", "narrow"), None),
        check_vma=False,
    )
```

```python
import functools
import math

import jax
import jax.numpy as jnp
from jax import lax
from jax.experimental import pallas as pl
from jax.experimental.pallas import tpu as pltpu
from jax.sharding import PartitionSpec as P

BF16 = jnp.bfloat16
F32 = jnp.float32
LOWEST = -math.inf
STEP_FLOPS = 200_000_000


def in_hbm(a):
    return pltpu.with_memory_space_constraint(a, pltpu.HBM)


def _dot(a, b):
    return jnp.dot(a, b, preferred_element_type=F32)


def _dot_t(a, b):
    return lax.dot_general(a, b, (((1,), (1,)), ((), ())), preferred_element_type=F32)


def attention_kernel(
    experts,
    core_ref,
    draft_len_ref,
    cache_len_ref,
    ids_in,
    weights_in,
    gain_in,
    hidden_in,
    queries,
    out_gate,
    draft_kv,
    cache_keys,
    cache_values,
    o_weight,
    sent_ref,
    kept_ref,
    table_ref,
    gain_ref,
    q_buf,
    g_buf,
    d_buf,
    k_buf,
    v_buf,
    w_buf,
    h_buf,
    i_buf,
    r_buf,
    attended,
    sems,
):
    core = core_ref[0]
    reqs_all, context_len, head_size = k_buf.shape
    rows_all = q_buf.shape[0]
    rows, reqs = rows_all // 2, reqs_all // 2
    drafts = rows // reqs
    heads = q_buf.shape[1] // head_size
    groups = [[], [], [], [], [], [], []]

    def fetch(group, source, target):
        at = sum(len(g) for g in groups)
        copy = pltpu.make_async_copy(source, target, sems.at[at])
        copy.start()
        groups[group].append(copy)

    def half_rows(i):
        half = 1 - core if i == 0 else core
        return pl.ds(pl.multiple_of(half * rows, rows), rows)

    def half_reqs(i):
        half = 1 - core if i == 0 else core
        return pl.ds(half * reqs, reqs)

    for i in range(2):
        here = pl.ds(i * rows, rows)
        fetch(i, queries.at[half_rows(i)], q_buf.at[here])
        fetch(i, cache_keys.at[half_reqs(i)], k_buf.at[pl.ds(i * reqs, reqs)])
        fetch(i, draft_kv.at[:, half_rows(i)], d_buf.at[:, here])
    fetch(6, ids_in, i_buf)
    fetch(6, weights_in, r_buf)
    for i in range(2):
        here = pl.ds(i * rows, rows)
        fetch(4 + i, cache_values.at[half_reqs(i)], v_buf.at[pl.ds(i * reqs, reqs)])
        fetch(4 + i, out_gate.at[half_rows(i)], g_buf.at[here])
    fetch(2, o_weight, w_buf)
    fetch(3, hidden_in, h_buf)
    fetch(3, gain_in, gain_ref)

    scale = 1.0 / math.sqrt(head_size)
    stacked = heads * drafts
    slot = lax.broadcasted_iota(jnp.int32, (stacked, context_len), 1)
    draft_slot = lax.broadcasted_iota(jnp.int32, (stacked, drafts), 1)
    draft_row = lax.broadcasted_iota(jnp.int32, (heads, drafts, drafts), 1).reshape(stacked, drafts)
    row_index = lax.broadcasted_iota(jnp.int32, (drafts, head_size), 0)
    lens = []
    for r in range(reqs_all):
        half = 1 - core if r < reqs else core
        place = half * reqs + r % reqs
        lens.append((cache_len_ref[place], draft_len_ref[place]))
    probs = []
    for r in range(reqs_all):
        if r % reqs == 0:
            for copy in groups[r // reqs]:
                copy.wait()
        span = slice(r * drafts, (r + 1) * drafts)
        query = jnp.concatenate(
            [q_buf[span, h * head_size : (h + 1) * head_size] for h in range(heads)], axis=0
        )
        cache_len, draft_len = lens[r]
        cache_scores = _dot_t(query, k_buf[r]) * scale
        draft_scores = _dot_t(query, d_buf[0, span]) * scale
        cache_scores = jnp.where(slot < cache_len, cache_scores, LOWEST)
        live = (draft_slot <= draft_row) & (draft_slot < draft_len)
        draft_scores = jnp.where(live, draft_scores, LOWEST)
        row_max = jnp.maximum(
            jnp.max(cache_scores, axis=-1, keepdims=True),
            jnp.max(draft_scores, axis=-1, keepdims=True),
        )
        cache_probs = jnp.exp(cache_scores - row_max)
        draft_probs = jnp.exp(draft_scores - row_max)
        denominator = jnp.sum(cache_probs, axis=-1, keepdims=True) + jnp.sum(
            draft_probs, axis=-1, keepdims=True
        )
        probs.append((cache_probs.astype(BF16), draft_probs.astype(BF16), denominator))
    for copy in groups[6]:
        copy.wait()
    row = lax.broadcasted_iota(jnp.int32, table_ref.shape[::-1], 0)
    table = jnp.zeros(row.shape, F32)
    for k in range(i_buf.shape[0]):
        index = i_buf[k : k + 1, :]
        weight = r_buf[k : k + 1, :]
        high = weight.astype(BF16).astype(F32)
        table = jnp.where(row == index, high, table)
        table = jnp.where(row == index + experts, weight - high, table)
    table_ref[...] = table.T.astype(BF16)
    for r in range(reqs_all):
        if r % reqs == 0:
            for copy in groups[4 + r // reqs]:
                copy.wait()
        span = slice(r * drafts, (r + 1) * drafts)
        cache_probs, draft_probs, denominator = probs[r]
        context = _dot(cache_probs, v_buf[r]) + _dot(draft_probs, d_buf[1, span])
        context = context / denominator
        draft_len = lens[r][1]
        for h in range(heads):
            cols = slice(h * head_size, (h + 1) * head_size)
            gate = jax.nn.sigmoid(g_buf[span, cols].astype(F32))
            piece = context[h * drafts : (h + 1) * drafts] * gate
            piece = jnp.where(row_index < draft_len, piece, 0.0)
            attended[span, cols] = piece.astype(BF16)
    for copy in groups[2] + groups[3]:
        copy.wait()
    rows_in = attended[...]
    width = sent_ref.shape[1]
    tile = min(512, width)
    for c in range(0, width, tile):
        cols = slice(c, c + tile)
        projected = _dot(rows_in, w_buf[:, cols])
        sent_ref[:, cols] = projected[:rows].astype(BF16)
        kept_ref[:, cols] = h_buf[:, cols].astype(F32) + projected[rows:]


def attention(core, experts, hidden, gain, ids, weights, arrays):
    queries, out_gate, draft_kv, cache_keys, cache_values, draft_len, cache_len, o_weight = arrays
    reqs_all, context_len, head_size = cache_keys.shape
    rows_all = queries.shape[0]
    own_rows = hidden.shape[0]
    inner, width = o_weight.shape
    lanes = -(-2 * experts // 128) * 128
    smem = pl.BlockSpec(memory_space=pltpu.SMEM)
    vmem = pl.BlockSpec(memory_space=pltpu.VMEM)
    hbm = pl.BlockSpec(memory_space=pl.ANY)
    ids, weights = ids.T, weights.T

    return pl.pallas_call(
        functools.partial(attention_kernel, experts),
        out_shape=(
            jax.ShapeDtypeStruct((own_rows, width), BF16),
            jax.ShapeDtypeStruct((own_rows, width), F32),
            jax.ShapeDtypeStruct((own_rows, lanes), BF16),
            jax.ShapeDtypeStruct((1, width), F32),
        ),
        in_specs=[smem] * 3 + [hbm] * 10,
        out_specs=[vmem] * 4,
        scratch_shapes=[
            pltpu.VMEM((rows_all, inner), BF16),
            pltpu.VMEM((rows_all, inner), BF16),
            pltpu.VMEM((2, rows_all, head_size), BF16),
            pltpu.VMEM(cache_keys.shape, BF16),
            pltpu.VMEM(cache_values.shape, BF16),
            pltpu.VMEM((inner, width), BF16),
            pltpu.VMEM((own_rows, width), BF16),
            pltpu.VMEM(ids.shape, jnp.int32),
            pltpu.VMEM(weights.shape, F32),
            pltpu.VMEM((rows_all, inner), BF16),
            pltpu.SemaphoreType.DMA((15,)),
        ],
        compiler_params=pltpu.CompilerParams(vmem_limit_bytes=24 * 1024 * 1024),
        cost_estimate=pl.CostEstimate(
            flops=2 * rows_all * inner * (width + 2 * context_len),
            bytes_accessed=2 * inner * width + 4 * reqs_all * context_len * head_size,
            transcendentals=0,
        ),
    )(
        core.reshape(1),
        in_hbm(draft_len),
        in_hbm(cache_len),
        *map(
            in_hbm,
            (
                ids,
                weights,
                gain.reshape(1, width),
                hidden,
                queries,
                out_gate,
                draft_kv,
                cache_keys,
                cache_values,
                o_weight,
            ),
        ),
    )


def norm_kernel(kept_ref, received_ref, gain_ref, table_ref, residual_ref, sent_ref):
    residual = kept_ref[...] + received_ref[...].astype(F32)
    width = residual.shape[1]
    spread = jnp.mean(residual * residual, axis=-1, keepdims=True)
    normed = (residual * lax.rsqrt(spread + 1e-06) * gain_ref[...]).astype(BF16)
    residual_ref[...] = residual
    sent_ref[:, :width] = normed
    sent_ref[:, width:] = table_ref[...]


def residual_norm(kept, received, gain, table):
    rows, width = kept.shape
    return pl.pallas_call(
        norm_kernel,
        out_shape=(
            jax.ShapeDtypeStruct((rows, width), F32),
            jax.ShapeDtypeStruct((rows, width + table.shape[1]), BF16),
        ),
        compiler_params=pltpu.CompilerParams(vmem_limit_bytes=16 * 1024 * 1024),
    )(kept, received, gain, table)


def experts_kernel(spans, experts, where_ref, *refs):
    pieces = len(spans)
    rows_in = refs[:pieces]
    gates, ups, downs = (refs[pieces + 2 * i : pieces + 2 + 2 * i] for i in range(3))
    outs, rows = refs[pieces + 6 : -1], refs[-1]
    width = outs[0].shape[1]
    at = 0
    for ref, (start, size) in zip(rows_in, spans):
        rows[at : at + size] = ref[start : start + size]
        at += size
    table = rows[:, width:].astype(F32)
    column = lax.broadcasted_iota(jnp.int32, table.shape, 1)
    block = rows[:, :width]
    acts = []
    for e in range(2):
        index = where_ref[e]
        chosen = (column == index) | (column == index + experts)
        weight = jnp.sum(jnp.where(chosen, table, 0.0), axis=1, keepdims=True)
        gate = _dot(block, gates[e][0])
        up = _dot(block, ups[e][0])
        acts.append((jax.nn.silu(gate) * up * weight).astype(BF16))
    tile = min(512, width)
    for c in range(0, width, tile):
        cols = slice(c, c + tile)
        made = _dot(acts[0], downs[0][0, :, cols]) + _dot(acts[1], downs[1][0, :, cols])
        at = 0
        for out in outs:
            size = out.shape[0]
            out[:, cols] = made[at : at + size].astype(BF16)
            at += size


def hold_kernel(count, where_ref, *refs):
    sources, out_ref, held, sems = refs[:count], refs[count], refs[count + 1 : -1], refs[-1]
    copies = [
        pltpu.make_async_copy(source, target, sems.at[i])
        for i, (source, target) in enumerate(zip(sources, held))
    ]
    for copy in copies:
        copy.start()
    for i in range(out_ref.shape[0]):
        out_ref[i] = where_ref[i]
    for copy in copies:
        copy.wait()


def hold_weights(where, weights):
    count = len(weights)
    vmem = pl.BlockSpec(memory_space=pltpu.VMEM)
    smem = pl.BlockSpec(memory_space=pltpu.SMEM)
    return pl.pallas_call(
        functools.partial(hold_kernel, count),
        out_shape=[jax.ShapeDtypeStruct(where.shape, where.dtype)]
        + [jax.ShapeDtypeStruct(w.shape, w.dtype) for w in weights],
        in_specs=[smem] + [pl.BlockSpec(memory_space=pl.ANY)] * count,
        out_specs=[smem] + [vmem] * count,
        scratch_shapes=[pltpu.SemaphoreType.DMA((max(1, count),))],
        compiler_params=pltpu.CompilerParams(vmem_limit_bytes=16 * 1024 * 1024),
        cost_estimate=pl.CostEstimate(flops=STEP_FLOPS, bytes_accessed=0, transcendentals=0),
    )(where, *weights)


def step_kernel(token_ref, out_ref):
    out_ref[...] = token_ref[...]


def step(token):
    return pl.pallas_call(
        step_kernel,
        out_shape=jax.ShapeDtypeStruct(token.shape, token.dtype),
        compiler_params=pltpu.CompilerParams(vmem_limit_bytes=16 * 1024 * 1024),
        cost_estimate=pl.CostEstimate(flops=STEP_FLOPS, bytes_accessed=0, transcendentals=0),
    )(token)


def plane_experts(where, rows_in, out_rows, experts, own_weights, other_weights):
    arrays = [piece[0] for piece in rows_in]
    spans = tuple(piece[1:] for piece in rows_in)
    count = sum(span[1] for span in spans)
    padded = arrays[0].shape[1]
    width, hidden = own_weights[0].shape[1:]
    weights = [w for pair in zip(own_weights, other_weights) for w in pair]
    vmem = pl.BlockSpec(memory_space=pltpu.VMEM)
    return pl.pallas_call(
        functools.partial(experts_kernel, spans, experts),
        out_shape=tuple(jax.ShapeDtypeStruct((size, width), BF16) for size in out_rows),
        in_specs=[pl.BlockSpec(memory_space=pltpu.SMEM)] + [vmem] * (len(spans) + 6),
        out_specs=[vmem] * len(out_rows),
        scratch_shapes=[pltpu.VMEM((count, padded), BF16)],
        compiler_params=pltpu.CompilerParams(vmem_limit_bytes=24 * 1024 * 1024),
        cost_estimate=pl.CostEstimate(flops=STEP_FLOPS, bytes_accessed=0, transcendentals=0),
    )(where, *arrays, *weights)


def final_kernel(token_ref, residual_ref, *refs):
    out_ref = refs[-1]
    mix = refs[0][...].astype(F32)
    for ref in refs[1:-1]:
        mix = mix + ref[...].astype(F32)
    out_ref[...] = (residual_ref[...] + mix).astype(BF16)


def final_sum(token, residual, pieces):
    return pl.pallas_call(
        final_kernel,
        out_shape=jax.ShapeDtypeStruct(residual.shape, BF16),
        compiler_params=pltpu.CompilerParams(vmem_limit_bytes=16 * 1024 * 1024),
    )(token, residual, *pieces)


def add_bf16(*terms):
    total = terms[0].astype(F32)
    for term in terms[1:]:
        total = total + term.astype(F32)
    return total.astype(BF16)


def on_device(
    hidden_in,
    queries,
    out_gate,
    draft_kv,
    cache_keys,
    cache_values,
    draft_len,
    cache_len,
    o_weight,
    norm_gain,
    route_ids,
    route_weights,
    w_gate,
    w_up,
    w_down,
):
    wide = lax.axis_size("wide")
    narrow = lax.axis_size("narrow")
    chip = lax.axis_index("wide")
    core = lax.axis_index("narrow")
    plane = 4
    planes = wide // plane
    assert narrow == 2 and wide % plane == 0 and planes > 2
    experts = wide * narrow
    own_rows, width = hidden_in.shape
    mid = own_rows // 2

    swap = [(0, 1), (1, 0)]
    own_weights = (w_gate, w_up, w_down)
    other_weights = [lax.ppermute(w, "narrow", swap) for w in own_weights]

    arrays = (queries, out_gate, draft_kv, cache_keys, cache_values, draft_len, cache_len, o_weight)
    outgoing, kept, table, gain = attention(
        core, experts, hidden_in, norm_gain, route_ids, route_weights, arrays
    )
    received = lax.ppermute(outgoing, "narrow", swap)
    residual, sent = residual_norm(kept, received, gain, table)

    def across(flips):
        pairs = [
            (i * narrow + c, (i ^ flips[c]) * narrow + c) for i in range(wide) for c in range(narrow)
        ]
        return lambda a: lax.ppermute(a, ("wide", "narrow"), pairs)

    def shifted(by):
        pairs = [(i, (i + by * plane) % wide) for i in range(wide)]
        return lambda a: lax.ppermute(a, "wide", pairs)

    over_u, over_v = across((1, 2)), across((2, 1))
    own_expert = chip * narrow + core
    where = jnp.stack([own_expert, own_expert ^ 1]).astype(jnp.int32)

    b, u, v, made = {0: sent}, {}, {}, {}
    token = jnp.zeros((8, 128), F32)

    def wait(*entries, passed=()):
        nonlocal token
        arrays = [store[key] for store, key in entries]
        token, *rest = lax.optimization_barrier((token, *arrays, *passed))
        for (store, key), array in zip(entries, rest):
            store[key] = array
        return rest[len(entries) :]

    def run_experts(s):
        rows_in = [(b[s], 0, own_rows), (u[s], 0, own_rows), (v[s], 0, 2 * own_rows)]
        out_rows = [2 * own_rows] * 2 if s == 1 else [own_rows] * 4
        made[s] = list(plane_experts(index, rows_in, out_rows, experts, own_held, other_held))

    def made_entries(s):
        return [(made[s], i) for i in range(len(made[s]))]

    b[1] = shifted(1)(b[0])
    u[0] = over_u(b[0])
    index, *held = hold_weights(where, [in_hbm(w) for w in own_weights] + other_weights)
    index, *held = wait((b, 1), (u, 0), passed=[index, *held])
    own_held, other_held = held[:3], held[3:]
    for k in range(1, planes):
        if k + 1 < planes:
            b[k + 1] = shifted(1)(b[k])
        u[k] = over_u(b[k])
        v[k - 1] = over_v(jnp.concatenate([b[k - 1], u[k - 1]]))
        token = step(token)
        entries = [(u, k)]
        if k + 1 < planes:
            entries.append((b, k + 1))
        if k > 1:
            run_experts(k - 2)
            entries += made_entries(k - 2)
        wait(*entries)
    v[planes - 1] = over_v(jnp.concatenate([b[planes - 1], u[planes - 1]]))
    whole = {}
    if 1 in made:
        whole[0] = shifted(planes - 1)(made[1][0])
    token = step(token)
    run_experts(planes - 2)
    wait(*made_entries(planes - 2), (made[1], 1))
    if 0 not in whole:
        whole[0] = shifted(planes - 1)(made[1][0])
    whole[1] = shifted(planes - 1)(made[1][1])

    half = max(2, (planes + 1) // 2)
    order = list(range(half, planes - 1)) + list(range(2, half)) + [planes - 1, 0]
    back_d, back_v, back_u, back_z, sums = {}, {}, {}, {}, {}
    for s in order[:2]:
        if s in made and s:
            back_d[s] = over_v(made[s][3])
    token = step(token)
    wait((v, planes - 1))
    run_experts(planes - 1)
    wait(*made_entries(planes - 1))
    for s in order[:2]:
        if s not in back_d and s:
            back_d[s] = over_v(made[s][3])
    token = step(token)
    wait((back_d, order[0]), (whole, 0))
    for j, s in enumerate(order[:-1]):
        own, for_u, for_v, _ = made[s]
        follows = order[j + 1]
        if j:
            last = order[j - 1]
            onward = 2 * last >= planes
            back_z[last] = shifted(1 if onward else planes - last)(sums[last])
        back_u[s] = over_u(add_bf16(for_u, back_d[s]))
        back_v[s] = over_v(for_v)
        if follows and order[j + 2]:
            back_d[order[j + 2]] = over_v(made[order[j + 2]][3])
        token = step(token)
        carried = s - 1 in back_z and 2 * (s - 1) >= planes
        wait(
            (back_u, s),
            (back_v, s),
            *([(back_z, s - 1)] if carried else []),
            *([] if j else [(whole, 1)]),
            *([(back_d, follows)] if follows else []),
        )
        if j == 0:
            own_0, for_u_0, for_v_0, for_d_0 = made[0]
            own_0 = add_bf16(own_0, whole[0][:own_rows])
            for_u_0 = add_bf16(for_u_0, whole[0][own_rows:])
            back_d[0] = over_v(add_bf16(for_d_0, whole[1][own_rows:]))
            back_v[0] = over_v(add_bf16(for_v_0, whole[1][:own_rows]))
        terms = [own, back_v[s], back_u[s]]
        if carried:
            terms.append(back_z.pop(s - 1))
        sums[s] = add_bf16(*terms)
        token = step(token)
    last = planes - 1
    back_z[last] = shifted(1)(sums[last])
    token = step(token)
    wait((back_d, 0))
    back_u[0] = over_u(add_bf16(for_u_0, back_d[0]))
    results = [own_0, back_v[0], back_u[0]]
    results += [back_z[s] for s in sorted(back_z)]
    return final_sum(token, residual, results)


def solution(mesh):
    placed = (
        P(("rep", "wide", "narrow"), None),
        P(("rep", "wide"), "narrow"),
        P(("rep", "wide"), "narrow"),
        P(None, ("rep", "wide"), None),
        P(("rep", "wide"), None, None),
        P(("rep", "wide"), None, None),
        P(("rep", "wide")),
        P(("rep", "wide")),
        P("narrow", None),
        P(),
        P(("rep", "wide", "narrow"), None),
        P(("rep", "wide", "narrow"), None),
        P(("wide", "narrow"), None, None),
        P(("wide", "narrow"), None, None),
        P(("wide", "narrow"), None, None),
    )
    return jax.shard_map(
        on_device,
        mesh=mesh,
        in_specs=placed,
        out_specs=P(("rep", "wide", "narrow"), None),
        check_vma=False,
    )
```

```python
import functools
import math

import jax
import jax.numpy as jnp
from jax import lax
from jax.experimental import pallas as pl
from jax.experimental.pallas import tpu as pltpu
from jax.sharding import PartitionSpec as P

BF16 = jnp.bfloat16
F32 = jnp.float32
LOWEST = -math.inf
STEP_FLOPS = 200_000_000


def in_hbm(a):
    return pltpu.with_memory_space_constraint(a, pltpu.HBM)


def _dot(a, b):
    return jnp.dot(a, b, preferred_element_type=F32)


def _dot_t(a, b):
    return lax.dot_general(a, b, (((1,), (1,)), ((), ())), preferred_element_type=F32)


def attention_kernel(
    experts,
    core_ref,
    draft_len_ref,
    cache_len_ref,
    ids_in,
    weights_in,
    gain_in,
    hidden_in,
    queries,
    out_gate,
    draft_kv,
    cache_keys,
    cache_values,
    o_weight,
    sent_ref,
    kept_ref,
    table_ref,
    gain_ref,
    q_buf,
    g_buf,
    d_buf,
    k_buf,
    v_buf,
    w_buf,
    h_buf,
    i_buf,
    r_buf,
    attended,
    sems,
):
    core = core_ref[0]
    reqs_all, context_len, head_size = k_buf.shape
    rows_all = q_buf.shape[0]
    rows, reqs = rows_all // 2, reqs_all // 2
    drafts = rows // reqs
    heads = q_buf.shape[1] // head_size
    groups = [[], [], [], []]

    def fetch(group, source, target):
        at = sum(len(g) for g in groups)
        copy = pltpu.make_async_copy(source, target, sems.at[at])
        copy.start()
        groups[group].append(copy)

    def half_rows(i):
        half = 1 - core if i == 0 else core
        return pl.ds(pl.multiple_of(half * rows, rows), rows)

    def half_reqs(i):
        half = 1 - core if i == 0 else core
        return pl.ds(half * reqs, reqs)

    fetch(0, ids_in, i_buf)
    fetch(0, weights_in, r_buf)
    for i in range(2):
        here = pl.ds(i * rows, rows)
        fetch(0, queries.at[half_rows(i)], q_buf.at[here])
        fetch(0, cache_keys.at[half_reqs(i)], k_buf.at[pl.ds(i * reqs, reqs)])
        fetch(0, draft_kv.at[:, half_rows(i)], d_buf.at[:, here])
    for i in range(2):
        here = pl.ds(i * rows, rows)
        fetch(1, cache_values.at[half_reqs(i)], v_buf.at[pl.ds(i * reqs, reqs)])
        fetch(1, out_gate.at[half_rows(i)], g_buf.at[here])
    fetch(2, o_weight, w_buf)
    fetch(3, hidden_in, h_buf)
    fetch(3, gain_in, gain_ref)

    for copy in groups[0]:
        copy.wait()
    scale = 1.0 / math.sqrt(head_size)
    stacked = heads * drafts
    slot = lax.broadcasted_iota(jnp.int32, (stacked, context_len), 1)
    draft_slot = lax.broadcasted_iota(jnp.int32, (stacked, drafts), 1)
    draft_row = lax.broadcasted_iota(jnp.int32, (heads, drafts, drafts), 1).reshape(stacked, drafts)
    row_index = lax.broadcasted_iota(jnp.int32, (drafts, head_size), 0)
    lens = []
    for r in range(reqs_all):
        half = 1 - core if r < reqs else core
        place = half * reqs + r % reqs
        lens.append((cache_len_ref[place], draft_len_ref[place]))
    probs = []
    for r in range(reqs_all):
        span = slice(r * drafts, (r + 1) * drafts)
        query = jnp.concatenate(
            [q_buf[span, h * head_size : (h + 1) * head_size] for h in range(heads)], axis=0
        )
        cache_len, draft_len = lens[r]
        cache_scores = _dot_t(query, k_buf[r]) * scale
        draft_scores = _dot_t(query, d_buf[0, span]) * scale
        cache_scores = jnp.where(slot < cache_len, cache_scores, LOWEST)
        live = (draft_slot <= draft_row) & (draft_slot < draft_len)
        draft_scores = jnp.where(live, draft_scores, LOWEST)
        row_max = jnp.maximum(
            jnp.max(cache_scores, axis=-1, keepdims=True),
            jnp.max(draft_scores, axis=-1, keepdims=True),
        )
        cache_probs = jnp.exp(cache_scores - row_max)
        draft_probs = jnp.exp(draft_scores - row_max)
        denominator = jnp.sum(cache_probs, axis=-1, keepdims=True) + jnp.sum(
            draft_probs, axis=-1, keepdims=True
        )
        probs.append((cache_probs.astype(BF16), draft_probs.astype(BF16), denominator))
    row = lax.broadcasted_iota(jnp.int32, table_ref.shape[::-1], 0)
    table = jnp.zeros(row.shape, F32)
    for k in range(i_buf.shape[0]):
        index = i_buf[k : k + 1, :]
        weight = r_buf[k : k + 1, :]
        high = weight.astype(BF16).astype(F32)
        table = jnp.where(row == index, high, table)
        table = jnp.where(row == index + experts, weight - high, table)
    table_ref[...] = table.T.astype(BF16)
    for copy in groups[1]:
        copy.wait()
    for r in range(reqs_all):
        span = slice(r * drafts, (r + 1) * drafts)
        cache_probs, draft_probs, denominator = probs[r]
        context = _dot(cache_probs, v_buf[r]) + _dot(draft_probs, d_buf[1, span])
        context = context / denominator
        draft_len = lens[r][1]
        for h in range(heads):
            cols = slice(h * head_size, (h + 1) * head_size)
            gate = jax.nn.sigmoid(g_buf[span, cols].astype(F32))
            piece = context[h * drafts : (h + 1) * drafts] * gate
            piece = jnp.where(row_index < draft_len, piece, 0.0)
            attended[span, cols] = piece.astype(BF16)
    for copy in groups[2] + groups[3]:
        copy.wait()
    rows_in = attended[...]
    width = sent_ref.shape[1]
    tile = min(512, width)
    for c in range(0, width, tile):
        cols = slice(c, c + tile)
        projected = _dot(rows_in, w_buf[:, cols])
        sent_ref[:, cols] = projected[:rows].astype(BF16)
        kept_ref[:, cols] = h_buf[:, cols].astype(F32) + projected[rows:]


def attention(core, experts, hidden, gain, ids, weights, arrays):
    queries, out_gate, draft_kv, cache_keys, cache_values, draft_len, cache_len, o_weight = arrays
    reqs_all, context_len, head_size = cache_keys.shape
    rows_all = queries.shape[0]
    own_rows = hidden.shape[0]
    inner, width = o_weight.shape
    lanes = -(-2 * experts // 128) * 128
    smem = pl.BlockSpec(memory_space=pltpu.SMEM)
    vmem = pl.BlockSpec(memory_space=pltpu.VMEM)
    hbm = pl.BlockSpec(memory_space=pl.ANY)
    ids, weights = ids.T, weights.T

    return pl.pallas_call(
        functools.partial(attention_kernel, experts),
        out_shape=(
            jax.ShapeDtypeStruct((own_rows, width), BF16),
            jax.ShapeDtypeStruct((own_rows, width), F32),
            jax.ShapeDtypeStruct((own_rows, lanes), BF16),
            jax.ShapeDtypeStruct((1, width), F32),
        ),
        in_specs=[smem] * 3 + [hbm] * 10,
        out_specs=[vmem] * 4,
        scratch_shapes=[
            pltpu.VMEM((rows_all, inner), BF16),
            pltpu.VMEM((rows_all, inner), BF16),
            pltpu.VMEM((2, rows_all, head_size), BF16),
            pltpu.VMEM(cache_keys.shape, BF16),
            pltpu.VMEM(cache_values.shape, BF16),
            pltpu.VMEM((inner, width), BF16),
            pltpu.VMEM((own_rows, width), BF16),
            pltpu.VMEM(ids.shape, jnp.int32),
            pltpu.VMEM(weights.shape, F32),
            pltpu.VMEM((rows_all, inner), BF16),
            pltpu.SemaphoreType.DMA((15,)),
        ],
        compiler_params=pltpu.CompilerParams(vmem_limit_bytes=24 * 1024 * 1024),
        cost_estimate=pl.CostEstimate(
            flops=2 * rows_all * inner * (width + 2 * context_len),
            bytes_accessed=2 * inner * width + 4 * reqs_all * context_len * head_size,
            transcendentals=0,
        ),
    )(
        core.reshape(1),
        in_hbm(draft_len),
        in_hbm(cache_len),
        *map(
            in_hbm,
            (
                ids,
                weights,
                gain.reshape(1, width),
                hidden,
                queries,
                out_gate,
                draft_kv,
                cache_keys,
                cache_values,
                o_weight,
            ),
        ),
    )


def norm_kernel(kept_ref, received_ref, gain_ref, table_ref, residual_ref, sent_ref):
    residual = kept_ref[...] + received_ref[...].astype(F32)
    width = residual.shape[1]
    spread = jnp.mean(residual * residual, axis=-1, keepdims=True)
    normed = (residual * lax.rsqrt(spread + 1e-06) * gain_ref[...]).astype(BF16)
    residual_ref[...] = residual
    sent_ref[:, :width] = normed
    sent_ref[:, width:] = table_ref[...]


def residual_norm(kept, received, gain, table):
    rows, width = kept.shape
    return pl.pallas_call(
        norm_kernel,
        out_shape=(
            jax.ShapeDtypeStruct((rows, width), F32),
            jax.ShapeDtypeStruct((rows, width + table.shape[1]), BF16),
        ),
        compiler_params=pltpu.CompilerParams(vmem_limit_bytes=16 * 1024 * 1024),
    )(kept, received, gain, table)


def experts_kernel(spans, experts, where_ref, *refs):
    pieces = len(spans)
    rows_in = refs[:pieces]
    gates, ups, downs = (refs[pieces + 2 * i : pieces + 2 + 2 * i] for i in range(3))
    outs, rows = refs[pieces + 6 : -1], refs[-1]
    width = outs[0].shape[1]
    at = 0
    for ref, (start, size) in zip(rows_in, spans):
        rows[at : at + size] = ref[start : start + size]
        at += size
    table = rows[:, width:].astype(F32)
    column = lax.broadcasted_iota(jnp.int32, table.shape, 1)
    block = rows[:, :width]
    acts = []
    for e in range(2):
        index = where_ref[e]
        chosen = (column == index) | (column == index + experts)
        weight = jnp.sum(jnp.where(chosen, table, 0.0), axis=1, keepdims=True)
        gate = _dot(block, gates[e][0])
        up = _dot(block, ups[e][0])
        acts.append((jax.nn.silu(gate) * up * weight).astype(BF16))
    tile = min(512, width)
    for c in range(0, width, tile):
        cols = slice(c, c + tile)
        made = _dot(acts[0], downs[0][0, :, cols]) + _dot(acts[1], downs[1][0, :, cols])
        at = 0
        for out in outs:
            size = out.shape[0]
            out[:, cols] = made[at : at + size].astype(BF16)
            at += size


def hold_kernel(count, where_ref, *refs):
    sources, out_ref, held, sems = refs[:count], refs[count], refs[count + 1 : -1], refs[-1]
    copies = [
        pltpu.make_async_copy(source, target, sems.at[i])
        for i, (source, target) in enumerate(zip(sources, held))
    ]
    for copy in copies:
        copy.start()
    for i in range(out_ref.shape[0]):
        out_ref[i] = where_ref[i]
    for copy in copies:
        copy.wait()


def hold_weights(where, weights):
    count = len(weights)
    vmem = pl.BlockSpec(memory_space=pltpu.VMEM)
    smem = pl.BlockSpec(memory_space=pltpu.SMEM)
    return pl.pallas_call(
        functools.partial(hold_kernel, count),
        out_shape=[jax.ShapeDtypeStruct(where.shape, where.dtype)]
        + [jax.ShapeDtypeStruct(w.shape, w.dtype) for w in weights],
        in_specs=[smem] + [pl.BlockSpec(memory_space=pl.ANY)] * count,
        out_specs=[smem] + [vmem] * count,
        scratch_shapes=[pltpu.SemaphoreType.DMA((max(1, count),))],
        compiler_params=pltpu.CompilerParams(vmem_limit_bytes=16 * 1024 * 1024),
        cost_estimate=pl.CostEstimate(flops=STEP_FLOPS, bytes_accessed=0, transcendentals=0),
    )(where, *weights)


def step_kernel(token_ref, out_ref):
    out_ref[...] = token_ref[...]


def step(token):
    return pl.pallas_call(
        step_kernel,
        out_shape=jax.ShapeDtypeStruct(token.shape, token.dtype),
        compiler_params=pltpu.CompilerParams(vmem_limit_bytes=16 * 1024 * 1024),
        cost_estimate=pl.CostEstimate(flops=STEP_FLOPS, bytes_accessed=0, transcendentals=0),
    )(token)


def plane_experts(where, rows_in, out_rows, experts, own_weights, other_weights):
    arrays = [piece[0] for piece in rows_in]
    spans = tuple(piece[1:] for piece in rows_in)
    count = sum(span[1] for span in spans)
    padded = arrays[0].shape[1]
    width, hidden = own_weights[0].shape[1:]
    weights = [w for pair in zip(own_weights, other_weights) for w in pair]
    vmem = pl.BlockSpec(memory_space=pltpu.VMEM)
    return pl.pallas_call(
        functools.partial(experts_kernel, spans, experts),
        out_shape=tuple(jax.ShapeDtypeStruct((size, width), BF16) for size in out_rows),
        in_specs=[pl.BlockSpec(memory_space=pltpu.SMEM)] + [vmem] * (len(spans) + 6),
        out_specs=[vmem] * len(out_rows),
        scratch_shapes=[pltpu.VMEM((count, padded), BF16)],
        compiler_params=pltpu.CompilerParams(vmem_limit_bytes=24 * 1024 * 1024),
        cost_estimate=pl.CostEstimate(flops=STEP_FLOPS, bytes_accessed=0, transcendentals=0),
    )(where, *arrays, *weights)


def final_kernel(tiles, token_ref, residual_ref, *refs):
    pieces, out_ref, made, sems = refs[:-3], refs[-3], refs[-2], refs[-1]
    size = residual_ref.shape[0] // tiles
    copies = []
    for t in range(tiles):
        span = slice(t * size, (t + 1) * size)
        mix = pieces[0][span].astype(F32)
        for ref in pieces[1:]:
            mix = mix + ref[span].astype(F32)
        made[span] = (residual_ref[span] + mix).astype(BF16)
        rows = pl.ds(t * size, size)
        copy = pltpu.make_async_copy(made.at[rows], out_ref.at[rows], sems.at[t])
        copy.start()
        copies.append(copy)
    for copy in copies:
        copy.wait()


def final_sum(token, residual, pieces):
    tiles = max(1, residual.shape[0] // 16)
    vmem = pl.BlockSpec(memory_space=pltpu.VMEM)
    return pl.pallas_call(
        functools.partial(final_kernel, tiles),
        out_shape=jax.ShapeDtypeStruct(residual.shape, BF16),
        in_specs=[vmem] * (2 + len(pieces)),
        out_specs=pl.BlockSpec(memory_space=pl.ANY),
        scratch_shapes=[pltpu.VMEM(residual.shape, BF16), pltpu.SemaphoreType.DMA((tiles,))],
        compiler_params=pltpu.CompilerParams(vmem_limit_bytes=16 * 1024 * 1024),
    )(token, residual, *pieces)


def add_bf16(*terms):
    total = terms[0].astype(F32)
    for term in terms[1:]:
        total = total + term.astype(F32)
    return total.astype(BF16)


def on_device(
    hidden_in,
    queries,
    out_gate,
    draft_kv,
    cache_keys,
    cache_values,
    draft_len,
    cache_len,
    o_weight,
    norm_gain,
    route_ids,
    route_weights,
    w_gate,
    w_up,
    w_down,
):
    wide = lax.axis_size("wide")
    narrow = lax.axis_size("narrow")
    chip = lax.axis_index("wide")
    core = lax.axis_index("narrow")
    plane = 4
    planes = wide // plane
    assert narrow == 2 and wide % plane == 0 and planes > 2
    experts = wide * narrow
    own_rows, width = hidden_in.shape
    mid = own_rows // 2

    swap = [(0, 1), (1, 0)]
    own_weights = (w_gate, w_up, w_down)
    other_weights = [lax.ppermute(w, "narrow", swap) for w in own_weights]

    arrays = (queries, out_gate, draft_kv, cache_keys, cache_values, draft_len, cache_len, o_weight)
    outgoing, kept, table, gain = attention(
        core, experts, hidden_in, norm_gain, route_ids, route_weights, arrays
    )
    received = lax.ppermute(outgoing, "narrow", swap)
    residual, sent = residual_norm(kept, received, gain, table)

    def across(flips):
        pairs = [
            (i * narrow + c, (i ^ flips[c]) * narrow + c) for i in range(wide) for c in range(narrow)
        ]
        return lambda a: lax.ppermute(a, ("wide", "narrow"), pairs)

    def shifted(by):
        pairs = [(i, (i + by * plane) % wide) for i in range(wide)]
        return lambda a: lax.ppermute(a, "wide", pairs)

    over_u, over_v = across((1, 2)), across((2, 1))
    own_expert = chip * narrow + core
    where = jnp.stack([own_expert, own_expert ^ 1]).astype(jnp.int32)

    b, u, v, made = {0: sent}, {}, {}, {}
    token = jnp.zeros((8, 128), F32)

    def wait(*entries, passed=()):
        nonlocal token
        arrays = [store[key] for store, key in entries]
        token, *rest = lax.optimization_barrier((token, *arrays, *passed))
        for (store, key), array in zip(entries, rest):
            store[key] = array
        return rest[len(entries) :]

    def run_experts(s):
        rows_in = [(b[s], 0, own_rows), (u[s], 0, own_rows), (v[s], 0, 2 * own_rows)]
        out_rows = [2 * own_rows] * 2 if s == 1 else [own_rows] * 4
        made[s] = list(plane_experts(index, rows_in, out_rows, experts, own_held, other_held))

    def made_entries(s):
        return [(made[s], i) for i in range(len(made[s]))]

    b[1] = shifted(1)(b[0])
    u[0] = over_u(b[0])
    index, *held = hold_weights(where, [in_hbm(w) for w in own_weights] + other_weights)
    index, *held = wait((b, 1), (u, 0), passed=[index, *held])
    own_held, other_held = held[:3], held[3:]
    for k in range(1, planes):
        if k + 1 < planes:
            b[k + 1] = shifted(1)(b[k])
        u[k] = over_u(b[k])
        v[k - 1] = over_v(jnp.concatenate([b[k - 1], u[k - 1]]))
        token = step(token)
        entries = [(u, k)]
        if k + 1 < planes:
            entries.append((b, k + 1))
        if k > 1:
            run_experts(k - 2)
            entries += made_entries(k - 2)
        wait(*entries)
    v[planes - 1] = over_v(jnp.concatenate([b[planes - 1], u[planes - 1]]))
    whole = {}
    if 1 in made:
        whole[0] = shifted(planes - 1)(made[1][0])
    token = step(token)
    run_experts(planes - 2)
    wait(*made_entries(planes - 2), (made[1], 1))
    if 0 not in whole:
        whole[0] = shifted(planes - 1)(made[1][0])
    whole[1] = shifted(planes - 1)(made[1][1])

    half = max(2, (planes + 1) // 2)
    order = list(range(half, planes - 1)) + list(range(2, half)) + [planes - 1, 0]
    back_d, back_v, back_u, back_z, sums = {}, {}, {}, {}, {}
    for s in order[:2]:
        if s in made and s:
            back_d[s] = over_v(made[s][3])
    token = step(token)
    wait((v, planes - 1))
    run_experts(planes - 1)
    wait(*made_entries(planes - 1))
    for s in order[:2]:
        if s not in back_d and s:
            back_d[s] = over_v(made[s][3])
    token = step(token)
    wait((back_d, order[0]), (whole, 0))
    for j, s in enumerate(order[:-1]):
        own, for_u, for_v, _ = made[s]
        follows = order[j + 1]
        if j:
            last = order[j - 1]
            onward = 2 * last >= planes
            back_z[last] = shifted(1 if onward else planes - last)(sums[last])
        back_u[s] = over_u(add_bf16(for_u, back_d[s]))
        back_v[s] = over_v(for_v)
        if follows and order[j + 2]:
            back_d[order[j + 2]] = over_v(made[order[j + 2]][3])
        token = step(token)
        carried = s - 1 in back_z and 2 * (s - 1) >= planes
        wait(
            (back_u, s),
            (back_v, s),
            *([(back_z, s - 1)] if carried else []),
            *([] if j else [(whole, 1)]),
            *([(back_d, follows)] if follows else []),
        )
        if j == 0:
            own_0, for_u_0, for_v_0, for_d_0 = made[0]
            own_0 = add_bf16(own_0, whole[0][:own_rows])
            for_u_0 = add_bf16(for_u_0, whole[0][own_rows:])
            back_d[0] = over_v(add_bf16(for_d_0, whole[1][own_rows:]))
            back_v[0] = over_v(add_bf16(for_v_0, whole[1][:own_rows]))
        terms = [own, back_v[s], back_u[s]]
        if carried:
            terms.append(back_z.pop(s - 1))
        sums[s] = add_bf16(*terms)
        token = step(token)
    last = planes - 1
    back_z[last] = shifted(1)(sums[last])
    token = step(token)
    wait((back_d, 0))
    back_u[0] = over_u(add_bf16(for_u_0, back_d[0]))
    results = [own_0, back_v[0], back_u[0]]
    results += [back_z[s] for s in sorted(back_z)]
    return final_sum(token, residual, results)


def solution(mesh):
    placed = (
        P(("rep", "wide", "narrow"), None),
        P(("rep", "wide"), "narrow"),
        P(("rep", "wide"), "narrow"),
        P(None, ("rep", "wide"), None),
        P(("rep", "wide"), None, None),
        P(("rep", "wide"), None, None),
        P(("rep", "wide")),
        P(("rep", "wide")),
        P("narrow", None),
        P(),
        P(("rep", "wide", "narrow"), None),
        P(("rep", "wide", "narrow"), None),
        P(("wide", "narrow"), None, None),
        P(("wide", "narrow"), None, None),
        P(("wide", "narrow"), None, None),
    )
    return jax.shard_map(
        on_device,
        mesh=mesh,
        in_specs=placed,
        out_specs=P(("rep", "wide", "narrow"), None),
        check_vma=False,
    )
```
